512 devices in a mesh: row: 32 (over y, z_lo), col: 16 (over z_hi, x, core).
Axes of the slice: x: 4, y: 4, z: 16 (z_hi: 2, z_lo: 8; z = z_hi * 8 + z_lo), core: 2. Of those that a mesh axis runs over, the one named last changes fastest.
Arguments:
- features: bfloat16 [32, 16, 4, 128, 128], P('row', 'col'), may hold values from -6 to 6
- adjacency: bfloat16 [32, 16, 28, 128, 128], P('row', 'col'), may hold values from 0 to 30, as said below
- edge_dst: int32 [32, 16, 28], P('row', 'col'), may hold values from 0 to 3
- edge_src: int32 [32, 16, 28], P('row', 'col'), may hold values from 0 to 51
- send_row: int32 [32, 16, 32, 1], P('row', 'col'), may hold values from 0 to 3
- send_col: int32 [32, 16, 16, 1], P('row', 'col'), may hold values from 0 to 3
- w_self1: bfloat16 [128, 128], replicated, may hold values from -0.5 to 0.5
- w_neigh1: bfloat16 [128, 128], replicated, may hold values from -1.5 to 1.5
- w_self2: bfloat16 [128, 128], replicated, may hold values from -0.5 to 0.5
- w_neigh2: bfloat16 [128, 128], replicated, may hold values from -1.5 to 1.5
- cotangent: bfloat16 [32, 16, 4, 128, 128], P('row', 'col'), may hold values from -6 to 6
Outputs:
- output: bfloat16 [32, 16, 4, 128, 128], P('row', 'col')
- grad_features: float32 [32, 16, 4, 128, 128], P('row', 'col')
- grad_self1: float32 [128, 128], replicated
- grad_neigh1: float32 [128, 128], replicated
- grad_self2: float32 [128, 128], replicated
- grad_neigh2: float32 [128, 128], replicated
The draws below stay inside these ranges and needn't reach their ends.
Inputs may be any that keep to these rules, and one draw needn't show every extreme that they name: send_row[r, c, p] lists the own blocks that device (r, c) sends to device (p, c), in slot order. send_col[r, c, q] lists the own blocks that device (r, c) sends to device (r, q), in slot order. `adjacency`: edge weights are nonnegative.
All inputs are finite; a program needn't handle non-finite values.
Results may differ from the reference program's by a relative error of at most 0.0059.
Values may be sent and summed in bfloat16 or wider, within the bound.
A program may use at most 64 MiB of HBM per device.

```python
import math
import jax
import jax.numpy as jnp
from jax import lax

FEAT = 128
BLOCK_NODES = 128
OWN_BLOCKS = 4
EDGE_TILES = 28
SENT = 1
TABLE = 52
NODES = 262144
N_ROW = 32
N_COL = 16


def draw_adjacency(key, part):
    key = jax.random.fold_in(key, 11)
    key_mask, key_value = jax.random.split(key)
    tile_shape = (N_ROW, N_COL, EDGE_TILES, BLOCK_NODES, BLOCK_NODES)
    present = jax.random.uniform(key_mask, tile_shape, dtype=jnp.float32) < 1.0 / 64.0
    values = jnp.exp(jax.random.uniform(key_value, tile_shape, dtype=jnp.float32, minval=math.log(0.03), maxval=math.log(30.0)))
    return jnp.where(present, values, 0.0).astype(jnp.bfloat16)


def plant(drawn, own_key, low, largest):
    shape = drawn.shape
    spot = [jax.random.randint(jax.random.fold_in(own_key, axis), (), 0, shape[axis]) for axis in range(len(shape))]
    drawn = drawn.at[tuple(spot)].set(low)
    longest = shape.index(max(shape))
    spot[longest] = (spot[longest] + 1) % shape[longest]
    return drawn.at[tuple(spot)].set(largest)


def levels(rng, extent, cuts, least, top_value):
    def one(axis_at, parts):
        draws = jax.random.uniform(jax.random.fold_in(jax.random.fold_in(rng, 6), axis_at), (parts,), jnp.float32, least / len(cuts), top_value / len(cuts))
        return jnp.repeat(jnp.exp(draws), extent[axis_at] // parts).reshape((-1,) + (1,) * (len(extent) - axis_at - 1))

    level = one(*cuts[0])
    for cut in cuts[1:]:
        level = level * one(*cut)
    return level


def centred(rng, extent, width, most, shards=(), held_as=jnp.bfloat16):
    gain = levels(rng, extent, shards, -0.22, 0.18) if shards else 1.0
    values = jax.random.normal(rng, extent, jnp.float32) * width * gain
    return jnp.minimum(jnp.maximum(values, -most), most).astype(held_as)


def setup_inputs(seed: int = 0) -> dict:
    seeds = jax.random.split(jax.random.key(seed), 12)
    features = centred(seeds[0], (N_ROW, N_COL, OWN_BLOCKS, BLOCK_NODES, FEAT), 1.0, 6.0, ((0, 32), (1, 16)))
    adjacency = draw_adjacency(jax.random.fold_in(seeds[11], 71), 0)
    edge_dst = plant(jax.random.randint(seeds[2], (N_ROW, N_COL, EDGE_TILES), 0, OWN_BLOCKS), jax.random.fold_in(seeds[2], 1), 0, OWN_BLOCKS - 1).astype(jnp.int32)
    edge_src = plant(jax.random.randint(seeds[3], (N_ROW, N_COL, EDGE_TILES), 0, TABLE), jax.random.fold_in(seeds[3], 1), 0, TABLE - 1).astype(jnp.int32)
    send_row = plant(jax.random.randint(seeds[4], (N_ROW, N_COL, N_ROW, SENT), 0, OWN_BLOCKS), jax.random.fold_in(seeds[4], 1), 0, OWN_BLOCKS - 1).astype(jnp.int32)
    send_col = plant(jax.random.randint(seeds[5], (N_ROW, N_COL, N_COL, SENT), 0, OWN_BLOCKS), jax.random.fold_in(seeds[5], 1), 0, OWN_BLOCKS - 1).astype(jnp.int32)
    w_self1 = centred(seeds[6], (FEAT, FEAT), FEAT ** -0.5, 0.5)
    w_neigh1 = centred(seeds[7], (FEAT, FEAT), (FEAT // 8) ** -0.5, 1.5)
    w_self2 = centred(seeds[8], (FEAT, FEAT), FEAT ** -0.5, 0.5)
    w_neigh2 = centred(seeds[9], (FEAT, FEAT), (FEAT // 8) ** -0.5, 1.5)
    cotangent = centred(seeds[10], (N_ROW, N_COL, OWN_BLOCKS, BLOCK_NODES, FEAT), 1.0, 6.0, ((0, 32), (1, 16)))
    return {"features": features, "adjacency": adjacency, "edge_dst": edge_dst, "edge_src": edge_src, "send_row": send_row, "send_col": send_col, "w_self1": w_self1, "w_neigh1": w_neigh1, "w_self2": w_self2, "w_neigh2": w_neigh2, "cotangent": cotangent}


HIGHEST = lax.Precision.HIGHEST

def silu_slope(pre):
    sigmoid = jax.nn.sigmoid(pre)
    return sigmoid * (1.0 + pre * (1.0 - sigmoid))

def device_table(layer_in, send_row, send_col, row_idx, col_idx):
    own_blocks = layer_in[row_idx, col_idx]
    row_pool = layer_in[:, col_idx].reshape(N_ROW * OWN_BLOCKS, BLOCK_NODES, FEAT)
    row_lists = send_row[:, col_idx, row_idx, :]
    row_pick = (jnp.arange(N_ROW, dtype=jnp.int32)[:, None] * OWN_BLOCKS + row_lists).reshape(-1)
    col_pool = layer_in[row_idx].reshape(N_COL * OWN_BLOCKS, BLOCK_NODES, FEAT)
    col_lists = send_col[row_idx, :, col_idx, :]
    col_pick = (jnp.arange(N_COL, dtype=jnp.int32)[:, None] * OWN_BLOCKS + col_lists).reshape(-1)
    return jnp.concatenate([own_blocks, row_pool[row_pick], col_pool[col_pick]], axis=0)

def forward_device(layer_in, adjacency, edge_dst, edge_src, send_row, send_col, device):
    row_idx = device // N_COL
    col_idx = device % N_COL
    table = device_table(layer_in, send_row, send_col, row_idx, col_idx)
    adj_tiles = adjacency[row_idx, col_idx].astype(jnp.float32)
    dst_index = edge_dst[row_idx, col_idx]
    src_index = edge_src[row_idx, col_idx]
    degree = 1.0 + jax.ops.segment_sum(lax.optimization_barrier(jnp.sum(adj_tiles, axis=-1)), dst_index, num_segments=OWN_BLOCKS)
    products = jnp.einsum('eij,ejh->eih', adj_tiles, table[src_index].astype(jnp.float32), precision=HIGHEST)
    summed = jax.ops.segment_sum(products, dst_index, num_segments=OWN_BLOCKS)
    mean_val = ((layer_in[row_idx, col_idx].astype(jnp.float32) + summed) / degree[:, :, None]).astype(jnp.bfloat16)
    return (mean_val, degree)

def spread(q_blocks, adjacency, edge_dst, edge_src, send_row, send_col):

    def scan_step(returned, device):
        row_idx = device // N_COL
        col_idx = device % N_COL
        adj_tiles = adjacency[row_idx, col_idx].astype(jnp.float32)
        own_q = q_blocks[row_idx, col_idx]
        q_picked = own_q[edge_dst[row_idx, col_idx]].astype(jnp.float32)
        contrib = jnp.einsum('eji,ejh->eih', adj_tiles, q_picked, precision=HIGHEST)
        table_grad = jax.ops.segment_sum(contrib, edge_src[row_idx, col_idx], num_segments=TABLE)
        returned = returned.at[row_idx, col_idx].add(table_grad[:OWN_BLOCKS] + own_q.astype(jnp.float32))
        row_end = OWN_BLOCKS + N_ROW * SENT
        row_part = table_grad[OWN_BLOCKS:row_end].reshape(N_ROW, SENT, BLOCK_NODES, FEAT)
        returned = returned.at[jnp.arange(N_ROW, dtype=jnp.int32)[:, None], col_idx, send_row[:, col_idx, row_idx, :]].add(row_part)
        col_part = table_grad[row_end:].reshape(N_COL, SENT, BLOCK_NODES, FEAT)
        returned = returned.at[row_idx, jnp.arange(N_COL, dtype=jnp.int32)[:, None], send_col[row_idx, :, col_idx, :]].add(col_part)
        return (returned, None)
    zeros_grad = jnp.zeros((N_ROW, N_COL, OWN_BLOCKS, BLOCK_NODES, FEAT), jnp.float32)
    devices = jnp.arange(N_ROW * N_COL, dtype=jnp.int32)
    returned, _ = lax.scan(scan_step, zeros_grad, devices)
    return returned

def reference(features, adjacency, edge_dst, edge_src, send_row, send_col, w_self1, w_neigh1, w_self2, w_neigh2, cotangent):
    devices = jnp.arange(N_ROW * N_COL, dtype=jnp.int32)
    block_shape = (N_ROW, N_COL, OWN_BLOCKS, BLOCK_NODES, FEAT)
    mean_one, degree = lax.map(lambda device: forward_device(features, adjacency, edge_dst, edge_src, send_row, send_col, device), devices)
    flat_in = features.reshape(-1, FEAT)
    mean_one_flat = mean_one.reshape(-1, FEAT)
    degree_flat = degree.reshape(-1)
    pre_one = jnp.dot(flat_in, w_self1, preferred_element_type=jnp.float32) + jnp.dot(mean_one_flat, w_neigh1, preferred_element_type=jnp.float32)
    hidden = jax.nn.silu(pre_one).astype(jnp.bfloat16)
    hidden_blocks = hidden.reshape(block_shape)
    mean_two, _ = lax.map(lambda device: forward_device(hidden_blocks, adjacency, edge_dst, edge_src, send_row, send_col, device), devices)
    mean_two_flat = mean_two.reshape(-1, FEAT)
    output = (jnp.dot(hidden, w_self2, preferred_element_type=jnp.float32) + jnp.dot(mean_two_flat, w_neigh2, preferred_element_type=jnp.float32)).astype(jnp.bfloat16)
    grad_scale = 1.0 / math.sqrt(NODES)
    cot_flat = cotangent.reshape(-1, FEAT)
    grad_self2 = jnp.dot(hidden.T, cot_flat, preferred_element_type=jnp.float32) * grad_scale
    grad_neigh2 = jnp.dot(mean_two_flat.T, cot_flat, preferred_element_type=jnp.float32) * grad_scale
    q_two = (jnp.dot(cot_flat, w_neigh2.T, preferred_element_type=jnp.float32) / degree_flat[:, None]).astype(jnp.bfloat16)
    back_two = spread(q_two.reshape(block_shape), adjacency, edge_dst, edge_src, send_row, send_col)
    dhidden = jnp.dot(cot_flat, w_self2.T, preferred_element_type=jnp.float32) + back_two.reshape(-1, FEAT)
    dpre_one = (dhidden * silu_slope(pre_one)).astype(jnp.bfloat16)
    grad_self1 = jnp.dot(flat_in.T, dpre_one, preferred_element_type=jnp.float32) * grad_scale
    grad_neigh1 = jnp.dot(mean_one_flat.T, dpre_one, preferred_element_type=jnp.float32) * grad_scale
    q_one = (jnp.dot(dpre_one, w_neigh1.T, preferred_element_type=jnp.float32) / degree_flat[:, None]).astype(jnp.bfloat16)
    back_one = spread(q_one.reshape(block_shape), adjacency, edge_dst, edge_src, send_row, send_col)
    grad_features = jnp.dot(dpre_one, w_self1.T, preferred_element_type=jnp.float32) + back_one.reshape(-1, FEAT)
    return (output.reshape(block_shape), grad_features.reshape(block_shape), grad_self1, grad_neigh1, grad_self2, grad_neigh2)
```

```python
import functools
import math

import jax
import jax.numpy as jnp
from jax import lax
from jax.experimental import pallas as pl
from jax.experimental.pallas import tpu as pltpu
from jax.sharding import PartitionSpec as P

MESH = pl.DeviceIdType.MESH
BF16 = jnp.bfloat16
F32 = jnp.float32
LIMIT = 44 * 1024 * 1024
SPLIT = {"y": 4, "z": 8, "zh": 2, "xc": 8}
LAG = 3


def dot(a, b):
    return jnp.dot(a, b, preferred_element_type=F32)


def dot_bt(a, b):
    return lax.dot_general(a, b, (((1,), (1,)), ((), ())), preferred_element_type=F32)


def dot_at(a, b):
    return lax.dot_general(a, b, (((0,), (0,)), ((), ())), preferred_element_type=F32)


def exchange_kernel(split, with_sum, *refs):
    ny, nz, nh, nx = split["y"], split["z"], split["zh"], split["xc"]
    nrow, ncol = ny * nz, nh * nx
    refs = list(refs)
    own, gsend, idx = refs[:3]
    del refs[:3]
    if with_sum:
        gr = refs.pop(0)
    table, back = refs[:2]
    del refs[:2]
    if with_sum:
        gout = refs.pop(0)
    (chain, far, tiles, pick_row, pick_col, stage_y, stage_c, land_y, land_c, from_left, from_right,
     to_right, to_left, far_out, far_in) = refs[:15]
    (i_s, i_r, f_r, f_sr, f_sl, h_s, h_r, yf_s, yf_r, cf_s, cf_r, yb_s, yb_r, cb_s, cb_r,
     b_rl, b_rr, b_sr, b_sl) = refs[15:34]
    own_count, rows, feat = own.shape

    r = lax.axis_index("row")
    c = lax.axis_index("col")
    y, z = lax.div(r, nz), lax.rem(r, nz)
    zh, xc = lax.div(c, nx), lax.rem(c, nx)

    def y_peer(d):
        return lax.rem(y + d, ny)

    def x_peer(d):
        return lax.rem(xc + d, nx)

    def remote(src, dst, ssem, rsem, row, col):
        return pltpu.make_async_remote_copy(
            src_ref=src, dst_ref=dst, send_sem=ssem, recv_sem=rsem,
            device_id=(row, col), device_id_type=MESH,
        )

    partner = (1 - zh) * nx + xc

    barrier = pltpu.get_barrier_semaphore()

    def greet(row, col):
        pl.semaphore_signal(barrier, inc=1, device_id=(row, col), device_id_type=MESH)

    for d in range(1, ny):
        greet(y_peer(d) * nz + z, c)
    for d in range(1, nz):
        greet(y * nz + lax.rem(z + d, nz), c)
    greet(r, partner)
    for d in range(1, nx):
        greet(r, zh * nx + x_peer(d))
    pl.semaphore_wait(barrier, (ny - 1) + (nz - 1) + 1 + (nx - 1))

    def idx_copy(d):
        zz = lax.rem(z + d, nz)
        return remote(idx, tiles.at[z], i_s.at[d], i_r.at[z], y * nz + zz, c)

    def idx_wait(d):
        zz = lax.rem(z + d, nz)
        return remote(idx, tiles.at[zz], i_s.at[d], i_r.at[zz], y * nz + zz, c)

    idx_far = remote(idx, tiles.at[nz], i_s.at[0], i_r.at[nz], r, partner)
    blocks_far = remote(own, far, h_s.at[0], h_r.at[0], r, partner)
    back_far = remote(far_out, far_in, h_s.at[1], h_r.at[1], r, partner)

    def right(src):
        return remote(chain.at[src], chain.at[src], f_sr.at[src], f_r.at[src], r + 1, c)

    def left(src):
        return remote(chain.at[src], chain.at[src], f_sl.at[src], f_r.at[src], r - 1, c)

    def back_right(o):
        return remote(to_right.at[o], from_left.at[o], b_sr.at[o], b_rl.at[o], r + 1, c)

    def back_left(o):
        return remote(to_left.at[o], from_right.at[o], b_sl.at[o], b_rr.at[o], r - 1, c)

    def y_back(d):
        yy = y_peer(d)
        return remote(gsend.at[pl.ds(yy * nz, nz)], land_y.at[(ny - d) % ny],
                      yb_s.at[d], yb_r.at[(ny - d) % ny], yy * nz + z, c)

    def x_back(d):
        xx = x_peer(d)
        return remote(gsend.at[pl.ds(nrow + xx * nh, nh)], land_c.at[(nx - d) % nx],
                      cb_s.at[d], cb_r.at[(nx - d) % nx], r, zh * nx + xx)

    def y_out(d, src):
        return remote(stage_y.at[d, src], table.at[own_count + y * nz + src],
                      yf_s.at[d, src], yf_r.at[d, src], y_peer(d) * nz + z, c)

    def y_in(d, src):
        yy = lax.rem(y + ny - d, ny)
        return remote(stage_y.at[d, src], table.at[own_count + yy * nz + src],
                      yf_s.at[d, src], yf_r.at[d, src], yy * nz + z, c)

    def col_slot(s, x_from):
        half = zh if s == 0 else 1 - zh
        return own_count + nrow + half * nx + x_from

    def c_out(d, s):
        return remote(stage_c.at[d, s], table.at[col_slot(s, xc)],
                      cf_s.at[d, s], cf_r.at[d, s], r, zh * nx + x_peer(d))

    def c_in(d, s):
        xx = lax.rem(xc + nx - d, nx)
        return remote(stage_c.at[d, s], table.at[col_slot(s, xx)],
                      cf_s.at[d, s], cf_r.at[d, s], r, zh * nx + xx)

    for d in range(1, nz):
        idx_copy(d).start()
    idx_far.start()
    chain[z] = own[...]
    tiles[z] = idx[...]

    @pl.when(z < nz - 1)
    def _():
        right(z).start()

    @pl.when(z > 0)
    def _():
        left(z).start()

    for d in range(1, ny):
        y_back(d).start()
    for d in range(1, nx):
        x_back(d).start()
    blocks_far.start()

    if with_sum:
        ar = sum_stages(split, gr, gout, refs[34:], (r, c, y, z, zh, xc), remote)
        ar[0]()

    table[pl.ds(0, own_count)] = own[...]
    land_y[0] = gsend[pl.ds(y * nz, nz)]
    land_c[0] = gsend[pl.ds(nrow + xc * nh, nh)]

    for d in range(1, nz):
        idx_wait(d).wait_recv()
    idx_far.wait_recv()
    lists = tiles[...].astype(F32)
    along = lists[:nz].reshape(nz * 8, 128).astype(BF16)
    pair = jnp.concatenate([tiles[z].astype(F32), lists[nz]], axis=0).astype(BF16)
    lane = lax.broadcasted_iota(jnp.int32, (128, 128), 0)
    for d in range(ny):
        hot = jnp.where(lane == y_peer(d) * nz + z, 1.0, 0.0).astype(BF16)
        pick_row[d] = dot(along, hot).reshape(nz, 8, 128)
    for d in range(nx):
        hot = jnp.where(lane == nrow + zh * nx + x_peer(d), 1.0, 0.0).astype(BF16)
        pick_col[d] = dot(pair, hot).reshape(2, 8, 128)

    def choose(which, blocks):
        row = which[0:1, :]
        total = None
        for k in range(own_count):
            term = blocks[k].astype(F32) * jnp.where(row == k, 1.0, 0.0)
            total = term if total is None else total + term
        return total.astype(BF16)

    def forward(src):
        blocks = chain.at[src]
        for d in range(ny):
            chosen = choose(pick_row[d, src], blocks)
            if d == 0:
                table[own_count + y * nz + src] = chosen
            else:
                stage_y[d, src] = chosen
                y_out(d, src).start()

    def forward_col(s, blocks):
        for d in range(nx):
            chosen = choose(pick_col[d, s], blocks)
            if d == 0:
                table[col_slot(s, xc)] = chosen
            else:
                stage_c[d, s] = chosen
                c_out(d, s).start()

    def placed(o, k):
        total = None
        for d in range(ny):
            hot = jnp.where(pick_row[d, o][0:1, :] == k, 1.0, 0.0)
            term = land_y[d, o].astype(F32) * hot
            total = term if total is None else total + term
        return total

    def placed_col(half, s, k):
        total = None
        for d in range(nx):
            hot = jnp.where(pick_col[d, s][0:1, :] == k, 1.0, 0.0)
            term = land_c[d, half].astype(F32) * hot
            total = term if total is None else total + term
        return total

    forward(z)
    forward_col(0, own)

    def fwd_step(s):
        src = z - s

        @pl.when(src >= 0)
        def _():
            right(src).wait_recv()

            @pl.when(z < nz - 1)
            def _():
                right(src).start()

            forward(src)

        src2 = z + s

        @pl.when(src2 < nz)
        def _():
            left(src2).wait_recv()

            @pl.when(z > 0)
            def _():
                left(src2).start()

            forward(src2)

    def bwd_step(t):
        o = nz - 1 + z - t

        @pl.when((o > z) & (o < nz))
        def _():
            @pl.when(z > 0)
            def _():
                back_right(o).wait_recv()
                for k in range(own_count):
                    to_right[o, k] = (placed(o, k) + from_left[o, k].astype(F32)).astype(BF16)

            @pl.when(z == 0)
            def _():
                for k in range(own_count):
                    to_right[o, k] = placed(o, k).astype(BF16)

            back_right(o).start()

        o2 = z - (nz - 1) + t

        @pl.when((o2 >= 0) & (o2 < z))
        def _():
            @pl.when(z < nz - 1)
            def _():
                back_left(o2).wait_recv()
                for k in range(own_count):
                    to_left[o2, k] = (placed(o2, k) + from_right[o2, k].astype(F32)).astype(BF16)

            @pl.when(z == nz - 1)
            def _():
                for k in range(own_count):
                    to_left[o2, k] = placed(o2, k).astype(BF16)

            back_left(o2).start()

    def step(s, carry):
        @pl.when(s < nz)
        def _():
            fwd_step(s)

        @pl.when(s == 1)
        def _():
            for d in range(1, nx):
                x_back(d).wait_recv()
            for k in range(own_count):
                far_out[k] = placed_col(1 - zh, 1, k).astype(BF16)
            back_far.start()

        @pl.when(s == LAG)
        def _():
            for d in range(1, ny):
                y_back(d).wait_recv()

        @pl.when(s >= LAG)
        def _():
            bwd_step(s - LAG)

        @pl.when(s == 3)
        def _():
            blocks_far.wait_recv()
            forward_col(1, far)

        if with_sum:
            for k in range(1, len(ar)):
                @pl.when(s == k)
                def _(k=k):
                    ar[k]()
        return carry

    lax.fori_loop(1, max(nz + LAG - 1, 10), step, 0)

    for k in range(own_count):
        back[k] = placed(z, k) + placed_col(zh, 0, k)

    @pl.when(z > 0)
    def _():
        back_right(z).wait_recv()
        for k in range(own_count):
            back[k] += from_left[z, k].astype(F32)

    @pl.when(z < nz - 1)
    def _():
        back_left(z).wait_recv()
        for k in range(own_count):
            back[k] += from_right[z, k].astype(F32)

    back_far.wait_recv()
    for k in range(own_count):
        back[k] += far_in[k].astype(F32)

    def arrive(src, carry):
        for d in range(1, ny):
            y_in(d, src).wait_recv()
            y_out(d, src).wait_send()

        @pl.when((src <= z) & (z < nz - 1))
        def _():
            right(src).wait_send()

        @pl.when((src >= z) & (z > 0))
        def _():
            left(src).wait_send()

        @pl.when(src > z)
        def _():
            back_right(src).wait_send()

        @pl.when(src < z)
        def _():
            back_left(src).wait_send()

        return carry

    lax.fori_loop(0, nz, arrive, 0)
    for d in range(1, nx):
        for s in range(2):
            c_in(d, s).wait_recv()
            c_out(d, s).wait_send()
        x_back(d).wait_send()
    for d in range(1, ny):
        y_back(d).wait_send()
    for d in range(1, nz):
        idx_copy(d).wait_send()
    idx_far.wait_send()
    blocks_far.wait_send()
    back_far.wait_send()


def sum_stages(split, gr, gout, refs, where, remote):
    ny, nz, nx = split["y"], split["z"], split["xc"] // 2
    r, c, y, z, zh, xc = where
    core, x = lax.rem(xc, 2), lax.div(xc, 2)
    (a1, v1, a2, v2, a3, a4, a5, v5, w1, w2, s1, r1, s2, r2, s3, r3, s4, r4, s5, r5,
     s6, r6, s7, r7, s8, r8) = refs
    half = gr.shape[0] // 2
    part = half // nx
    piece = part // ny
    sx = split["xc"]
    partner = (1 - zh) * sx + xc
    other = zh * sx + x * 2 + (1 - core)

    def xcol(d):
        xx = lax.rem(x + d, nx)
        return xx, zh * sx + xx * 2 + core

    def yrow(d):
        yy = lax.rem(y + d, ny)
        return yy, yy * nz + z

    def rows_of(i, n):
        return pl.ds(pl.multiple_of(i * n, n), n)

    c1 = remote(gr.at[rows_of(1 - core, half)], a1, s1.at[0], r1.at[0], r, other)

    def c2(d):
        xx, col = xcol(d)
        return remote(v1.at[rows_of(xx, part)], a2.at[(nx - d) % nx], s2.at[d], r2.at[(nx - d) % nx], r, col)

    def c3(d):
        yy, row = yrow(d)
        return remote(v2.at[rows_of(yy, piece)], a3.at[(ny - d) % ny], s3.at[d], r3.at[(ny - d) % ny], row, c)

    def c4(d, slot):
        zz = lax.rem(z + d, nz)
        to = z if slot is None else zz
        return remote(a4.at[z], a4.at[to], s4.at[d], r4.at[to], y * nz + zz, c)

    c5 = remote(v5.at[0], a5, s5.at[0], r5.at[0], r, partner)

    def c6(d, slot):
        yy, row = yrow(d)
        to = y if slot is None else yy
        here = w1.at[rows_of(y, piece)]
        return remote(here, w1.at[rows_of(to, piece)], s6.at[d], r6.at[to], row, c)

    def c7(d, slot):
        xx, col = xcol(d)
        to = x if slot is None else xx
        here = w2.at[rows_of(x, part)]
        return remote(here, w2.at[rows_of(to, part)], s7.at[d], r7.at[to], r, col)

    c8 = remote(w2, gout.at[rows_of(core, half)], s8.at[0], r8.at[0], r, other)
    c8_in = remote(w2, gout.at[rows_of(1 - core, half)], s8.at[0], r8.at[0], r, other)

    def t0():
        c1.start()

    def t1():
        c1.wait_recv()
        v1[...] = gr[rows_of(core, half)] + a1[...]
        for d in range(1, nx):
            c2(d).start()

    def t2():
        total = v1[rows_of(x, part)]
        for d in range(1, nx):
            c2(d).wait_recv()
        for d in range(1, nx):
            total = total + a2[d]
        v2[...] = total
        for d in range(1, ny):
            c3(d).start()

    def t3():
        total = v2[rows_of(y, piece)]
        for d in range(1, ny):
            c3(d).wait_recv()
        for d in range(1, ny):
            total = total + a3[d]
        a4[z] = total
        for d in range(1, nz):
            c4(d, None).start()

    def t4():
        for d in range(1, nz):
            c4(d, 1).wait_recv()
        total = a4[0]
        for i in range(1, nz):
            total = total + a4[i]
        v5[0] = total
        c5.start()

    def t5():
        c5.wait_recv()
        w1[rows_of(y, piece)] = v5[0] + a5[...]
        for d in range(1, ny):
            c6(d, None).start()

    def t6():
        for d in range(1, ny):
            c6(d, 1).wait_recv()
        w2[rows_of(x, part)] = w1[...]
        for d in range(1, nx):
            c7(d, None).start()

    def t7():
        for d in range(1, nx):
            c7(d, 1).wait_recv()
        gout[rows_of(core, half)] = w2[...]
        c8.start()

    def t8():
        c8_in.wait_recv()
        c1.wait_send()
        for d in range(1, nx):
            c2(d).wait_send()
            c7(d, None).wait_send()
        for d in range(1, ny):
            c3(d).wait_send()
            c6(d, None).wait_send()
        for d in range(1, nz):
            c4(d, None).wait_send()
        c5.wait_send()
        c8.wait_send()

    return [t0, t1, t2, t3, t4, t5, t6, t7, t8]


def exchange(split, own, gsend, idx, grads, collective_id):
    ny, nz, nh, nx = split["y"], split["z"], split["zh"], split["xc"]
    own_count, rows, feat = own.shape
    size = own_count + ny * nz + nh * nx
    blocks = (own_count, rows, feat)
    one = (rows, feat)
    dma = pltpu.SemaphoreType.DMA
    scratch = [
        pltpu.VMEM((nz,) + blocks, BF16),
        pltpu.VMEM(blocks, BF16),
        pltpu.VMEM((nz + 1, 8, 128), jnp.int32),
        pltpu.VMEM((ny, nz, 8, 128), F32),
        pltpu.VMEM((nx, 2, 8, 128), F32),
        pltpu.VMEM((ny, nz) + one, BF16),
        pltpu.VMEM((nx, 2) + one, BF16),
        pltpu.VMEM((ny, nz) + one, BF16),
        pltpu.VMEM((nx, nh) + one, BF16),
        pltpu.VMEM((nz,) + blocks, BF16),
        pltpu.VMEM((nz,) + blocks, BF16),
        pltpu.VMEM((nz,) + blocks, BF16),
        pltpu.VMEM((nz,) + blocks, BF16),
        pltpu.VMEM(blocks, BF16),
        pltpu.VMEM(blocks, BF16),
        dma((nz,)), dma((nz + 1,)), dma((nz,)), dma((nz,)), dma((nz,)), dma((2,)), dma((2,)),
        dma((ny, nz)), dma((ny, nz)), dma((nx, 2)), dma((nx, 2)),
        dma((ny,)), dma((ny,)), dma((nx,)), dma((nx,)),
        dma((nz,)), dma((nz,)), dma((nz,)), dma((nz,)),
    ]
    out_shape = [
        jax.ShapeDtypeStruct((size, rows, feat), BF16),
        jax.ShapeDtypeStruct(blocks, F32),
    ]
    args = [own, gsend, idx]
    if grads is not None:
        args.append(grads)
        out_shape.append(jax.ShapeDtypeStruct(grads.shape, F32))
        half = grads.shape[0] // 2
        cx = nx // 2
        part = half // cx
        piece = part // ny
        scratch += [
            pltpu.VMEM((half, 128), F32),
            pltpu.VMEM((half, 128), F32),
            pltpu.VMEM((cx, part, 128), F32),
            pltpu.VMEM((part, 128), F32),
            pltpu.VMEM((ny, piece, 128), F32),
            pltpu.VMEM((nz, piece, 128), F32),
            pltpu.VMEM((piece, 128), F32),
            pltpu.VMEM((1, piece, 128), F32),
            pltpu.VMEM((part, 128), F32),
            pltpu.VMEM((half, 128), F32),
            dma((1,)), dma((1,)), dma((cx,)), dma((cx,)), dma((ny,)), dma((ny,)),
            dma((nz,)), dma((nz,)), dma((1,)), dma((1,)), dma((ny,)), dma((ny,)),
            dma((cx,)), dma((cx,)), dma((1,)), dma((1,)),
        ]
    vmem = pl.BlockSpec(memory_space=pltpu.VMEM)
    return pl.pallas_call(
        functools.partial(exchange_kernel, split, grads is not None),
        out_shape=out_shape,
        in_specs=[vmem] * len(args),
        out_specs=[vmem] * len(out_shape),
        scratch_shapes=scratch,
        compiler_params=pltpu.CompilerParams(
            collective_id=collective_id, has_side_effects=True, vmem_limit_bytes=LIMIT
        ),
    )(*args)


def grad_slot(split, own_count, t):
    nh, nx = split["zh"], split["xc"]
    first = own_count + split["y"] * split["z"]
    q = t - first
    return jnp.where(t < first, t, first + nh * lax.rem(q, nx) + lax.div(q, nx))


def spread(split, own_count, adj, dst, src, q, grad):
    @pl.loop(0, grad.shape[0])
    def _(i):
        grad[i] = jnp.zeros(grad.shape[1:], F32)

    def one(e, carry):
        grad[grad_slot(split, own_count, src[e])] += dot_at(adj[e], q[dst[e]])
        return carry

    lax.fori_loop(0, adj.shape[0], one, 0, unroll=4)


def gather(adj, dst, src, table, acc):
    def one(e, carry):
        acc[dst[e]] += dot(adj[e], table[src[e]])
        return carry

    lax.fori_loop(0, adj.shape[0], one, 0, unroll=4)


def send_out(own_count, grad, gsend):
    @pl.loop(0, gsend.shape[0])
    def _(i):
        gsend[i] = grad[own_count + i].astype(BF16)


def first_kernel(split, dst, src, adj, cot, deg, u_own, gsend, grad, q):
    own_count = cot.shape[0]
    deg[...] = jnp.ones_like(deg)
    ones = jnp.ones(adj.shape[1:], BF16)

    def one(e, carry):
        deg[dst[e]] += dot(adj[e], ones)
        return carry

    lax.fori_loop(0, adj.shape[0], one, 0, unroll=4)
    for b in range(own_count):
        q[b] = (cot[b].astype(F32) / deg[b]).astype(BF16)
    spread(split, own_count, adj, dst, src, q, grad)
    for b in range(own_count):
        u_own[b] = grad[b] + q[b].astype(F32)
    send_out(own_count, grad, gsend)


def middle_kernel(split, scale, dst, src, adj, feat, table, deg, u_own, u_back, cot,
                  ws1, wn1, ws2, wn2, hidden, base, gsend, grads, acc, grad, q):
    own_count, rows, width = feat.shape
    for b in range(own_count):
        acc[b] = feat[b].astype(F32)
    gather(adj, dst, src, table, acc)
    g1, g2, g3, g4 = 0.0, 0.0, 0.0, 0.0
    for b in range(own_count):
        mean = (acc[b] / deg[b]).astype(BF16)
        pre = dot(feat[b], ws1[...]) + dot(mean, wn1[...])
        s = 1.0 / (1.0 + jnp.exp(-pre))
        hid = (pre * s).astype(BF16)
        hidden[b] = hid
        u = u_own[b] + u_back[b]
        hi = u.astype(BF16)
        lo = (u - hi.astype(F32)).astype(BF16)
        dh = dot_bt(cot[b], ws2[...]) + (dot_bt(hi, wn2[...]) + dot_bt(lo, wn2[...]))
        dpre = (dh * (s * (1.0 + pre * (1.0 - s)))).astype(BF16)
        qb = (dot_bt(dpre, wn1[...]) / deg[b]).astype(BF16)
        q[b] = qb
        base[b] = dot_bt(dpre, ws1[...]) + qb.astype(F32)
        g1 = g1 + dot_at(feat[b], dpre)
        g2 = g2 + dot_at(mean, dpre)
        g3 = g3 + dot_at(hid, cot[b])
        g4 = g4 + (dot_at(hid, hi) + dot_at(hid, lo))
    for i, g in enumerate((g1, g2, g3, g4)):
        grads[pl.ds(i * width, width), :] = g * scale
    spread(split, own_count, adj, dst, src, q, grad)
    for b in range(own_count):
        base[b] += grad[b]
    send_out(own_count, grad, gsend)


def last_kernel(dst, src, adj, hidden, table, deg, base, back, ws2, wn2, out, grad_in, acc):
    own_count = hidden.shape[0]
    for b in range(own_count):
        acc[b] = hidden[b].astype(F32)
    gather(adj, dst, src, table, acc)
    for b in range(own_count):
        mean = (acc[b] / deg[b]).astype(BF16)
        out[b] = (dot(hidden[b], ws2[...]) + dot(mean, wn2[...])).astype(BF16)
        grad_in[b] = base[b] + back[b]


def on_device(body, edges, args, out_shape, scratch):
    smem = pl.BlockSpec(memory_space=pltpu.SMEM)
    vmem = pl.BlockSpec(memory_space=pltpu.VMEM)
    return pl.pallas_call(
        body,
        out_shape=out_shape,
        in_specs=[smem] * len(edges) + [vmem] * len(args),
        out_specs=[vmem] * len(out_shape),
        scratch_shapes=scratch,
        compiler_params=pltpu.CompilerParams(vmem_limit_bytes=LIMIT),
    )(*edges, *args)


def local(
    split,
    nodes,
    features,
    adjacency,
    edge_dst,
    edge_src,
    send_row,
    send_col,
    w_self1,
    w_neigh1,
    w_self2,
    w_neigh2,
    cotangent,
):
    own = features[0, 0]
    adj = adjacency[0, 0]
    edges = (edge_dst[0, 0], edge_src[0, 0])
    cot = cotangent[0, 0]
    own_count, rows, width = own.shape
    lists = jnp.concatenate([send_row.reshape(-1), send_col.reshape(-1)])
    remote_count = lists.size
    idx = jnp.broadcast_to(jnp.pad(lists, (0, 128 - remote_count))[None, :], (8, 128))
    size = own_count + remote_count
    blocks = (own_count, rows, width)
    full = jax.ShapeDtypeStruct(blocks, F32)
    half = jax.ShapeDtypeStruct(blocks, BF16)
    sends = jax.ShapeDtypeStruct((remote_count, rows, width), BF16)
    grad = pltpu.VMEM((size, rows, width), F32)
    acc = pltpu.VMEM(blocks, F32)
    q = pltpu.VMEM(blocks, BF16)
    deg, u_own, gsend = on_device(
        functools.partial(first_kernel, split), edges, (adj, cot), [full, full, sends], [grad, q]
    )
    table, u_back = exchange(split, own, gsend, idx, None, 0)
    weights = jax.ShapeDtypeStruct((4 * width, width), F32)
    hidden, base, gsend, grads = on_device(
        functools.partial(middle_kernel, split, 1.0 / math.sqrt(nodes)),
        edges,
        (adj, own, table, deg, u_own, u_back, cot, w_self1, w_neigh1, w_self2, w_neigh2),
        [half, full, sends, weights],
        [acc, grad, q],
    )
    table, back, grads = exchange(split, hidden, gsend, idx, grads, 1)
    out, grad_in = on_device(
        last_kernel,
        edges,
        (adj, hidden, table, deg, base, back, w_self2, w_neigh2),
        [half, full],
        [acc],
    )
    g = grads.reshape(4, width, width)
    return (
        out.reshape(features.shape),
        grad_in.reshape(features.shape),
        g[0],
        g[1],
        g[2],
        g[3],
    )


def solution(mesh):
    blocked = P("row", "col", None, None, None)
    placed = (
        blocked,
        blocked,
        P("row", "col", None),
        P("row", "col", None),
        P("row", "col", None, None),
        P("row", "col", None, None),
        P(),
        P(),
        P(),
        P(),
        blocked,
    )

    def whole(*args):
        shape = args[0].shape
        nodes = shape[0] * shape[1] * shape[2] * shape[3]
        return jax.shard_map(
            functools.partial(local, SPLIT, nodes),
            mesh=mesh,
            in_specs=placed,
            out_specs=(blocked, blocked, P(), P(), P(), P()),
            check_vma=False,
        )(*args)

    return whole
```

```python
import functools
import math

import jax
import jax.numpy as jnp
from jax import lax
from jax.experimental import pallas as pl
from jax.experimental.pallas import tpu as pltpu
from jax.sharding import PartitionSpec as P

MESH = pl.DeviceIdType.MESH
BF16 = jnp.bfloat16
F32 = jnp.float32
LIMIT = 44 * 1024 * 1024
SPLIT = {"y": 4, "z": 8, "zh": 2, "xc": 8}
LAG = 2
CUT = 2


def dot(a, b):
    return jnp.dot(a, b, preferred_element_type=F32)


def dot_bt(a, b):
    return lax.dot_general(a, b, (((1,), (1,)), ((), ())), preferred_element_type=F32)


def dot_at(a, b):
    return lax.dot_general(a, b, (((0,), (0,)), ((), ())), preferred_element_type=F32)


def exchange_kernel(split, lag, cut, with_sum, *refs):
    ny, nz, nh, nx = split["y"], split["z"], split["zh"], split["xc"]
    nrow, ring = ny * nz, nh * nz
    refs = list(refs)
    own, gsend, idx = refs[:3]
    del refs[:3]
    if with_sum:
        gr = refs.pop(0)
    table, back = refs[:2]
    del refs[:2]
    if with_sum:
        gout = refs.pop(0)
    (chain, tiles, pick_row, pick_col, stage_y, stage_c, land_y, land_c, in_right, in_left,
     out_left, out_right, ready, far_out) = refs[:14]
    (i_s, i_r, f_r, f_sr, f_sl, yf_s, yf_r, cf_s, cf_r, yb_s, yb_r, cb_s, cb_r,
     br_r, bl_r, b_sl, b_sr) = refs[14:31]
    own_count, rows, feat = own.shape
    per = own_count // cut

    r = lax.axis_index("row")
    c = lax.axis_index("col")
    y, z = lax.div(r, nz), lax.rem(r, nz)
    zh, xc = lax.div(c, nx), lax.rem(c, nx)
    g = zh * nz + z
    partner = (1 - zh) * nx + xc

    def y_peer(d):
        return lax.rem(y + d, ny)

    def x_peer(d):
        return lax.rem(xc + d, nx)

    def at_ring(pos):
        pos = lax.rem(pos + ring, ring)
        return y * nz + lax.rem(pos, nz), lax.div(pos, nz) * nx + xc

    def reach_right(src):
        return jnp.where(src < nz // 2, nz, nz - 1 - src)

    def reach_left(src):
        return jnp.where(src < nz // 2, src, nz)

    def remote(src, dst, ssem, rsem, row, col):
        return pltpu.make_async_remote_copy(
            src_ref=src, dst_ref=dst, send_sem=ssem, recv_sem=rsem,
            device_id=(row, col), device_id_type=MESH,
        )

    barrier = pltpu.get_barrier_semaphore()

    def greet(row, col):
        pl.semaphore_signal(barrier, inc=1, device_id=(row, col), device_id_type=MESH)

    for d in range(1, ny):
        greet(y_peer(d) * nz + z, c)
    for d in range(1, nz):
        greet(y * nz + lax.rem(z + d, nz), c)
    greet(r, partner)
    for d in range(1, nx):
        greet(r, zh * nx + x_peer(d))
    at_end = (z == 0) | (z == nz - 1)

    @pl.when(z == 0)
    def _():
        greet(*at_ring(g - 1))

    @pl.when(z == nz - 1)
    def _():
        greet(*at_ring(g + 1))

    met = (ny - 1) + (nz - 1) + 1 + (nx - 1)

    @pl.when(at_end)
    def _():
        pl.semaphore_wait(barrier, met + 1)

    @pl.when(jnp.logical_not(at_end))
    def _():
        pl.semaphore_wait(barrier, met)

    def idx_copy(d):
        zz = lax.rem(z + d, nz)
        return remote(idx, tiles.at[z], i_s.at[d], i_r.at[z], y * nz + zz, c)

    def idx_wait(d):
        zz = lax.rem(z + d, nz)
        return remote(idx, tiles.at[zz], i_s.at[d], i_r.at[zz], y * nz + zz, c)

    idx_far = remote(idx, tiles.at[nz], i_s.at[0], i_r.at[nz], r, partner)

    def part(ref, slot, ch):
        return ref.at[slot, pl.ds(ch * per, per)]

    def right(src, ch):
        ref = part(chain, src, ch)
        return remote(ref, ref, f_sr.at[src, ch], f_r.at[src, ch], *at_ring(g + 1))

    def left(src, ch):
        ref = part(chain, src, ch)
        return remote(ref, ref, f_sl.at[src, ch], f_r.at[src, ch], *at_ring(g - 1))

    def back_left(o, ch, buf):
        return remote(part(buf, o, ch), part(in_right, o, ch), b_sl.at[o, ch], br_r.at[o, ch],
                      *at_ring(g - 1))

    def back_right(o, ch, buf):
        return remote(part(buf, o, ch), part(in_left, o, ch), b_sr.at[o, ch], bl_r.at[o, ch],
                      *at_ring(g + 1))

    def y_back(d, o):
        yy = y_peer(d)
        return remote(gsend.at[yy * nz + o], land_y.at[(ny - d) % ny, o],
                      yb_s.at[d, o], yb_r.at[(ny - d) % ny, o], yy * nz + z, c)

    def x_back(d):
        xx = x_peer(d)
        return remote(gsend.at[pl.ds(nrow + xx * nh, nh)], land_c.at[(nx - d) % nx],
                      cb_s.at[d], cb_r.at[(nx - d) % nx], r, zh * nx + xx)

    def y_out(d, src):
        return remote(stage_y.at[d, src], table.at[own_count + y * nz + src],
                      yf_s.at[d, src], yf_r.at[d, src], y_peer(d) * nz + z, c)

    def y_in(d, src):
        yy = lax.rem(y + ny - d, ny)
        return remote(stage_y.at[d, src], table.at[own_count + yy * nz + src],
                      yf_s.at[d, src], yf_r.at[d, src], yy * nz + z, c)

    def col_slot(s, x_from):
        half = zh if s == 0 else 1 - zh
        return own_count + nrow + half * nx + x_from

    def c_out(d, s):
        return remote(stage_c.at[d, s], table.at[col_slot(s, xc)],
                      cf_s.at[d, s], cf_r.at[d, s], r, zh * nx + x_peer(d))

    def c_in(d, s):
        xx = lax.rem(xc + nx - d, nx)
        return remote(stage_c.at[d, s], table.at[col_slot(s, xx)],
                      cf_s.at[d, s], cf_r.at[d, s], r, zh * nx + xx)

    for d in range(1, nz):
        idx_copy(d).start()
    idx_far.start()
    chain[g] = own[...]
    tiles[z] = idx[...]
    for ch in range(cut):
        @pl.when(reach_right(z) > 0)
        def _(ch=ch):
            right(g, ch).start()

        @pl.when(reach_left(z) > 0)
        def _(ch=ch):
            left(g, ch).start()

    for d in range(1, nx):
        x_back(d).start()

    def first_y(i, carry):
        away = nz - 1 - i
        for o, ok in ((z - away, away <= z), (z + away, (away > 0) & (z + away < nz))):
            @pl.when(ok)
            def _(o=o):
                for d in range(1, ny):
                    y_back(d, o).start()
        return carry

    lax.fori_loop(0, nz, first_y, 0)

    if with_sum:
        ar = sum_stages(split, gr, gout, refs[31:], (r, c, y, z, zh, xc), remote)
        ar[0]()

    table[pl.ds(0, own_count)] = own[...]
    land_y[0] = gsend[pl.ds(y * nz, nz)]
    land_c[0] = gsend[pl.ds(nrow + xc * nh, nh)]

    for d in range(1, nz):
        idx_wait(d).wait_recv()
    idx_far.wait_recv()
    lists = tiles[...].astype(F32)
    along = lists[:nz].reshape(nz * 8, 128).astype(BF16)
    pair = jnp.concatenate([tiles[z].astype(F32), lists[nz]], axis=0).astype(BF16)
    lane = lax.broadcasted_iota(jnp.int32, (128, 128), 0)
    for d in range(ny):
        hot = jnp.where(lane == y_peer(d) * nz + z, 1.0, 0.0).astype(BF16)
        pick_row[d] = dot(along, hot).reshape(nz, 8, 128)
    for d in range(nx):
        hot = jnp.where(lane == nrow + zh * nx + x_peer(d), 1.0, 0.0).astype(BF16)
        pick_col[d] = dot(pair, hot).reshape(2, 8, 128)

    def hot_row(which, k):
        return jnp.where(which[0:1, :] == k, 1.0, 0.0)

    def choose(which, slot):
        total = None
        for k in range(own_count):
            term = chain[slot, k] * hot_row(which, k).astype(BF16)
            total = term if total is None else total + term
        return total

    def forward(src):
        slot = zh * nz + src
        for d in range(ny):
            chosen = choose(pick_row[d, src], slot)
            if d == 0:
                table[own_count + y * nz + src] = chosen
            else:
                stage_y[d, src] = chosen
                y_out(d, src).start()

    def forward_col(s, slot):
        for d in range(nx):
            chosen = choose(pick_col[d, s], slot)
            if d == 0:
                table[col_slot(s, xc)] = chosen
            else:
                stage_c[d, s] = chosen
                c_out(d, s).start()

    def placed(o, k):
        total = None
        for d in range(ny):
            term = land_y[d, o].astype(F32) * hot_row(pick_row[d, o], k)
            total = term if total is None else total + term
        return total

    def placed_col(half, s, k):
        total = None
        for d in range(nx):
            term = land_c[d, half].astype(F32) * hot_row(pick_col[d, s], k)
            total = term if total is None else total + term
        return total

    def y_arrived(o):
        for d in range(1, ny):
            y_back(d, o).wait_recv()

    forward(z)

    def coming(s, way):
        src = lax.rem(g + ring - s if way == 0 else g + s, ring)
        low = lax.rem(src, nz)
        reach = reach_right(low) if way == 0 else reach_left(low)
        return src, low, (s >= 1) & (s <= nz) & (s <= reach), s < reach, lax.div(src, nz) == zh

    def fwd_step(s, ch):
        for way, copy in ((0, right), (1, left)):
            src, low, comes, goes_on, mine = coming(s, way)

            @pl.when(comes)
            def _():
                copy(src, ch).wait_recv()

            @pl.when(comes & goes_on)
            def _():
                copy(src, ch).start()

    def deliver(s):
        for way in range(2):
            src, low, comes, goes_on, mine = coming(s, way)

            @pl.when(comes & mine)
            def _():
                forward(low)

        @pl.when(s == nz)
        def _():
            forward_col(1, lax.rem(g + nz, ring))

    def prepare(t):
        for way in range(2):
            o, low, comes, has_in, mine = coming(nz - t, way)

            @pl.when(comes & mine & (t >= 0))
            def _():
                y_arrived(low)
                for k in range(own_count):
                    ready[way, k] = placed(low, k)

        @pl.when(t == 0)
        def _():
            for d in range(1, nx):
                x_back(d).wait_recv()
            for k in range(own_count):
                far_out[0, k] = placed_col(1 - zh, 1, k).astype(BF16)

    def far_copy(way, o, ch):
        if way == 0:
            return remote(part(far_out, 0, ch), part(in_right, o, ch), b_sl.at[o, ch], br_r.at[o, ch],
                          *at_ring(g - 1))
        return remote(part(far_out, 0, ch), part(in_left, o, ch), b_sr.at[o, ch], bl_r.at[o, ch],
                      *at_ring(g + 1))

    def bwd_step(t, ch):
        for way, copy, got, out in ((0, back_left, in_right, out_left), (1, back_right, in_left, out_right)):
            o, low, comes, has_in, mine = coming(nz - t, way)
            sends = comes & (t >= 0)

            @pl.when(sends & has_in)
            def _():
                copy(o, ch, out).wait_recv()

            @pl.when(sends & has_in & mine)
            def _():
                for k in range(ch * per, ch * per + per):
                    out[o, k] = (ready[way, k] + got[o, k].astype(F32)).astype(BF16)
                copy(o, ch, out).start()

            @pl.when(sends & has_in & jnp.logical_not(mine))
            def _():
                copy(o, ch, got).start()

            @pl.when(sends & jnp.logical_not(has_in) & mine)
            def _():
                for k in range(ch * per, ch * per + per):
                    out[o, k] = ready[way, k].astype(BF16)
                copy(o, ch, out).start()

            @pl.when(sends & jnp.logical_not(has_in) & jnp.logical_not(mine))
            def _():
                far_copy(way, o, ch).start()

    def step(s, carry):
        for ch in range(cut):
            fwd_step(s, ch)
            bwd_step(s - lag, ch)
        deliver(s)

        @pl.when(s == 1)
        def _():
            forward_col(0, g)

        prepare(s + 1 - lag)
        if with_sum:
            for k in range(1, len(ar)):
                @pl.when(s == k)
                def _(k=k):
                    ar[k]()
        return carry

    if lag == 1:
        prepare(0)
    lax.fori_loop(1, max(nz + lag, 10), step, 0)

    y_arrived(z)
    for k in range(own_count):
        back[k] = placed(z, k) + placed_col(zh, 0, k)
    for way, copy, got, some in (
        (0, back_left, in_right, reach_right(z) > 0), (1, back_right, in_left, reach_left(z) > 0)
    ):
        @pl.when(some)
        def _():
            for ch in range(cut):
                copy(g, ch, got).wait_recv()
            for k in range(own_count):
                back[k] += got[g, k].astype(F32)

    def arrive(src, carry):
        for d in range(1, ny):
            y_in(d, src).wait_recv()
            y_out(d, src).wait_send()
            y_back(d, src).wait_send()
        return carry

    lax.fori_loop(0, nz, arrive, 0)

    def sent(s, carry):
        for way, copy, back_copy, buf in ((0, right, back_left, out_left), (1, left, back_right, out_right)):
            src, low, comes, goes_on, mine = coming(s, way)

            @pl.when((comes | (s == 0)) & goes_on)
            def _():
                for ch in range(cut):
                    copy(src, ch).wait_send()

            @pl.when(comes)
            def _():
                for ch in range(cut):
                    back_copy(src, ch, buf).wait_send()
        return carry

    lax.fori_loop(0, nz + 1, sent, 0)
    for d in range(1, nx):
        for s in range(2):
            c_in(d, s).wait_recv()
            c_out(d, s).wait_send()
        x_back(d).wait_send()
    for d in range(1, nz):
        idx_copy(d).wait_send()
    idx_far.wait_send()


def sum_stages(split, gr, gout, refs, where, remote):
    ny, nz, nx = split["y"], split["z"], split["xc"] // 2
    r, c, y, z, zh, xc = where
    core, x = lax.rem(xc, 2), lax.div(xc, 2)
    (a1, v1, a2, v2, a3, a4, a5, v5, w1, w2, s1, r1, s2, r2, s3, r3, s4, r4, s5, r5,
     s6, r6, s7, r7, s8, r8) = refs
    half = gr.shape[0] // 2
    part = half // nx
    piece = part // ny
    sx = split["xc"]
    partner = (1 - zh) * sx + xc
    other = zh * sx + x * 2 + (1 - core)

    def xcol(d):
        xx = lax.rem(x + d, nx)
        return xx, zh * sx + xx * 2 + core

    def yrow(d):
        yy = lax.rem(y + d, ny)
        return yy, yy * nz + z

    def rows_of(i, n):
        return pl.ds(pl.multiple_of(i * n, n), n)

    c1 = remote(gr.at[rows_of(1 - core, half)], a1, s1.at[0], r1.at[0], r, other)

    def c2(d):
        xx, col = xcol(d)
        return remote(v1.at[rows_of(xx, part)], a2.at[(nx - d) % nx], s2.at[d], r2.at[(nx - d) % nx], r, col)

    def c3(d):
        yy, row = yrow(d)
        return remote(v2.at[rows_of(yy, piece)], a3.at[(ny - d) % ny], s3.at[d], r3.at[(ny - d) % ny], row, c)

    def c4(d, slot):
        zz = lax.rem(z + d, nz)
        to = z if slot is None else zz
        return remote(a4.at[z], a4.at[to], s4.at[d], r4.at[to], y * nz + zz, c)

    c5 = remote(v5.at[0], a5, s5.at[0], r5.at[0], r, partner)

    def c6(d, slot):
        yy, row = yrow(d)
        to = y if slot is None else yy
        here = w1.at[rows_of(y, piece)]
        return remote(here, w1.at[rows_of(to, piece)], s6.at[d], r6.at[to], row, c)

    def c7(d, slot):
        xx, col = xcol(d)
        to = x if slot is None else xx
        here = w2.at[rows_of(x, part)]
        return remote(here, w2.at[rows_of(to, part)], s7.at[d], r7.at[to], r, col)

    c8 = remote(w2, gout.at[rows_of(core, half)], s8.at[0], r8.at[0], r, other)
    c8_in = remote(w2, gout.at[rows_of(1 - core, half)], s8.at[0], r8.at[0], r, other)

    def t0():
        c1.start()

    def t1():
        c1.wait_recv()
        v1[...] = gr[rows_of(core, half)] + a1[...]
        for d in range(1, nx):
            c2(d).start()

    def t2():
        total = v1[rows_of(x, part)]
        for d in range(1, nx):
            c2(d).wait_recv()
        for d in range(1, nx):
            total = total + a2[d]
        v2[...] = total
        for d in range(1, ny):
            c3(d).start()

    def t3():
        total = v2[rows_of(y, piece)]
        for d in range(1, ny):
            c3(d).wait_recv()
        for d in range(1, ny):
            total = total + a3[d]
        a4[z] = total
        for d in range(1, nz):
            c4(d, None).start()

    def t4():
        for d in range(1, nz):
            c4(d, 1).wait_recv()
        total = a4[0]
        for i in range(1, nz):
            total = total + a4[i]
        v5[0] = total
        c5.start()

    def t5():
        c5.wait_recv()
        w1[rows_of(y, piece)] = v5[0] + a5[...]
        for d in range(1, ny):
            c6(d, None).start()

    def t6():
        for d in range(1, ny):
            c6(d, 1).wait_recv()
        w2[rows_of(x, part)] = w1[...]
        for d in range(1, nx):
            c7(d, None).start()

    def t7():
        for d in range(1, nx):
            c7(d, 1).wait_recv()
        gout[rows_of(core, half)] = w2[...]
        c8.start()

    def t8():
        c8_in.wait_recv()
        c1.wait_send()
        for d in range(1, nx):
            c2(d).wait_send()
            c7(d, None).wait_send()
        for d in range(1, ny):
            c3(d).wait_send()
            c6(d, None).wait_send()
        for d in range(1, nz):
            c4(d, None).wait_send()
        c5.wait_send()
        c8.wait_send()

    return [t0, t1, t2, t3, t4, t5, t6, t7, t8]


def exchange(split, own, gsend, idx, grads, collective_id):
    ny, nz, nh, nx = split["y"], split["z"], split["zh"], split["xc"]
    own_count, rows, feat = own.shape
    size = own_count + ny * nz + nh * nx
    blocks = (own_count, rows, feat)
    one = (rows, feat)
    dma = pltpu.SemaphoreType.DMA
    ring = nh * nz
    pieces = dma((ring, CUT))
    scratch = [
        pltpu.VMEM((ring,) + blocks, BF16),
        pltpu.VMEM((nz + 1, 8, 128), jnp.int32),
        pltpu.VMEM((ny, nz, 8, 128), F32),
        pltpu.VMEM((nx, 2, 8, 128), F32),
        pltpu.VMEM((ny, nz) + one, BF16),
        pltpu.VMEM((nx, 2) + one, BF16),
        pltpu.VMEM((ny, nz) + one, BF16),
        pltpu.VMEM((nx, nh) + one, BF16),
        pltpu.VMEM((ring,) + blocks, BF16),
        pltpu.VMEM((ring,) + blocks, BF16),
        pltpu.VMEM((ring,) + blocks, BF16),
        pltpu.VMEM((ring,) + blocks, BF16),
        pltpu.VMEM((2,) + blocks, F32),
        pltpu.VMEM((1,) + blocks, BF16),
        dma((nz,)), dma((nz + 1,)), pieces, pieces, pieces,
        dma((ny, nz)), dma((ny, nz)), dma((nx, 2)), dma((nx, 2)),
        dma((ny, nz)), dma((ny, nz)), dma((nx,)), dma((nx,)),
        pieces, pieces, pieces, pieces,
    ]
    out_shape = [
        jax.ShapeDtypeStruct((size, rows, feat), BF16),
        jax.ShapeDtypeStruct(blocks, F32),
    ]
    args = [own, gsend, idx]
    if grads is not None:
        args.append(grads)
        out_shape.append(jax.ShapeDtypeStruct(grads.shape, F32))
        half = grads.shape[0] // 2
        cx = nx // 2
        part = half // cx
        piece = part // ny
        scratch += [
            pltpu.VMEM((half, 128), F32),
            pltpu.VMEM((half, 128), F32),
            pltpu.VMEM((cx, part, 128), F32),
            pltpu.VMEM((part, 128), F32),
            pltpu.VMEM((ny, piece, 128), F32),
            pltpu.VMEM((nz, piece, 128), F32),
            pltpu.VMEM((piece, 128), F32),
            pltpu.VMEM((1, piece, 128), F32),
            pltpu.VMEM((part, 128), F32),
            pltpu.VMEM((half, 128), F32),
            dma((1,)), dma((1,)), dma((cx,)), dma((cx,)), dma((ny,)), dma((ny,)),
            dma((nz,)), dma((nz,)), dma((1,)), dma((1,)), dma((ny,)), dma((ny,)),
            dma((cx,)), dma((cx,)), dma((1,)), dma((1,)),
        ]
    vmem = pl.BlockSpec(memory_space=pltpu.VMEM)
    return pl.pallas_call(
        functools.partial(exchange_kernel, split, LAG, CUT, grads is not None),
        out_shape=out_shape,
        in_specs=[vmem] * len(args),
        out_specs=[vmem] * len(out_shape),
        scratch_shapes=scratch,
        compiler_params=pltpu.CompilerParams(
            collective_id=collective_id, has_side_effects=True, vmem_limit_bytes=LIMIT
        ),
    )(*args)


def grad_slot(split, own_count, t):
    nh, nx = split["zh"], split["xc"]
    first = own_count + split["y"] * split["z"]
    q = t - first
    return jnp.where(t < first, t, first + nh * lax.rem(q, nx) + lax.div(q, nx))


def spread(split, own_count, adj, dst, src, q, grad):
    @pl.loop(0, grad.shape[0])
    def _(i):
        grad[i] = jnp.zeros(grad.shape[1:], F32)

    def one(e, carry):
        grad[grad_slot(split, own_count, src[e])] += dot_at(adj[e], q[dst[e]])
        return carry

    lax.fori_loop(0, adj.shape[0], one, 0, unroll=4)


def gather(adj, dst, src, table, acc):
    def one(e, carry):
        acc[dst[e]] += dot(adj[e], table[src[e]])
        return carry

    lax.fori_loop(0, adj.shape[0], one, 0, unroll=4)


def send_out(own_count, grad, gsend):
    @pl.loop(0, gsend.shape[0])
    def _(i):
        gsend[i] = grad[own_count + i].astype(BF16)


def first_kernel(split, dst, src, adj, cot, deg, u_own, gsend, grad, q):
    own_count = cot.shape[0]
    deg[...] = jnp.ones_like(deg)
    ones = jnp.ones(adj.shape[1:], BF16)

    def one(e, carry):
        deg[dst[e]] += dot(adj[e], ones)
        return carry

    lax.fori_loop(0, adj.shape[0], one, 0, unroll=4)
    for b in range(own_count):
        q[b] = (cot[b].astype(F32) / deg[b]).astype(BF16)
    spread(split, own_count, adj, dst, src, q, grad)
    for b in range(own_count):
        u_own[b] = grad[b] + q[b].astype(F32)
    send_out(own_count, grad, gsend)


def middle_kernel(split, scale, dst, src, adj, feat, table, deg, u_own, u_back, cot,
                  ws1, wn1, ws2, wn2, hidden, base, gsend, grads, acc, grad, q):
    own_count, rows, width = feat.shape
    for b in range(own_count):
        acc[b] = feat[b].astype(F32)
    gather(adj, dst, src, table, acc)
    g1, g2, g3, g4 = 0.0, 0.0, 0.0, 0.0
    for b in range(own_count):
        mean = (acc[b] / deg[b]).astype(BF16)
        pre = dot(feat[b], ws1[...]) + dot(mean, wn1[...])
        s = 1.0 / (1.0 + jnp.exp(-pre))
        hid = (pre * s).astype(BF16)
        hidden[b] = hid
        u = u_own[b] + u_back[b]
        hi = u.astype(BF16)
        lo = (u - hi.astype(F32)).astype(BF16)
        dh = dot_bt(cot[b], ws2[...]) + (dot_bt(hi, wn2[...]) + dot_bt(lo, wn2[...]))
        dpre = (dh * (s * (1.0 + pre * (1.0 - s)))).astype(BF16)
        qb = (dot_bt(dpre, wn1[...]) / deg[b]).astype(BF16)
        q[b] = qb
        base[b] = dot_bt(dpre, ws1[...]) + qb.astype(F32)
        g1 = g1 + dot_at(feat[b], dpre)
        g2 = g2 + dot_at(mean, dpre)
        g3 = g3 + dot_at(hid, cot[b])
        g4 = g4 + (dot_at(hid, hi) + dot_at(hid, lo))
    for i, g in enumerate((g1, g2, g3, g4)):
        grads[pl.ds(i * width, width), :] = g * scale
    spread(split, own_count, adj, dst, src, q, grad)
    for b in range(own_count):
        base[b] += grad[b]
    send_out(own_count, grad, gsend)


def last_kernel(dst, src, adj, hidden, table, deg, base, back, ws2, wn2, out, grad_in, acc):
    own_count = hidden.shape[0]
    for b in range(own_count):
        acc[b] = hidden[b].astype(F32)
    gather(adj, dst, src, table, acc)
    for b in range(own_count):
        mean = (acc[b] / deg[b]).astype(BF16)
        out[b] = (dot(hidden[b], ws2[...]) + dot(mean, wn2[...])).astype(BF16)
        grad_in[b] = base[b] + back[b]


def on_device(body, edges, args, out_shape, scratch):
    smem = pl.BlockSpec(memory_space=pltpu.SMEM)
    vmem = pl.BlockSpec(memory_space=pltpu.VMEM)
    return pl.pallas_call(
        body,
        out_shape=out_shape,
        in_specs=[smem] * len(edges) + [vmem] * len(args),
        out_specs=[vmem] * len(out_shape),
        scratch_shapes=scratch,
        compiler_params=pltpu.CompilerParams(vmem_limit_bytes=LIMIT),
    )(*edges, *args)


def local(
    split,
    nodes,
    features,
    adjacency,
    edge_dst,
    edge_src,
    send_row,
    send_col,
    w_self1,
    w_neigh1,
    w_self2,
    w_neigh2,
    cotangent,
):
    own = features[0, 0]
    adj = adjacency[0, 0]
    edges = (edge_dst[0, 0], edge_src[0, 0])
    cot = cotangent[0, 0]
    own_count, rows, width = own.shape
    lists = jnp.concatenate([send_row.reshape(-1), send_col.reshape(-1)])
    remote_count = lists.size
    idx = jnp.broadcast_to(jnp.pad(lists, (0, 128 - remote_count))[None, :], (8, 128))
    size = own_count + remote_count
    blocks = (own_count, rows, width)
    full = jax.ShapeDtypeStruct(blocks, F32)
    half = jax.ShapeDtypeStruct(blocks, BF16)
    sends = jax.ShapeDtypeStruct((remote_count, rows, width), BF16)
    grad = pltpu.VMEM((size, rows, width), F32)
    acc = pltpu.VMEM(blocks, F32)
    q = pltpu.VMEM(blocks, BF16)
    deg, u_own, gsend = on_device(
        functools.partial(first_kernel, split), edges, (adj, cot), [full, full, sends], [grad, q]
    )
    table, u_back = exchange(split, own, gsend, idx, None, 0)
    weights = jax.ShapeDtypeStruct((4 * width, width), F32)
    hidden, base, gsend, grads = on_device(
        functools.partial(middle_kernel, split, 1.0 / math.sqrt(nodes)),
        edges,
        (adj, own, table, deg, u_own, u_back, cot, w_self1, w_neigh1, w_self2, w_neigh2),
        [half, full, sends, weights],
        [acc, grad, q],
    )
    table, back, grads = exchange(split, hidden, gsend, idx, grads, 1)
    out, grad_in = on_device(
        last_kernel,
        edges,
        (adj, hidden, table, deg, base, back, w_self2, w_neigh2),
        [half, full],
        [acc],
    )
    g = grads.reshape(4, width, width)
    return (
        out.reshape(features.shape),
        grad_in.reshape(features.shape),
        g[0],
        g[1],
        g[2],
        g[3],
    )


def solution(mesh):
    blocked = P("row", "col", None, None, None)
    placed = (
        blocked,
        blocked,
        P("row", "col", None),
        P("row", "col", None),
        P("row", "col", None, None),
        P("row", "col", None, None),
        P(),
        P(),
        P(),
        P(),
        blocked,
    )

    def whole(*args):
        shape = args[0].shape
        nodes = shape[0] * shape[1] * shape[2] * shape[3]
        return jax.shard_map(
            functools.partial(local, SPLIT, nodes),
            mesh=mesh,
            in_specs=placed,
            out_specs=(blocked, blocked, P(), P(), P(), P()),
            check_vma=False,
        )(*args)

    return whole
```

```python
import functools
import math

import jax
import jax.numpy as jnp
from jax import lax
from jax.experimental import pallas as pl
from jax.experimental.pallas import tpu as pltpu
from jax.sharding import PartitionSpec as P

MESH = pl.DeviceIdType.MESH
BF16 = jnp.bfloat16
F32 = jnp.float32
LIMIT = 52 * 1024 * 1024
SPLIT = {"y": 4, "z": 8, "zh": 2, "xc": 8}
CUT = 2
UNIT = 16


def dot(a, b):
    return jnp.dot(a, b, preferred_element_type=F32)


def dot_bt(a, b):
    return lax.dot_general(a, b, (((1,), (1,)), ((), ())), preferred_element_type=F32)


def dot_at(a, b):
    return lax.dot_general(a, b, (((0,), (0,)), ((), ())), preferred_element_type=F32)


class Place:
    def __init__(self, split):
        self.split = split
        self.ny, self.nz, self.nh, self.nx = split["y"], split["z"], split["zh"], split["xc"]
        self.nrow, self.ring = self.ny * self.nz, self.nh * self.nz
        self.r = lax.axis_index("row")
        self.c = lax.axis_index("col")
        self.y, self.z = lax.div(self.r, self.nz), lax.rem(self.r, self.nz)
        self.zh, self.xc = lax.div(self.c, self.nx), lax.rem(self.c, self.nx)
        self.g = self.zh * self.nz + self.z
        self.partner = (1 - self.zh) * self.nx + self.xc

    def y_peer(self, d):
        return lax.rem(self.y + d, self.ny)

    def x_peer(self, d):
        return lax.rem(self.xc + d, self.nx)

    def at_ring(self, pos):
        pos = lax.rem(pos + self.ring, self.ring)
        return self.y * self.nz + lax.rem(pos, self.nz), lax.div(pos, self.nz) * self.nx + self.xc

    def reach_right(self, src):
        return jnp.where(src < self.nz // 2, self.nz, self.nz - 1 - src)

    def reach_left(self, src):
        return jnp.where(src < self.nz // 2, src, self.nz)


def remote(src, dst, ssem, rsem, row, col):
    return pltpu.make_async_remote_copy(
        src_ref=src, dst_ref=dst, send_sem=ssem, recv_sem=rsem,
        device_id=(row, col), device_id_type=MESH,
    )


def greet_all(place):
    barrier = pltpu.get_barrier_semaphore()
    y, z, zh, g, r, c = place.y, place.z, place.zh, place.g, place.r, place.c
    ny, nz, nx = place.ny, place.nz, place.nx

    def greet(row, col):
        pl.semaphore_signal(barrier, inc=1, device_id=(row, col), device_id_type=MESH)

    greet(r, place.partner)
    for d in range(1, nz):
        greet(y * nz + lax.rem(z + d, nz), c)
    for d in range(1, ny):
        greet(place.y_peer(d) * nz + z, c)
    for d in range(1, nx):
        greet(r, zh * nx + place.x_peer(d))

    @pl.when(z == 0)
    def _():
        greet(*place.at_ring(g - 1))

    @pl.when(z == nz - 1)
    def _():
        greet(*place.at_ring(g + 1))


def await_all(place):
    barrier = pltpu.get_barrier_semaphore()
    met = (place.ny - 1) + (place.nz - 1) + 1 + (place.nx - 1)
    at_end = (place.z == 0) | (place.z == place.nz - 1)

    @pl.when(at_end)
    def _():
        pl.semaphore_wait(barrier, met + 1)

    @pl.when(jnp.logical_not(at_end))
    def _():
        pl.semaphore_wait(barrier, met)


def phase(place, cut, own, table, back, picks, scratch, lists, fill, sums):
    ny, nz, nh, nx = place.ny, place.nz, place.nh, place.nx
    nrow, ring = place.nrow, place.ring
    r, c, y, z, zh, xc, g = place.r, place.c, place.y, place.z, place.zh, place.xc, place.g
    y_peer, x_peer, at_ring = place.y_peer, place.x_peer, place.at_ring
    reach_right, reach_left = place.reach_right, place.reach_left
    pick_row, pick_col = picks
    (gsend, chain, stage_y, stage_c, land_y, land_c, in_right, in_left,
     out_left, out_right, ready, far_out,
     f_r, f_sr, f_sl, yf_s, yf_r, cf_s, cf_r, yb_s, yb_r, cb_s, cb_r,
     br_r, bl_r, b_sl, b_sr) = scratch
    own_count, rows, feat = own.shape
    per = own_count // cut

    def part(ref, slot, ch):
        return ref.at[slot, pl.ds(ch * per, per)]

    def right(src, ch):
        ref = part(chain, src, ch)
        return remote(ref, ref, f_sr.at[src, ch], f_r.at[src, ch], *at_ring(g + 1))

    def left(src, ch):
        ref = part(chain, src, ch)
        return remote(ref, ref, f_sl.at[src, ch], f_r.at[src, ch], *at_ring(g - 1))

    def back_left(o, ch, buf):
        return remote(part(buf, o, ch), part(in_right, o, ch), b_sl.at[o, ch], br_r.at[o, ch],
                      *at_ring(g - 1))

    def back_right(o, ch, buf):
        return remote(part(buf, o, ch), part(in_left, o, ch), b_sr.at[o, ch], bl_r.at[o, ch],
                      *at_ring(g + 1))

    def y_back(d, o):
        yy = y_peer(d)
        return remote(gsend.at[yy * nz + o], land_y.at[(ny - d) % ny, o],
                      yb_s.at[d, o], yb_r.at[(ny - d) % ny, o], yy * nz + z, c)

    def x_back(d):
        xx = x_peer(d)
        return remote(gsend.at[pl.ds(nrow + xx * nh, nh)], land_c.at[(nx - d) % nx],
                      cb_s.at[d], cb_r.at[(nx - d) % nx], r, zh * nx + xx)

    def y_out(d, src):
        return remote(stage_y.at[d, src], table.at[own_count + y * nz + src],
                      yf_s.at[d, src], yf_r.at[d, src], y_peer(d) * nz + z, c)

    def y_in(d, src):
        yy = lax.rem(y + ny - d, ny)
        return remote(stage_y.at[d, src], table.at[own_count + yy * nz + src],
                      yf_s.at[d, src], yf_r.at[d, src], yy * nz + z, c)

    def col_slot(s, x_from):
        half = zh if s == 0 else 1 - zh
        return own_count + nrow + half * nx + x_from

    def c_out(d, s):
        return remote(stage_c.at[d, s], table.at[col_slot(s, xc)],
                      cf_s.at[d, s], cf_r.at[d, s], r, zh * nx + x_peer(d))

    def c_in(d, s):
        xx = lax.rem(xc + nx - d, nx)
        return remote(stage_c.at[d, s], table.at[col_slot(s, xx)],
                      cf_s.at[d, s], cf_r.at[d, s], r, zh * nx + xx)

    chain[g] = own[...]
    for ch in range(cut):
        @pl.when(reach_right(z) > 0)
        def _(ch=ch):
            right(g, ch).start()

        @pl.when(reach_left(z) > 0)
        def _(ch=ch):
            left(g, ch).start()

    fill(gsend)
    for d in range(1, nx):
        x_back(d).start()

    def first_y(i, carry):
        away = nz - 1 - i
        for o, ok in ((z - away, away <= z), (z + away, (away > 0) & (z + away < nz))):
            @pl.when(ok)
            def _(o=o):
                for d in range(1, ny):
                    y_back(d, o).start()
        return carry

    lax.fori_loop(0, nz, first_y, 0)

    if sums is not None:
        sums[0]()

    table[pl.ds(0, own_count)] = own[...]
    land_y[0] = gsend[pl.ds(y * nz, nz)]
    land_c[0] = gsend[pl.ds(nrow + xc * nh, nh)]

    def hot_row(which, k):
        return jnp.where(which[0:1, :] == k, 1.0, 0.0)

    def choose(which, slot):
        total = None
        for k in range(own_count):
            term = chain[slot, k] * hot_row(which, k).astype(BF16)
            total = term if total is None else total + term
        return total

    def forward(src):
        slot = zh * nz + src
        for d in range(ny):
            chosen = choose(pick_row[d, src], slot)
            if d == 0:
                table[own_count + y * nz + src] = chosen
            else:
                stage_y[d, src] = chosen
                y_out(d, src).start()

    def forward_col(s, slot):
        for d in range(nx):
            chosen = choose(pick_col[d, s], slot)
            if d == 0:
                table[col_slot(s, xc)] = chosen
            else:
                stage_c[d, s] = chosen
                c_out(d, s).start()

    def placed(o, k):
        total = None
        for d in range(ny):
            term = land_y[d, o].astype(F32) * hot_row(pick_row[d, o], k)
            total = term if total is None else total + term
        return total

    def placed_col(half, s, k):
        total = None
        for d in range(nx):
            term = land_c[d, half].astype(F32) * hot_row(pick_col[d, s], k)
            total = term if total is None else total + term
        return total

    def y_arrived(o):
        for d in range(1, ny):
            y_back(d, o).wait_recv()

    def coming(s, way):
        src = lax.rem(g + ring - s if way == 0 else g + s, ring)
        low = lax.rem(src, nz)
        reach = reach_right(low) if way == 0 else reach_left(low)
        return src, low, (s >= 1) & (s <= nz) & (s <= reach), s < reach, lax.div(src, nz) == zh

    def fwd_step(s, ch):
        for way, copy in ((0, right), (1, left)):
            src, low, comes, goes_on, mine = coming(s, way)

            @pl.when(comes)
            def _():
                copy(src, ch).wait_recv()

            @pl.when(comes & goes_on)
            def _():
                copy(src, ch).start()

    def deliver(s):
        for way in range(2):
            src, low, comes, goes_on, mine = coming(s, way)

            @pl.when(comes & mine)
            def _():
                forward(low)

        @pl.when(s == nz)
        def _():
            forward_col(1, lax.rem(g + nz, ring))

    def prepare(t):
        for way in range(2):
            o, low, comes, has_in, mine = coming(nz - t, way)

            @pl.when(comes & mine & (t >= 0))
            def _():
                y_arrived(low)
                for k in range(own_count):
                    ready[way, k] = placed(low, k)

        @pl.when(t == 0)
        def _():
            for d in range(1, nx):
                x_back(d).wait_recv()
            for k in range(own_count):
                far_out[0, k] = placed_col(1 - zh, 1, k).astype(BF16)

    def far_copy(way, o, ch):
        if way == 0:
            return remote(part(far_out, 0, ch), part(in_right, o, ch), b_sl.at[o, ch], br_r.at[o, ch],
                          *at_ring(g - 1))
        return remote(part(far_out, 0, ch), part(in_left, o, ch), b_sr.at[o, ch], bl_r.at[o, ch],
                      *at_ring(g + 1))

    def bwd_step(t, ch):
        for way, copy, got, out in ((0, back_left, in_right, out_left), (1, back_right, in_left, out_right)):
            o, low, comes, has_in, mine = coming(nz - t, way)
            sends = comes & (t >= 0)

            @pl.when(sends & has_in)
            def _():
                copy(o, ch, out).wait_recv()

            @pl.when(sends & has_in & mine)
            def _():
                for k in range(ch * per, ch * per + per):
                    out[o, k] = (ready[way, k] + got[o, k].astype(F32)).astype(BF16)
                copy(o, ch, out).start()

            @pl.when(sends & has_in & jnp.logical_not(mine))
            def _():
                copy(o, ch, got).start()

            @pl.when(sends & jnp.logical_not(has_in) & mine)
            def _():
                for k in range(ch * per, ch * per + per):
                    out[o, k] = ready[way, k].astype(BF16)
                copy(o, ch, out).start()

            @pl.when(sends & jnp.logical_not(has_in) & jnp.logical_not(mine))
            def _():
                far_copy(way, o, ch).start()

    def step(s, carry):
        for ch in range(cut):
            @pl.when(s > 1)
            def _(ch=ch):
                fwd_step(s, ch)

            bwd_step(s - 1, ch)
        prepare(s)
        deliver(s)
        if sums is not None:
            for k in range(1, len(sums)):
                @pl.when(s == k)
                def _(k=k):
                    sums[k]()
        return carry

    for ch in range(cut):
        fwd_step(1, ch)
    if lists is not None:
        lists()
    prepare(0)
    forward(z)
    forward_col(0, g)
    lax.fori_loop(1, max(nz + 1, 9 if sums is None else 10), step, 0)

    y_arrived(z)
    for k in range(own_count):
        back[k] = placed(z, k) + placed_col(zh, 0, k)
    for way, copy, got, some in (
        (0, back_left, in_right, reach_right(z) > 0), (1, back_right, in_left, reach_left(z) > 0)
    ):
        @pl.when(some)
        def _():
            for ch in range(cut):
                copy(g, ch, got).wait_recv()
            for k in range(own_count):
                back[k] += got[g, k].astype(F32)

    def arrive(src, carry):
        for d in range(1, ny):
            y_in(d, src).wait_recv()
            y_out(d, src).wait_send()
            y_back(d, src).wait_send()
        return carry

    lax.fori_loop(0, nz, arrive, 0)

    def sent(s, carry):
        for way, copy, back_copy, buf in ((0, right, back_left, out_left), (1, left, back_right, out_right)):
            src, low, comes, goes_on, mine = coming(s, way)

            @pl.when((comes | (s == 0)) & goes_on)
            def _():
                for ch in range(cut):
                    copy(src, ch).wait_send()

            @pl.when(comes)
            def _():
                for ch in range(cut):
                    back_copy(src, ch, buf).wait_send()
        return carry

    lax.fori_loop(0, nz + 1, sent, 0)
    for d in range(1, nx):
        for s in range(2):
            c_in(d, s).wait_recv()
            c_out(d, s).wait_send()
        x_back(d).wait_send()


def list_exchange(place, idx, tiles, picks, i_s, i_r):
    ny, nz, nx, nrow = place.ny, place.nz, place.nx, place.nrow
    y, z, zh, r, c = place.y, place.z, place.zh, place.r, place.c
    pick_row, pick_col = picks

    def idx_copy(d):
        zz = lax.rem(z + d, nz)
        return remote(idx, tiles.at[z], i_s.at[d], i_r.at[z], y * nz + zz, c)

    def idx_wait(d):
        zz = lax.rem(z + d, nz)
        return remote(idx, tiles.at[zz], i_s.at[d], i_r.at[zz], y * nz + zz, c)

    idx_far = remote(idx, tiles.at[nz], i_s.at[0], i_r.at[nz], r, place.partner)

    def send():
        idx_far.start()
        for d in range(1, nz):
            idx_copy(d).start()
        tiles[z] = idx[...]

    def pick():
        for d in range(1, nz):
            idx_wait(d).wait_recv()
        idx_far.wait_recv()
        lists = tiles[...].astype(F32)
        along = lists[:nz].reshape(nz * 8, 128).astype(BF16)
        pair = jnp.concatenate([tiles[z].astype(F32), lists[nz]], axis=0).astype(BF16)
        lane = lax.broadcasted_iota(jnp.int32, (128, 128), 0)
        for d in range(ny):
            hot = jnp.where(lane == place.y_peer(d) * nz + z, 1.0, 0.0).astype(BF16)
            pick_row[d] = dot(along, hot).reshape(nz, 8, 128)
        for d in range(nx):
            hot = jnp.where(lane == nrow + zh * nx + place.x_peer(d), 1.0, 0.0).astype(BF16)
            pick_col[d] = dot(pair, hot).reshape(2, 8, 128)
        for d in range(1, nz):
            idx_copy(d).wait_send()
        idx_far.wait_send()

    return send, pick


def sum_stages(place, gr, gout, refs):
    ny, nz, sx = place.ny, place.nz, place.nx
    nx = sx // 2
    r, c, y, z, zh, xc = place.r, place.c, place.y, place.z, place.zh, place.xc
    core, x = lax.rem(xc, 2), lax.div(xc, 2)
    (a1, v1, a2, v2, a3, a4, a5, v5, w1, w2, s1, r1, s2, r2, s3, r3, s4, r4, s5, r5,
     s6, r6, s7, r7, s8, r8) = refs
    half = gr.shape[0] // 2
    part = half // nx
    piece = part // ny
    other = zh * sx + x * 2 + (1 - core)

    def xcol(d):
        xx = lax.rem(x + d, nx)
        return xx, zh * sx + xx * 2 + core

    def yrow(d):
        yy = lax.rem(y + d, ny)
        return yy, yy * nz + z

    def rows_of(i, n):
        return pl.ds(i * n, n)

    c1 = remote(gr.at[rows_of(1 - core, half)], a1, s1.at[0], r1.at[0], r, other)

    def c2(d):
        xx, col = xcol(d)
        return remote(v1.at[rows_of(xx, part)], a2.at[(nx - d) % nx], s2.at[d], r2.at[(nx - d) % nx], r, col)

    def c3(d):
        yy, row = yrow(d)
        return remote(v2.at[rows_of(yy, piece)], a3.at[(ny - d) % ny], s3.at[d], r3.at[(ny - d) % ny], row, c)

    def c4(d, slot):
        zz = lax.rem(z + d, nz)
        to = z if slot is None else zz
        return remote(a4.at[z], a4.at[to], s4.at[d], r4.at[to], y * nz + zz, c)

    c5 = remote(v5.at[0], a5, s5.at[0], r5.at[0], r, place.partner)

    def c6(d, slot):
        yy, row = yrow(d)
        to = y if slot is None else yy
        here = w1.at[rows_of(y, piece)]
        return remote(here, w1.at[rows_of(to, piece)], s6.at[d], r6.at[to], row, c)

    def c7(d, slot):
        xx, col = xcol(d)
        to = x if slot is None else xx
        here = w2.at[rows_of(x, part)]
        return remote(here, w2.at[rows_of(to, part)], s7.at[d], r7.at[to], r, col)

    c8 = remote(w2, gout.at[rows_of(core, half)], s8.at[0], r8.at[0], r, other)
    c8_in = remote(w2, gout.at[rows_of(1 - core, half)], s8.at[0], r8.at[0], r, other)

    def t0():
        c1.start()

    def t1():
        c1.wait_recv()
        v1[...] = gr[rows_of(core, half)] + a1[...]
        for d in range(1, nx):
            c2(d).start()

    def t2():
        total = v1[rows_of(x, part)]
        for d in range(1, nx):
            c2(d).wait_recv()
        for d in range(1, nx):
            total = total + a2[d]
        v2[...] = total
        for d in range(1, ny):
            c3(d).start()

    def t3():
        total = v2[rows_of(y, piece)]
        for d in range(1, ny):
            c3(d).wait_recv()
        for d in range(1, ny):
            total = total + a3[d]
        a4[z] = total
        for d in range(1, nz):
            c4(d, None).start()

    def t4():
        for d in range(1, nz):
            c4(d, 1).wait_recv()
        total = a4[0]
        for i in range(1, nz):
            total = total + a4[i]
        v5[0] = total
        c5.start()

    def t5():
        c5.wait_recv()
        w1[rows_of(y, piece)] = v5[0] + a5[...]
        for d in range(1, ny):
            c6(d, None).start()

    def t6():
        for d in range(1, ny):
            c6(d, 1).wait_recv()
        w2[rows_of(x, part)] = w1[...]
        for d in range(1, nx):
            c7(d, None).start()

    def t7():
        for d in range(1, nx):
            c7(d, 1).wait_recv()
        gout[rows_of(core, half)] = w2[...]
        c8.start()

    def t8():
        c8_in.wait_recv()
        c1.wait_send()
        for d in range(1, nx):
            c2(d).wait_send()
            c7(d, None).wait_send()
        for d in range(1, ny):
            c3(d).wait_send()
            c6(d, None).wait_send()
        for d in range(1, nz):
            c4(d, None).wait_send()
        c5.wait_send()
        c8.wait_send()

    return [t0, t1, t2, t3, t4, t5, t6, t7, t8]


class Links:
    def __init__(self, meta, edges, own_count):
        self.meta, self.edges, self.own_count = meta, edges, own_count

    def prev_dst(self, e):
        return self.meta[e]

    def prev_slot(self, e):
        return self.meta[self.edges + e]

    def last_dst(self, b):
        return self.meta[2 * self.edges + b]

    def last_slot(self, i):
        return self.meta[2 * self.edges + self.own_count + i]


def edge_links(split, own_count, size, dst, src):
    edges = dst.size
    slot = grad_slot(split, own_count, src)
    e = jnp.arange(edges, dtype=jnp.int32)
    early = e[None, :] < e[:, None]

    def latest(match):
        found = jnp.max(jnp.where(match, e[None, :], -1), axis=1)
        return jnp.where(found < 0, edges, found)

    return jnp.concatenate([
        latest((dst[None, :] == dst[:, None]) & early),
        latest((slot[None, :] == slot[:, None]) & early),
        latest(dst[None, :] == jnp.arange(own_count, dtype=jnp.int32)[:, None]),
        latest(slot[None, :] == jnp.arange(size, dtype=jnp.int32)[:, None]),
    ])


def grad_slot(split, own_count, t):
    nh, nx = split["zh"], split["xc"]
    first = own_count + split["y"] * split["z"]
    q = t - first
    return jnp.where(t < first, t, first + nh * lax.rem(q, nx) + lax.div(q, nx))


def running(edges, run, term, prev):
    def one(e, carry):
        run[e] = term(e) + run[prev(e)]
        return carry

    lax.fori_loop(0, edges, one, 0, unroll=4)


def spread(links, adj, dst, q, run):
    running(links.edges, run, lambda e: dot_at(adj[e], q[dst[e]]), links.prev_slot)


def gather(links, adj, src, table, run):
    running(links.edges, run, lambda e: dot(adj[e], table[src[e]]), links.prev_dst)


def send_out(links, own_count, run, gsend):
    @pl.loop(0, gsend.shape[0])
    def _(i):
        gsend[i] = run[links.last_slot(own_count + i)].astype(BF16)


def main_kernel(split, scale, n_phase, dst, src, meta, adj, feat, cot, idx, ws1, wn1, ws2, wn2,
                hidden, table2, deg, base, back, gout, *scratch):
    place = Place(split)
    greet_all(place)
    scratch = list(scratch)
    table1, u_own, u_back, q, keep, grads, run_d, run_s, tiles, pick_row, pick_col, i_s, i_r = scratch[:13]
    first, second, rest = scratch[13:13 + n_phase], scratch[13 + n_phase:13 + 2 * n_phase], scratch[13 + 2 * n_phase:]
    picks = (pick_row, pick_col)
    own_count, rows, width = feat.shape
    edges = adj.shape[0]
    links = Links(meta, edges, own_count)
    run_d[edges] = jnp.zeros((rows, width), F32)
    run_s[edges] = jnp.zeros((rows, width), F32)

    ones = jnp.ones((rows, rows), BF16)
    running(edges, run_d, lambda e: dot(adj[e], ones), links.prev_dst)
    for b in range(own_count):
        deg[b] = 1.0 + run_d[links.last_dst(b)]
        q[b] = (cot[b].astype(F32) / deg[b]).astype(BF16)
    spread(links, adj, dst, q, run_s)
    for b in range(own_count):
        u_own[b] = run_s[links.last_slot(b)] + q[b].astype(F32)
    send_out(links, own_count, run_s, first[0])

    await_all(place)
    send, pick = list_exchange(place, idx, tiles, picks, i_s, i_r)
    send()
    phase(place, CUT, feat, table1, u_back, picks, first, pick, lambda gsend: None, None)

    gather(links, adj, src, table1, run_d)
    for b in range(own_count):
        mean = ((feat[b].astype(F32) + run_d[links.last_dst(b)]) / deg[b]).astype(BF16)
        pre = dot(feat[b], ws1[...]) + dot(mean, wn1[...])
        s = 1.0 / (1.0 + jnp.exp(-pre))
        hid = (pre * s).astype(BF16)
        hidden[b] = hid
        u = u_own[b] + u_back[b]
        hi = u.astype(BF16)
        lo = (u - hi.astype(F32)).astype(BF16)
        dh = dot_bt(cot[b], ws2[...]) + (dot_bt(hi, wn2[...]) + dot_bt(lo, wn2[...]))
        dpre = (dh * (s * (1.0 + pre * (1.0 - s)))).astype(BF16)
        qb = (dot_bt(dpre, wn1[...]) / deg[b]).astype(BF16)
        q[b] = qb
        base[b] = dot_bt(dpre, ws1[...]) + qb.astype(F32)
        keep[0, b] = dpre
        keep[1, b] = mean
        keep[2, b] = hi
        keep[3, b] = lo
    def weights(b, total):
        dpre = keep[0, b]
        return (
            total[0] + dot_at(feat[b], dpre),
            total[1] + dot_at(keep[1, b], dpre),
            total[2] + dot_at(hidden[b], cot[b]),
            total[3] + (dot_at(hidden[b], keep[2, b]) + dot_at(hidden[b], keep[3, b])),
        )

    zero = jnp.zeros((width, width), F32)
    for i, part in enumerate(lax.fori_loop(0, own_count, weights, (zero,) * 4)):
        grads[pl.ds(i * width // UNIT, width // UNIT)] = (part * scale).reshape(width // UNIT, UNIT, width)

    def fill(gsend):
        spread(links, adj, dst, q, run_s)
        for b in range(own_count):
            base[b] += run_s[links.last_slot(b)]
        send_out(links, own_count, run_s, gsend)

    phase(place, CUT, hidden, table2, back, picks, second, None, fill,
          sum_stages(place, grads, gout, rest))


def phase_scratch(split, own_count, rows, feat):
    ny, nz, nh, nx = split["y"], split["z"], split["zh"], split["xc"]
    ring = nh * nz
    blocks = (own_count, rows, feat)
    one = (rows, feat)
    dma = pltpu.SemaphoreType.DMA
    pieces = dma((ring, CUT))
    return [
        pltpu.VMEM((ny * nz + nh * nx,) + one, BF16),
        pltpu.VMEM((ring,) + blocks, BF16),
        pltpu.VMEM((ny, nz) + one, BF16),
        pltpu.VMEM((nx, 2) + one, BF16),
        pltpu.VMEM((ny, nz) + one, BF16),
        pltpu.VMEM((nx, nh) + one, BF16),
        pltpu.VMEM((ring,) + blocks, BF16),
        pltpu.VMEM((ring,) + blocks, BF16),
        pltpu.VMEM((ring,) + blocks, BF16),
        pltpu.VMEM((ring,) + blocks, BF16),
        pltpu.VMEM((2,) + blocks, F32),
        pltpu.VMEM((1,) + blocks, BF16),
        pieces, pieces, pieces,
        dma((ny, nz)), dma((ny, nz)), dma((nx, 2)), dma((nx, 2)),
        dma((ny, nz)), dma((ny, nz)), dma((nx,)), dma((nx,)),
        pieces, pieces, pieces, pieces,
    ]


def sum_scratch(split, units):
    ny, nz, cx = split["y"], split["z"], split["xc"] // 2
    half = units // 2
    part = half // cx
    piece = part // ny
    dma = pltpu.SemaphoreType.DMA
    return [
        pltpu.VMEM((half, UNIT, 128), F32),
        pltpu.VMEM((half, UNIT, 128), F32),
        pltpu.VMEM((cx, part, UNIT, 128), F32),
        pltpu.VMEM((part, UNIT, 128), F32),
        pltpu.VMEM((ny, piece, UNIT, 128), F32),
        pltpu.VMEM((nz, piece, UNIT, 128), F32),
        pltpu.VMEM((piece, UNIT, 128), F32),
        pltpu.VMEM((1, piece, UNIT, 128), F32),
        pltpu.VMEM((part, UNIT, 128), F32),
        pltpu.VMEM((half, UNIT, 128), F32),
        dma((1,)), dma((1,)), dma((cx,)), dma((cx,)), dma((ny,)), dma((ny,)),
        dma((nz,)), dma((nz,)), dma((1,)), dma((1,)), dma((ny,)), dma((ny,)),
        dma((cx,)), dma((cx,)), dma((1,)), dma((1,)),
    ]


def last_kernel(dst, src, meta, adj, hidden, table, deg, base, back, grads, ws2, wn2,
                out, grad_in, g1, g2, g3, g4, run):
    own_count, rows, width = hidden.shape
    edges = adj.shape[0]
    links = Links(meta, edges, own_count)
    run[edges] = jnp.zeros((rows, width), F32)
    gather(links, adj, src, table, run)
    for b in range(own_count):
        mean = ((hidden[b].astype(F32) + run[links.last_dst(b)]) / deg[b]).astype(BF16)
        out[b] = (dot(hidden[b], ws2[...]) + dot(mean, wn2[...])).astype(BF16)
        grad_in[b] = base[b] + back[b]
    for i, g in enumerate((g1, g2, g3, g4)):
        g[...] = grads[pl.ds(i * width // UNIT, width // UNIT)].reshape(width, width)


def call(body, edges, args, out_shape, scratch, params):
    smem = pl.BlockSpec(memory_space=pltpu.SMEM)
    vmem = pl.BlockSpec(memory_space=pltpu.VMEM)
    return pl.pallas_call(
        body,
        out_shape=out_shape,
        in_specs=[smem] * len(edges) + [vmem] * len(args),
        out_specs=[vmem] * len(out_shape),
        scratch_shapes=scratch,
        compiler_params=pltpu.CompilerParams(vmem_limit_bytes=LIMIT, **params),
    )(*edges, *args)


def local(
    split,
    nodes,
    features,
    adjacency,
    edge_dst,
    edge_src,
    send_row,
    send_col,
    w_self1,
    w_neigh1,
    w_self2,
    w_neigh2,
    cotangent,
):
    own = features[0, 0]
    adj = adjacency[0, 0]
    dst, src = edge_dst[0, 0], edge_src[0, 0]
    cot = cotangent[0, 0]
    own_count, rows, width = own.shape
    lists = jnp.concatenate([send_row.reshape(-1), send_col.reshape(-1)])
    remote_count = lists.size
    idx = jnp.broadcast_to(jnp.pad(lists, (0, 128 - remote_count))[None, :], (8, 128))
    size = own_count + remote_count
    edges = (dst, src, edge_links(split, own_count, size, dst, src))
    blocks = (own_count, rows, width)
    full = jax.ShapeDtypeStruct(blocks, F32)
    half = jax.ShapeDtypeStruct(blocks, BF16)
    weight = jax.ShapeDtypeStruct((width, width), F32)
    run = pltpu.VMEM((adj.shape[0] + 1, rows, width), F32)
    ny, nz, nx = split["y"], split["z"], split["xc"]
    dma = pltpu.SemaphoreType.DMA
    per_phase = phase_scratch(split, own_count, rows, width)
    scratch = [
        pltpu.VMEM((size, rows, width), BF16),
        pltpu.VMEM(blocks, F32),
        pltpu.VMEM(blocks, F32),
        pltpu.VMEM(blocks, BF16),
        pltpu.VMEM((4,) + blocks, BF16),
        pltpu.VMEM((4 * width // UNIT, UNIT, width), F32),
        run,
        run,
        pltpu.VMEM((nz + 1, 8, 128), jnp.int32),
        pltpu.VMEM((ny, nz, 8, 128), F32),
        pltpu.VMEM((nx, 2, 8, 128), F32),
        dma((nz,)),
        dma((nz + 1,)),
    ] + per_phase + per_phase + sum_scratch(split, 4 * width // UNIT)
    hidden, table, deg, base, back, grads = call(
        functools.partial(main_kernel, split, 1.0 / math.sqrt(nodes), len(per_phase)),
        edges,
        (adj, own, cot, idx, w_self1, w_neigh1, w_self2, w_neigh2),
        [half, jax.ShapeDtypeStruct((size, rows, width), BF16), full, full, full,
         jax.ShapeDtypeStruct((4 * width // UNIT, UNIT, width), F32)],
        scratch,
        dict(collective_id=0, has_side_effects=True),
    )
    out, grad_in, g1, g2, g3, g4 = call(
        last_kernel,
        edges,
        (adj, hidden, table, deg, base, back, grads, w_self2, w_neigh2),
        [half, full, weight, weight, weight, weight],
        [run],
        {},
    )
    return out.reshape(features.shape), grad_in.reshape(features.shape), g1, g2, g3, g4


def solution(mesh):
    blocked = P("row", "col", None, None, None)
    placed = (
        blocked,
        blocked,
        P("row", "col", None),
        P("row", "col", None),
        P("row", "col", None, None),
        P("row", "col", None, None),
        P(),
        P(),
        P(),
        P(),
        blocked,
    )

    def whole(*args):
        shape = args[0].shape
        nodes = shape[0] * shape[1] * shape[2] * shape[3]
        return jax.shard_map(
            functools.partial(local, SPLIT, nodes),
            mesh=mesh,
            in_specs=placed,
            out_specs=(blocked, blocked, P(), P(), P(), P()),
            check_vma=False,
        )(*args)

    return whole
```

```python
import functools
import math

import jax
import jax.numpy as jnp
from jax import lax
from jax.experimental import pallas as pl
from jax.experimental.pallas import tpu as pltpu
from jax.sharding import PartitionSpec as P

MESH = pl.DeviceIdType.MESH
BF16 = jnp.bfloat16
F32 = jnp.float32
LIMIT = 52 * 1024 * 1024
SPLIT = {"y": 4, "z": 8, "zh": 2, "xc": 8}
CUT = 2
UNIT = 16


def dot(a, b):
    return jnp.dot(a, b, preferred_element_type=F32)


def dot_bt(a, b):
    return lax.dot_general(a, b, (((1,), (1,)), ((), ())), preferred_element_type=F32)


def dot_at(a, b):
    return lax.dot_general(a, b, (((0,), (0,)), ((), ())), preferred_element_type=F32)


class Place:
    def __init__(self, split):
        self.split = split
        self.ny, self.nz, self.nh, self.nx = split["y"], split["z"], split["zh"], split["xc"]
        self.nrow, self.ring = self.ny * self.nz, self.nh * self.nz
        self.r = lax.axis_index("row")
        self.c = lax.axis_index("col")
        self.y, self.z = lax.div(self.r, self.nz), lax.rem(self.r, self.nz)
        self.zh, self.xc = lax.div(self.c, self.nx), lax.rem(self.c, self.nx)
        self.g = self.zh * self.nz + self.z
        self.partner = (1 - self.zh) * self.nx + self.xc

    def y_peer(self, d):
        return lax.rem(self.y + d, self.ny)

    def x_peer(self, d):
        return lax.rem(self.xc + d, self.nx)

    def at_ring(self, pos):
        pos = lax.rem(pos + self.ring, self.ring)
        return self.y * self.nz + lax.rem(pos, self.nz), lax.div(pos, self.nz) * self.nx + self.xc

    def reach_right(self, src):
        return jnp.where(src < self.nz // 2, self.nz, self.nz - 1 - src)

    def reach_left(self, src):
        return jnp.where(src < self.nz // 2, src, self.nz)


def remote(src, dst, ssem, rsem, row, col):
    return pltpu.make_async_remote_copy(
        src_ref=src, dst_ref=dst, send_sem=ssem, recv_sem=rsem,
        device_id=(row, col), device_id_type=MESH,
    )


def greet_all(place):
    barrier = pltpu.get_barrier_semaphore()
    y, z, zh, g, r, c = place.y, place.z, place.zh, place.g, place.r, place.c
    ny, nz, nx = place.ny, place.nz, place.nx

    def greet(row, col):
        pl.semaphore_signal(barrier, inc=1, device_id=(row, col), device_id_type=MESH)

    greet(r, place.partner)
    for d in range(1, nz):
        greet(y * nz + lax.rem(z + d, nz), c)
    for d in range(1, ny):
        greet(place.y_peer(d) * nz + z, c)
    for d in range(1, nx):
        greet(r, zh * nx + place.x_peer(d))

    @pl.when(z == 0)
    def _():
        greet(*place.at_ring(g - 1))

    @pl.when(z == nz - 1)
    def _():
        greet(*place.at_ring(g + 1))


def await_all(place):
    barrier = pltpu.get_barrier_semaphore()
    met = (place.ny - 1) + (place.nz - 1) + 1 + (place.nx - 1)
    at_end = (place.z == 0) | (place.z == place.nz - 1)

    @pl.when(at_end)
    def _():
        pl.semaphore_wait(barrier, met + 1)

    @pl.when(jnp.logical_not(at_end))
    def _():
        pl.semaphore_wait(barrier, met)


def phase(place, cut, own, table, back, picks, scratch, lists, fill, after, sums):
    ny, nz, nh, nx = place.ny, place.nz, place.nh, place.nx
    nrow, ring = place.nrow, place.ring
    r, c, y, z, zh, xc, g = place.r, place.c, place.y, place.z, place.zh, place.xc, place.g
    y_peer, x_peer, at_ring = place.y_peer, place.x_peer, place.at_ring
    reach_right, reach_left = place.reach_right, place.reach_left
    pick_row, pick_col = picks
    (gsend, chain, stage_y, stage_c, land_y, land_c, in_right, in_left,
     out_left, out_right, ready, far_out,
     f_r, f_sr, f_sl, yf_s, yf_r, cf_s, cf_r, yb_s, yb_r, cb_s, cb_r,
     br_r, bl_r, b_sl, b_sr) = scratch
    own_count, rows, feat = own.shape
    per = own_count // cut

    def part(ref, slot, ch):
        return ref.at[slot, pl.ds(ch * per, per)]

    def right(src, ch):
        ref = part(chain, src, ch)
        return remote(ref, ref, f_sr.at[src, ch], f_r.at[src, ch], *at_ring(g + 1))

    def left(src, ch):
        ref = part(chain, src, ch)
        return remote(ref, ref, f_sl.at[src, ch], f_r.at[src, ch], *at_ring(g - 1))

    def back_left(o, ch, buf):
        return remote(part(buf, o, ch), part(in_right, o, ch), b_sl.at[o, ch], br_r.at[o, ch],
                      *at_ring(g - 1))

    def back_right(o, ch, buf):
        return remote(part(buf, o, ch), part(in_left, o, ch), b_sr.at[o, ch], bl_r.at[o, ch],
                      *at_ring(g + 1))

    def y_back(d, o):
        yy = y_peer(d)
        return remote(gsend.at[yy * nz + o], land_y.at[(ny - d) % ny, o],
                      yb_s.at[d, o], yb_r.at[(ny - d) % ny, o], yy * nz + z, c)

    def x_back(d):
        xx = x_peer(d)
        return remote(gsend.at[pl.ds(nrow + xx * nh, nh)], land_c.at[(nx - d) % nx],
                      cb_s.at[d], cb_r.at[(nx - d) % nx], r, zh * nx + xx)

    def y_out(d, src):
        return remote(stage_y.at[d, src], table.at[own_count + y * nz + src],
                      yf_s.at[d, src], yf_r.at[d, src], y_peer(d) * nz + z, c)

    def y_in(d, src):
        yy = lax.rem(y + ny - d, ny)
        return remote(stage_y.at[d, src], table.at[own_count + yy * nz + src],
                      yf_s.at[d, src], yf_r.at[d, src], yy * nz + z, c)

    def col_slot(s, x_from):
        half = zh if s == 0 else 1 - zh
        return own_count + nrow + half * nx + x_from

    def c_out(d, s):
        return remote(stage_c.at[d, s], table.at[col_slot(s, xc)],
                      cf_s.at[d, s], cf_r.at[d, s], r, zh * nx + x_peer(d))

    def c_in(d, s):
        xx = lax.rem(xc + nx - d, nx)
        return remote(stage_c.at[d, s], table.at[col_slot(s, xx)],
                      cf_s.at[d, s], cf_r.at[d, s], r, zh * nx + xx)

    chain[g] = own[...]
    for ch in range(cut):
        @pl.when(reach_right(z) > 0)
        def _(ch=ch):
            right(g, ch).start()

        @pl.when(reach_left(z) > 0)
        def _(ch=ch):
            left(g, ch).start()

    fill(gsend)
    for d in range(1, nx):
        x_back(d).start()

    def first_y(i, carry):
        away = nz - 1 - i
        for o, ok in ((z - away, away <= z), (z + away, (away > 0) & (z + away < nz))):
            @pl.when(ok)
            def _(o=o):
                for d in range(1, ny):
                    y_back(d, o).start()
        return carry

    lax.fori_loop(0, nz, first_y, 0)

    def hot_row(which, k):
        return jnp.where(which[0:1, :] == k, 1.0, 0.0)

    def choose(which, slot):
        total = None
        for k in range(own_count):
            term = chain[slot, k] * hot_row(which, k).astype(BF16)
            total = term if total is None else total + term
        return total

    def forward(src):
        slot = zh * nz + src
        for d in range(ny):
            chosen = choose(pick_row[d, src], slot)
            if d == 0:
                table[own_count + y * nz + src] = chosen
            else:
                stage_y[d, src] = chosen
                y_out(d, src).start()

    def forward_col(s, slot):
        for d in range(nx):
            chosen = choose(pick_col[d, s], slot)
            if d == 0:
                table[col_slot(s, xc)] = chosen
            else:
                stage_c[d, s] = chosen
                c_out(d, s).start()

    def placed(o, k):
        total = None
        for d in range(ny):
            term = land_y[d, o].astype(F32) * hot_row(pick_row[d, o], k)
            total = term if total is None else total + term
        return total

    def placed_col(half, s, k):
        total = None
        for d in range(nx):
            term = land_c[d, half].astype(F32) * hot_row(pick_col[d, s], k)
            total = term if total is None else total + term
        return total

    def y_arrived(o):
        for d in range(1, ny):
            y_back(d, o).wait_recv()

    def coming(s, way):
        src = lax.rem(g + ring - s if way == 0 else g + s, ring)
        low = lax.rem(src, nz)
        reach = reach_right(low) if way == 0 else reach_left(low)
        return src, low, (s >= 1) & (s <= nz) & (s <= reach), s < reach, lax.div(src, nz) == zh

    def fwd_step(s, ch):
        for way, copy in ((0, right), (1, left)):
            src, low, comes, goes_on, mine = coming(s, way)

            @pl.when(comes)
            def _():
                copy(src, ch).wait_recv()

            @pl.when(comes & goes_on)
            def _():
                copy(src, ch).start()

    def deliver(s):
        for way in range(2):
            src, low, comes, goes_on, mine = coming(s, way)

            @pl.when(comes & mine)
            def _():
                forward(low)

        @pl.when(s == nz)
        def _():
            forward_col(1, lax.rem(g + nz, ring))

    def prepare(t):
        for way in range(2):
            o, low, comes, has_in, mine = coming(nz - t, way)

            @pl.when(comes & mine & (t >= 0))
            def _():
                y_arrived(low)
                for k in range(own_count):
                    ready[way, k] = placed(low, k)

        @pl.when(t == 0)
        def _():
            for d in range(1, nx):
                x_back(d).wait_recv()
            for k in range(own_count):
                far_out[0, k] = placed_col(1 - zh, 1, k).astype(BF16)

    def far_copy(way, o, ch):
        if way == 0:
            return remote(part(far_out, 0, ch), part(in_right, o, ch), b_sl.at[o, ch], br_r.at[o, ch],
                          *at_ring(g - 1))
        return remote(part(far_out, 0, ch), part(in_left, o, ch), b_sr.at[o, ch], bl_r.at[o, ch],
                      *at_ring(g + 1))

    def bwd_step(t, ch):
        for way, copy, got, out in ((0, back_left, in_right, out_left), (1, back_right, in_left, out_right)):
            o, low, comes, has_in, mine = coming(nz - t, way)
            sends = comes & (t >= 0)

            @pl.when(sends & has_in)
            def _():
                copy(o, ch, out).wait_recv()

            @pl.when(sends & has_in & mine)
            def _():
                for k in range(ch * per, ch * per + per):
                    out[o, k] = (ready[way, k] + got[o, k].astype(F32)).astype(BF16)
                copy(o, ch, out).start()

            @pl.when(sends & has_in & jnp.logical_not(mine))
            def _():
                copy(o, ch, got).start()

            @pl.when(sends & jnp.logical_not(has_in) & mine)
            def _():
                for k in range(ch * per, ch * per + per):
                    out[o, k] = ready[way, k].astype(BF16)
                copy(o, ch, out).start()

            @pl.when(sends & jnp.logical_not(has_in) & jnp.logical_not(mine))
            def _():
                far_copy(way, o, ch).start()

    def step(s, carry):
        for ch in range(cut):
            @pl.when(s > 1)
            def _(ch=ch):
                fwd_step(s, ch)

            bwd_step(s - 1, ch)
        prepare(s)
        deliver(s)
        if sums is not None:
            for k in range(1, len(sums)):
                @pl.when(s == k)
                def _(k=k):
                    sums[k]()
        return carry

    for ch in range(cut):
        fwd_step(1, ch)
    after()
    if sums is not None:
        sums[0]()
    table[pl.ds(0, own_count)] = own[...]
    land_y[0] = gsend[pl.ds(y * nz, nz)]
    land_c[0] = gsend[pl.ds(nrow + xc * nh, nh)]
    if lists is not None:
        lists()
    prepare(0)
    forward(z)
    forward_col(0, g)
    lax.fori_loop(1, max(nz + 1, 9 if sums is None else 10), step, 0)

    y_arrived(z)
    for k in range(own_count):
        back[k] = placed(z, k) + placed_col(zh, 0, k)
    for way, copy, got, some in (
        (0, back_left, in_right, reach_right(z) > 0), (1, back_right, in_left, reach_left(z) > 0)
    ):
        @pl.when(some)
        def _():
            for ch in range(cut):
                copy(g, ch, got).wait_recv()
            for k in range(own_count):
                back[k] += got[g, k].astype(F32)

    def arrive(src, carry):
        for d in range(1, ny):
            y_in(d, src).wait_recv()
            y_out(d, src).wait_send()
            y_back(d, src).wait_send()
        return carry

    lax.fori_loop(0, nz, arrive, 0)

    def sent(s, carry):
        for way, copy, back_copy, buf in ((0, right, back_left, out_left), (1, left, back_right, out_right)):
            src, low, comes, goes_on, mine = coming(s, way)

            @pl.when((comes | (s == 0)) & goes_on)
            def _():
                for ch in range(cut):
                    copy(src, ch).wait_send()

            @pl.when(comes)
            def _():
                for ch in range(cut):
                    back_copy(src, ch, buf).wait_send()
        return carry

    lax.fori_loop(0, nz + 1, sent, 0)
    for d in range(1, nx):
        for s in range(2):
            c_in(d, s).wait_recv()
            c_out(d, s).wait_send()
        x_back(d).wait_send()


def list_exchange(place, idx, tiles, picks, i_s, i_r):
    ny, nz, nx, nrow = place.ny, place.nz, place.nx, place.nrow
    y, z, zh, r, c = place.y, place.z, place.zh, place.r, place.c
    pick_row, pick_col = picks

    def idx_copy(d):
        zz = lax.rem(z + d, nz)
        return remote(idx, tiles.at[z], i_s.at[d], i_r.at[z], y * nz + zz, c)

    def idx_wait(d):
        zz = lax.rem(z + d, nz)
        return remote(idx, tiles.at[zz], i_s.at[d], i_r.at[zz], y * nz + zz, c)

    idx_far = remote(idx, tiles.at[nz], i_s.at[0], i_r.at[nz], r, place.partner)

    def send():
        idx_far.start()
        for d in range(1, nz):
            idx_copy(d).start()
        tiles[z] = idx[...]

    def pick():
        for d in range(1, nz):
            idx_wait(d).wait_recv()
        idx_far.wait_recv()
        lists = tiles[...].astype(F32)
        along = lists[:nz].reshape(nz * 8, 128).astype(BF16)
        pair = jnp.concatenate([tiles[z].astype(F32), lists[nz]], axis=0).astype(BF16)
        lane = lax.broadcasted_iota(jnp.int32, (128, 128), 0)
        for d in range(ny):
            hot = jnp.where(lane == place.y_peer(d) * nz + z, 1.0, 0.0).astype(BF16)
            pick_row[d] = dot(along, hot).reshape(nz, 8, 128)
        for d in range(nx):
            hot = jnp.where(lane == nrow + zh * nx + place.x_peer(d), 1.0, 0.0).astype(BF16)
            pick_col[d] = dot(pair, hot).reshape(2, 8, 128)
        for d in range(1, nz):
            idx_copy(d).wait_send()
        idx_far.wait_send()

    return send, pick


def sum_stages(place, gr, gout, refs):
    ny, nz, sx = place.ny, place.nz, place.nx
    nx = sx // 2
    r, c, y, z, zh, xc = place.r, place.c, place.y, place.z, place.zh, place.xc
    core, x = lax.rem(xc, 2), lax.div(xc, 2)
    (a1, v1, a2, v2, a3, a4, a5, v5, w1, w2, s1, r1, s2, r2, s3, r3, s4, r4, s5, r5,
     s6, r6, s7, r7, s8, r8) = refs
    half = gr.shape[0] // 2
    part = half // nx
    piece = part // ny
    other = zh * sx + x * 2 + (1 - core)

    def xcol(d):
        xx = lax.rem(x + d, nx)
        return xx, zh * sx + xx * 2 + core

    def yrow(d):
        yy = lax.rem(y + d, ny)
        return yy, yy * nz + z

    def rows_of(i, n):
        return pl.ds(i * n, n)

    c1 = remote(gr.at[rows_of(1 - core, half)], a1, s1.at[0], r1.at[0], r, other)

    def c2(d):
        xx, col = xcol(d)
        return remote(v1.at[rows_of(xx, part)], a2.at[(nx - d) % nx], s2.at[d], r2.at[(nx - d) % nx], r, col)

    def c3(d):
        yy, row = yrow(d)
        return remote(v2.at[rows_of(yy, piece)], a3.at[(ny - d) % ny], s3.at[d], r3.at[(ny - d) % ny], row, c)

    def c4(d, slot):
        zz = lax.rem(z + d, nz)
        to = z if slot is None else zz
        return remote(a4.at[z], a4.at[to], s4.at[d], r4.at[to], y * nz + zz, c)

    c5 = remote(v5.at[0], a5, s5.at[0], r5.at[0], r, place.partner)

    def c6(d, slot):
        yy, row = yrow(d)
        to = y if slot is None else yy
        here = w1.at[rows_of(y, piece)]
        return remote(here, w1.at[rows_of(to, piece)], s6.at[d], r6.at[to], row, c)

    def c7(d, slot):
        xx, col = xcol(d)
        to = x if slot is None else xx
        here = w2.at[rows_of(x, part)]
        return remote(here, w2.at[rows_of(to, part)], s7.at[d], r7.at[to], r, col)

    c8 = remote(w2, gout.at[rows_of(core, half)], s8.at[0], r8.at[0], r, other)
    c8_in = remote(w2, gout.at[rows_of(1 - core, half)], s8.at[0], r8.at[0], r, other)

    def t0():
        c1.start()

    def t1():
        c1.wait_recv()
        v1[...] = gr[rows_of(core, half)] + a1[...]
        for d in range(1, nx):
            c2(d).start()

    def t2():
        total = v1[rows_of(x, part)]
        for d in range(1, nx):
            c2(d).wait_recv()
        for d in range(1, nx):
            total = total + a2[d]
        v2[...] = total
        for d in range(1, ny):
            c3(d).start()

    def t3():
        total = v2[rows_of(y, piece)]
        for d in range(1, ny):
            c3(d).wait_recv()
        for d in range(1, ny):
            total = total + a3[d]
        a4[z] = total
        for d in range(1, nz):
            c4(d, None).start()

    def t4():
        for d in range(1, nz):
            c4(d, 1).wait_recv()
        total = a4[0]
        for i in range(1, nz):
            total = total + a4[i]
        v5[0] = total
        c5.start()

    def t5():
        c5.wait_recv()
        w1[rows_of(y, piece)] = v5[0] + a5[...]
        for d in range(1, ny):
            c6(d, None).start()

    def t6():
        for d in range(1, ny):
            c6(d, 1).wait_recv()
        w2[rows_of(x, part)] = w1[...]
        for d in range(1, nx):
            c7(d, None).start()

    def t7():
        for d in range(1, nx):
            c7(d, 1).wait_recv()
        gout[rows_of(core, half)] = w2[...]
        c8.start()

    def t8():
        c8_in.wait_recv()
        c1.wait_send()
        for d in range(1, nx):
            c2(d).wait_send()
            c7(d, None).wait_send()
        for d in range(1, ny):
            c3(d).wait_send()
            c6(d, None).wait_send()
        for d in range(1, nz):
            c4(d, None).wait_send()
        c5.wait_send()
        c8.wait_send()

    return [t0, t1, t2, t3, t4, t5, t6, t7, t8]


class Links:
    def __init__(self, meta, edges, own_count):
        self.meta, self.edges, self.own_count = meta, edges, own_count

    def prev_dst(self, e):
        return self.meta[e]

    def prev_slot(self, e):
        return self.meta[self.edges + e]

    def last_dst(self, b):
        return self.meta[2 * self.edges + b]

    def last_slot(self, i):
        return self.meta[2 * self.edges + self.own_count + i]


def edge_links(split, own_count, size, dst, src):
    edges = dst.size
    slot = grad_slot(split, own_count, src)
    e = jnp.arange(edges, dtype=jnp.int32)
    early = e[None, :] < e[:, None]

    def latest(match):
        found = jnp.max(jnp.where(match, e[None, :], -1), axis=1)
        return jnp.where(found < 0, edges, found)

    return jnp.concatenate([
        latest((dst[None, :] == dst[:, None]) & early),
        latest((slot[None, :] == slot[:, None]) & early),
        latest(dst[None, :] == jnp.arange(own_count, dtype=jnp.int32)[:, None]),
        latest(slot[None, :] == jnp.arange(size, dtype=jnp.int32)[:, None]),
    ])


def grad_slot(split, own_count, t):
    nh, nx = split["zh"], split["xc"]
    first = own_count + split["y"] * split["z"]
    q = t - first
    return jnp.where(t < first, t, first + nh * lax.rem(q, nx) + lax.div(q, nx))


def running(edges, run, term, prev):
    def one(e, carry):
        run[e] = term(e) + run[prev(e)]
        return carry

    lax.fori_loop(0, edges, one, 0, unroll=4)


def spread(links, adj, dst, q, run):
    running(links.edges, run, lambda e: dot_at(adj[e], q[dst[e]]), links.prev_slot)


def gather(links, adj, src, table, run):
    running(links.edges, run, lambda e: dot(adj[e], table[src[e]]), links.prev_dst)


def send_out(links, own_count, run, gsend):
    @pl.loop(0, gsend.shape[0])
    def _(i):
        gsend[i] = run[links.last_slot(own_count + i)].astype(BF16)


def main_kernel(split, scale, n_phase, n_in, dst, src, meta, idx, *refs):
    place = Place(split)
    greet_all(place)
    far_in, refs = refs[:n_in], refs[n_in:]
    (hidden, table2, deg, base, back, gout), refs = refs[:6], refs[6:]
    near_in, refs = refs[:n_in], list(refs[n_in:])
    (in_s, table1, u_own, u_back, q, keep, grads, run_d, run_s, tiles, pick_row, pick_col,
     i_s, i_r) = refs[:14]
    del refs[:14]
    first, second, rest = refs[:n_phase], refs[n_phase:2 * n_phase], refs[2 * n_phase:]
    feat, adj, cot, ws1, wn1, ws2, wn2 = near_in
    loads = [pltpu.make_async_copy(a, b, in_s.at[i]) for i, (a, b) in enumerate(zip(far_in, near_in))]
    for load in loads:
        load.start()
    picks = (pick_row, pick_col)
    own_count, rows, width = feat.shape
    edges = adj.shape[0]
    links = Links(meta, edges, own_count)
    run_d[edges] = jnp.zeros((rows, width), F32)
    run_s[edges] = jnp.zeros((rows, width), F32)
    loads[0].wait()
    await_all(place)
    send, pick = list_exchange(place, idx, tiles, picks, i_s, i_r)
    send()

    def fill_two(gsend):
        for load in loads[1:]:
            load.wait()
        ones = jnp.ones((rows, rows), BF16)
        running(edges, run_d, lambda e: dot(adj[e], ones), links.prev_dst)
        for b in range(own_count):
            deg[b] = 1.0 + run_d[links.last_dst(b)]
            q[b] = (cot[b].astype(F32) / deg[b]).astype(BF16)
        spread(links, adj, dst, q, run_s)
        send_out(links, own_count, run_s, gsend)

    def after_two():
        for b in range(own_count):
            u_own[b] = run_s[links.last_slot(b)] + q[b].astype(F32)

    phase(place, CUT, feat, table1, u_back, picks, first, pick, fill_two, after_two, None)

    gather(links, adj, src, table1, run_d)
    for b in range(own_count):
        mean = ((feat[b].astype(F32) + run_d[links.last_dst(b)]) / deg[b]).astype(BF16)
        pre = dot(feat[b], ws1[...]) + dot(mean, wn1[...])
        s = 1.0 / (1.0 + jnp.exp(-pre))
        hidden[b] = (pre * s).astype(BF16)
        u = u_own[b] + u_back[b]
        hi = u.astype(BF16)
        lo = (u - hi.astype(F32)).astype(BF16)
        dh = dot_bt(cot[b], ws2[...]) + (dot_bt(hi, wn2[...]) + dot_bt(lo, wn2[...]))
        dpre = (dh * (s * (1.0 + pre * (1.0 - s)))).astype(BF16)
        q[b] = (dot_bt(dpre, wn1[...]) / deg[b]).astype(BF16)
        keep[0, b] = dpre
        keep[1, b] = mean
        keep[2, b] = hi
        keep[3, b] = lo

    def fill_one(gsend):
        spread(links, adj, dst, q, run_s)
        send_out(links, own_count, run_s, gsend)

    def weights(b, total):
        dpre = keep[0, b]
        return (
            total[0] + dot_at(feat[b], dpre),
            total[1] + dot_at(keep[1, b], dpre),
            total[2] + dot_at(hidden[b], cot[b]),
            total[3] + (dot_at(hidden[b], keep[2, b]) + dot_at(hidden[b], keep[3, b])),
        )

    def after_one():
        zero = jnp.zeros((width, width), F32)
        for i, part in enumerate(lax.fori_loop(0, own_count, weights, (zero,) * 4)):
            grads[pl.ds(i * width // UNIT, width // UNIT)] = (part * scale).reshape(width // UNIT, UNIT, width)
        for b in range(own_count):
            base[b] = dot_bt(keep[0, b], ws1[...]) + q[b].astype(F32) + run_s[links.last_slot(b)]

    phase(place, CUT, hidden, table2, back, picks, second, None, fill_one, after_one,
          sum_stages(place, grads, gout, rest))


def phase_scratch(split, own_count, rows, feat):
    ny, nz, nh, nx = split["y"], split["z"], split["zh"], split["xc"]
    ring = nh * nz
    blocks = (own_count, rows, feat)
    one = (rows, feat)
    dma = pltpu.SemaphoreType.DMA
    pieces = dma((ring, CUT))
    return [
        pltpu.VMEM((ny * nz + nh * nx,) + one, BF16),
        pltpu.VMEM((ring,) + blocks, BF16),
        pltpu.VMEM((ny, nz) + one, BF16),
        pltpu.VMEM((nx, 2) + one, BF16),
        pltpu.VMEM((ny, nz) + one, BF16),
        pltpu.VMEM((nx, nh) + one, BF16),
        pltpu.VMEM((ring,) + blocks, BF16),
        pltpu.VMEM((ring,) + blocks, BF16),
        pltpu.VMEM((ring,) + blocks, BF16),
        pltpu.VMEM((ring,) + blocks, BF16),
        pltpu.VMEM((2,) + blocks, F32),
        pltpu.VMEM((1,) + blocks, BF16),
        pieces, pieces, pieces,
        dma((ny, nz)), dma((ny, nz)), dma((nx, 2)), dma((nx, 2)),
        dma((ny, nz)), dma((ny, nz)), dma((nx,)), dma((nx,)),
        pieces, pieces, pieces, pieces,
    ]


def sum_scratch(split, units):
    ny, nz, cx = split["y"], split["z"], split["xc"] // 2
    half = units // 2
    part = half // cx
    piece = part // ny
    dma = pltpu.SemaphoreType.DMA
    return [
        pltpu.VMEM((half, UNIT, 128), F32),
        pltpu.VMEM((half, UNIT, 128), F32),
        pltpu.VMEM((cx, part, UNIT, 128), F32),
        pltpu.VMEM((part, UNIT, 128), F32),
        pltpu.VMEM((ny, piece, UNIT, 128), F32),
        pltpu.VMEM((nz, piece, UNIT, 128), F32),
        pltpu.VMEM((piece, UNIT, 128), F32),
        pltpu.VMEM((1, piece, UNIT, 128), F32),
        pltpu.VMEM((part, UNIT, 128), F32),
        pltpu.VMEM((half, UNIT, 128), F32),
        dma((1,)), dma((1,)), dma((cx,)), dma((cx,)), dma((ny,)), dma((ny,)),
        dma((nz,)), dma((nz,)), dma((1,)), dma((1,)), dma((ny,)), dma((ny,)),
        dma((cx,)), dma((cx,)), dma((1,)), dma((1,)),
    ]


def last_kernel(dst, src, meta, adj, hidden, table, deg, base, back, grads, ws2, wn2,
                out, grad_in, g1, g2, g3, g4, run):
    own_count, rows, width = hidden.shape
    edges = adj.shape[0]
    links = Links(meta, edges, own_count)
    run[edges] = jnp.zeros((rows, width), F32)
    gather(links, adj, src, table, run)
    for b in range(own_count):
        mean = ((hidden[b].astype(F32) + run[links.last_dst(b)]) / deg[b]).astype(BF16)
        out[b] = (dot(hidden[b], ws2[...]) + dot(mean, wn2[...])).astype(BF16)
        grad_in[b] = base[b] + back[b]
    for i, g in enumerate((g1, g2, g3, g4)):
        g[...] = grads[pl.ds(i * width // UNIT, width // UNIT)].reshape(width, width)


def call(body, edges, args, far, out_shape, scratch, params):
    smem = pl.BlockSpec(memory_space=pltpu.SMEM)
    vmem = pl.BlockSpec(memory_space=pltpu.VMEM)
    where = pl.BlockSpec(memory_space=pl.ANY)
    return pl.pallas_call(
        body,
        out_shape=out_shape,
        in_specs=[smem] * len(edges) + [vmem] * len(args) + [where] * len(far),
        out_specs=[vmem] * len(out_shape),
        scratch_shapes=scratch,
        compiler_params=pltpu.CompilerParams(vmem_limit_bytes=LIMIT, **params),
    )(*edges, *args, *far)


def local(
    split,
    nodes,
    features,
    adjacency,
    edge_dst,
    edge_src,
    send_row,
    send_col,
    w_self1,
    w_neigh1,
    w_self2,
    w_neigh2,
    cotangent,
):
    own = features[0, 0]
    adj = adjacency[0, 0]
    dst, src = edge_dst[0, 0], edge_src[0, 0]
    cot = cotangent[0, 0]
    own_count, rows, width = own.shape
    lists = jnp.concatenate([send_row.reshape(-1), send_col.reshape(-1)])
    remote_count = lists.size
    idx = jnp.broadcast_to(jnp.pad(lists, (0, 128 - remote_count))[None, :], (8, 128))
    size = own_count + remote_count
    edges = (dst, src, edge_links(split, own_count, size, dst, src))
    blocks = (own_count, rows, width)
    full = jax.ShapeDtypeStruct(blocks, F32)
    half = jax.ShapeDtypeStruct(blocks, BF16)
    weight = jax.ShapeDtypeStruct((width, width), F32)
    run = pltpu.VMEM((adj.shape[0] + 1, rows, width), F32)
    ny, nz, nx = split["y"], split["z"], split["xc"]
    dma = pltpu.SemaphoreType.DMA
    per_phase = phase_scratch(split, own_count, rows, width)
    far = (own, adj, cot, w_self1, w_neigh1, w_self2, w_neigh2)
    scratch = [pltpu.VMEM(a.shape, BF16) for a in far] + [
        dma((len(far),)),
        pltpu.VMEM((size, rows, width), BF16),
        pltpu.VMEM(blocks, F32),
        pltpu.VMEM(blocks, F32),
        pltpu.VMEM(blocks, BF16),
        pltpu.VMEM((4,) + blocks, BF16),
        pltpu.VMEM((4 * width // UNIT, UNIT, width), F32),
        run,
        run,
        pltpu.VMEM((nz + 1, 8, 128), jnp.int32),
        pltpu.VMEM((ny, nz, 8, 128), F32),
        pltpu.VMEM((nx, 2, 8, 128), F32),
        dma((nz,)),
        dma((nz + 1,)),
    ] + per_phase + per_phase + sum_scratch(split, 4 * width // UNIT)
    hidden, table, deg, base, back, grads = call(
        functools.partial(main_kernel, split, 1.0 / math.sqrt(nodes), len(per_phase), len(far)),
        edges,
        (idx,),
        far,
        [half, jax.ShapeDtypeStruct((size, rows, width), BF16), full, full, full,
         jax.ShapeDtypeStruct((4 * width // UNIT, UNIT, width), F32)],
        scratch,
        dict(collective_id=0, has_side_effects=True),
    )
    out, grad_in, g1, g2, g3, g4 = call(
        last_kernel,
        edges,
        (adj, hidden, table, deg, base, back, grads, w_self2, w_neigh2),
        (),
        [half, full, weight, weight, weight, weight],
        [run],
        {},
    )
    return out.reshape(features.shape), grad_in.reshape(features.shape), g1, g2, g3, g4


def solution(mesh):
    blocked = P("row", "col", None, None, None)
    placed = (
        blocked,
        blocked,
        P("row", "col", None),
        P("row", "col", None),
        P("row", "col", None, None),
        P("row", "col", None, None),
        P(),
        P(),
        P(),
        P(),
        blocked,
    )

    def whole(*args):
        shape = args[0].shape
        nodes = shape[0] * shape[1] * shape[2] * shape[3]
        return jax.shard_map(
            functools.partial(local, SPLIT, nodes),
            mesh=mesh,
            in_specs=placed,
            out_specs=(blocked, blocked, P(), P(), P(), P()),
            check_vma=False,
        )(*args)

    return whole
```

```python
import functools
import math

import jax
import jax.numpy as jnp
from jax import lax
from jax.experimental import pallas as pl
from jax.experimental.pallas import tpu as pltpu
from jax.sharding import PartitionSpec as P

MESH = pl.DeviceIdType.MESH
BF16 = jnp.bfloat16
F32 = jnp.float32
LIMIT = 60 * 1024 * 1024
SPLIT = {"y": 4, "z": 8, "zh": 2, "xc": 8}
CUT = 2
UNIT = 16


def dot(a, b):
    return jnp.dot(a, b, preferred_element_type=F32)


def dot_bt(a, b):
    return lax.dot_general(a, b, (((1,), (1,)), ((), ())), preferred_element_type=F32)


def dot_at(a, b):
    return lax.dot_general(a, b, (((0,), (0,)), ((), ())), preferred_element_type=F32)


class Place:
    def __init__(self, split):
        self.split = split
        self.ny, self.nz, self.nh, self.nx = split["y"], split["z"], split["zh"], split["xc"]
        self.nrow, self.ring = self.ny * self.nz, self.nh * self.nz
        self.r = lax.axis_index("row")
        self.c = lax.axis_index("col")
        self.y, self.z = lax.div(self.r, self.nz), lax.rem(self.r, self.nz)
        self.zh, self.xc = lax.div(self.c, self.nx), lax.rem(self.c, self.nx)
        self.g = self.zh * self.nz + self.z
        self.partner = (1 - self.zh) * self.nx + self.xc

    def y_peer(self, d):
        return lax.rem(self.y + d, self.ny)

    def x_peer(self, d):
        return lax.rem(self.xc + d, self.nx)

    def at_ring(self, pos):
        pos = lax.rem(pos + self.ring, self.ring)
        return self.y * self.nz + lax.rem(pos, self.nz), lax.div(pos, self.nz) * self.nx + self.xc

    def reach_right(self, src):
        return jnp.where(src < self.nz // 2, self.nz, self.nz - 1 - src)

    def reach_left(self, src):
        return jnp.where(src < self.nz // 2, src, self.nz)


def remote(src, dst, ssem, rsem, row, col):
    return pltpu.make_async_remote_copy(
        src_ref=src, dst_ref=dst, send_sem=ssem, recv_sem=rsem,
        device_id=(row, col), device_id_type=MESH,
    )


def greet_all(place):
    barrier = pltpu.get_barrier_semaphore()
    y, z, zh, g, r, c = place.y, place.z, place.zh, place.g, place.r, place.c
    ny, nz, nx = place.ny, place.nz, place.nx

    def greet(row, col):
        pl.semaphore_signal(barrier, inc=1, device_id=(row, col), device_id_type=MESH)

    greet(r, place.partner)
    for d in range(1, nz):
        greet(y * nz + lax.rem(z + d, nz), c)
    for d in range(1, ny):
        greet(place.y_peer(d) * nz + z, c)
    for d in range(1, nx):
        greet(r, zh * nx + place.x_peer(d))

    @pl.when(z == 0)
    def _():
        greet(*place.at_ring(g - 1))

    @pl.when(z == nz - 1)
    def _():
        greet(*place.at_ring(g + 1))


def await_all(place):
    barrier = pltpu.get_barrier_semaphore()
    met = (place.ny - 1) + (place.nz - 1) + 1 + (place.nx - 1)
    at_end = (place.z == 0) | (place.z == place.nz - 1)

    @pl.when(at_end)
    def _():
        pl.semaphore_wait(barrier, met + 1)

    @pl.when(jnp.logical_not(at_end))
    def _():
        pl.semaphore_wait(barrier, met)


def phase(place, cut, own, table, back, picks, scratch, lists, fill, after, sums):
    ny, nz, nh, nx = place.ny, place.nz, place.nh, place.nx
    nrow, ring = place.nrow, place.ring
    r, c, y, z, zh, xc, g = place.r, place.c, place.y, place.z, place.zh, place.xc, place.g
    y_peer, x_peer, at_ring = place.y_peer, place.x_peer, place.at_ring
    reach_right, reach_left = place.reach_right, place.reach_left
    pick_row, pick_col = picks
    (gsend, chain, stage_y, stage_c, land_y, land_c, in_right, in_left,
     out_left, out_right, ready, far_out,
     f_r, f_sr, f_sl, yf_s, yf_r, cf_s, cf_r, yb_s, yb_r, cb_s, cb_r,
     br_r, bl_r, b_sl, b_sr) = scratch
    own_count, rows, feat = own.shape
    per = own_count // cut

    def part(ref, slot, ch):
        return ref.at[slot, pl.ds(ch * per, per)]

    def right(src, ch):
        ref = part(chain, src, ch)
        return remote(ref, ref, f_sr.at[src, ch], f_r.at[src, ch], *at_ring(g + 1))

    def left(src, ch):
        ref = part(chain, src, ch)
        return remote(ref, ref, f_sl.at[src, ch], f_r.at[src, ch], *at_ring(g - 1))

    def back_left(o, ch, buf):
        return remote(part(buf, o, ch), part(in_right, o, ch), b_sl.at[o, ch], br_r.at[o, ch],
                      *at_ring(g - 1))

    def back_right(o, ch, buf):
        return remote(part(buf, o, ch), part(in_left, o, ch), b_sr.at[o, ch], bl_r.at[o, ch],
                      *at_ring(g + 1))

    def y_back(d, o):
        yy = y_peer(d)
        return remote(gsend.at[yy * nz + o], land_y.at[(ny - d) % ny, o],
                      yb_s.at[d, o], yb_r.at[(ny - d) % ny, o], yy * nz + z, c)

    def x_back(d):
        xx = x_peer(d)
        return remote(gsend.at[pl.ds(nrow + xx * nh, nh)], land_c.at[(nx - d) % nx],
                      cb_s.at[d], cb_r.at[(nx - d) % nx], r, zh * nx + xx)

    def y_out(d, src):
        return remote(stage_y.at[d, src], table.at[own_count + y * nz + src],
                      yf_s.at[d, src], yf_r.at[d, src], y_peer(d) * nz + z, c)

    def y_in(d, src):
        yy = lax.rem(y + ny - d, ny)
        return remote(stage_y.at[d, src], table.at[own_count + yy * nz + src],
                      yf_s.at[d, src], yf_r.at[d, src], yy * nz + z, c)

    def col_slot(s, x_from):
        half = zh if s == 0 else 1 - zh
        return own_count + nrow + half * nx + x_from

    def c_out(d, s):
        return remote(stage_c.at[d, s], table.at[col_slot(s, xc)],
                      cf_s.at[d, s], cf_r.at[d, s], r, zh * nx + x_peer(d))

    def c_in(d, s):
        xx = lax.rem(xc + nx - d, nx)
        return remote(stage_c.at[d, s], table.at[col_slot(s, xx)],
                      cf_s.at[d, s], cf_r.at[d, s], r, zh * nx + xx)

    chain[g] = own[...]
    for ch in range(cut):
        @pl.when(reach_right(z) > 0)
        def _(ch=ch):
            right(g, ch).start()

        @pl.when(reach_left(z) > 0)
        def _(ch=ch):
            left(g, ch).start()

    fill(gsend)
    for d in range(1, nx):
        x_back(d).start()

    def first_y(i, carry):
        away = nz - 1 - i
        for o, ok in ((z - away, away <= z), (z + away, (away > 0) & (z + away < nz))):
            @pl.when(ok)
            def _(o=o):
                for d in range(1, ny):
                    y_back(d, o).start()
        return carry

    lax.fori_loop(0, nz, first_y, 0)

    def hot_row(which, k):
        return jnp.where(which[0:1, :] == k, 1.0, 0.0)

    def choose(which, slot):
        total = None
        for k in range(own_count):
            term = chain[slot, k] * hot_row(which, k).astype(BF16)
            total = term if total is None else total + term
        return total

    def forward(src):
        slot = zh * nz + src
        for d in range(ny):
            chosen = choose(pick_row[d, src], slot)
            if d == 0:
                table[own_count + y * nz + src] = chosen
            else:
                stage_y[d, src] = chosen
                y_out(d, src).start()

    def forward_col(s, slot):
        for d in range(nx):
            chosen = choose(pick_col[d, s], slot)
            if d == 0:
                table[col_slot(s, xc)] = chosen
            else:
                stage_c[d, s] = chosen
                c_out(d, s).start()

    def placed(o, k):
        total = None
        for d in range(ny):
            term = land_y[d, o].astype(F32) * hot_row(pick_row[d, o], k)
            total = term if total is None else total + term
        return total

    def placed_col(half, s, k):
        total = None
        for d in range(nx):
            term = land_c[d, half].astype(F32) * hot_row(pick_col[d, s], k)
            total = term if total is None else total + term
        return total

    def y_arrived(o):
        for d in range(1, ny):
            y_back(d, o).wait_recv()

    def coming(s, way):
        src = lax.rem(g + ring - s if way == 0 else g + s, ring)
        low = lax.rem(src, nz)
        reach = reach_right(low) if way == 0 else reach_left(low)
        return src, low, (s >= 1) & (s <= nz) & (s <= reach), s < reach, lax.div(src, nz) == zh

    def fwd_step(s, ch):
        for way, copy in ((0, right), (1, left)):
            src, low, comes, goes_on, mine = coming(s, way)

            @pl.when(comes)
            def _():
                copy(src, ch).wait_recv()

            @pl.when(comes & goes_on)
            def _():
                copy(src, ch).start()

    def deliver(s):
        for way in range(2):
            src, low, comes, goes_on, mine = coming(s, way)

            @pl.when(comes & mine)
            def _():
                forward(low)

        @pl.when(s == nz)
        def _():
            forward_col(1, lax.rem(g + nz, ring))

    def prepare(t):
        for way in range(2):
            o, low, comes, has_in, mine = coming(nz - t, way)

            @pl.when(comes & mine & (t >= 0))
            def _():
                y_arrived(low)
                for k in range(own_count):
                    ready[way, k] = placed(low, k)

        @pl.when(t == 0)
        def _():
            for d in range(1, nx):
                x_back(d).wait_recv()
            for k in range(own_count):
                far_out[0, k] = placed_col(1 - zh, 1, k).astype(BF16)

    def far_copy(way, o, ch):
        if way == 0:
            return remote(part(far_out, 0, ch), part(in_right, o, ch), b_sl.at[o, ch], br_r.at[o, ch],
                          *at_ring(g - 1))
        return remote(part(far_out, 0, ch), part(in_left, o, ch), b_sr.at[o, ch], bl_r.at[o, ch],
                      *at_ring(g + 1))

    def bwd_step(t, ch):
        for way, copy, got, out in ((0, back_left, in_right, out_left), (1, back_right, in_left, out_right)):
            o, low, comes, has_in, mine = coming(nz - t, way)
            sends = comes & (t >= 0)

            @pl.when(sends & has_in)
            def _():
                copy(o, ch, out).wait_recv()

            @pl.when(sends & has_in & mine)
            def _():
                for k in range(ch * per, ch * per + per):
                    out[o, k] = (ready[way, k] + got[o, k].astype(F32)).astype(BF16)
                copy(o, ch, out).start()

            @pl.when(sends & has_in & jnp.logical_not(mine))
            def _():
                copy(o, ch, got).start()

            @pl.when(sends & jnp.logical_not(has_in) & mine)
            def _():
                for k in range(ch * per, ch * per + per):
                    out[o, k] = ready[way, k].astype(BF16)
                copy(o, ch, out).start()

            @pl.when(sends & jnp.logical_not(has_in) & jnp.logical_not(mine))
            def _():
                far_copy(way, o, ch).start()

    def settle(s):
        for way, copy in ((0, right), (1, left)):
            src, low, comes, goes_on, mine = coming(s, way)

            @pl.when((comes | (s == 0)) & goes_on)
            def _():
                for ch in range(cut):
                    copy(src, ch).wait_send()

            @pl.when((comes & mine) | ((s == 0) & (way == 0)))
            def _():
                for d in range(1, ny):
                    y_in(d, low).wait_recv()
                    y_out(d, low).wait_send()
                    y_back(d, low).wait_send()

    def step(s, carry):
        for ch in range(cut):
            @pl.when(s > 1)
            def _(ch=ch):
                fwd_step(s, ch)

            bwd_step(s - 1, ch)
        prepare(s)
        deliver(s)

        @pl.when(s == 1)
        def _():
            forward(z)

        @pl.when(s == 3)
        def _():
            forward_col(0, g)

        @pl.when(s == 5)
        def _():
            y_arrived(z)
            for k in range(own_count):
                back[k] = placed(z, k) + placed_col(zh, 0, k)

        @pl.when(s == 6)
        def _():
            for d in range(1, nx):
                x_back(d).wait_send()

        @pl.when(s == 7)
        def _():
            for d in range(1, nx):
                c_in(d, 0).wait_recv()
                c_out(d, 0).wait_send()

        @pl.when(s >= 3)
        def _():
            settle(s - 3)

        if sums is not None:
            for k in range(1, len(sums)):
                @pl.when(s == k)
                def _(k=k):
                    sums[k]()
        return carry

    for ch in range(cut):
        fwd_step(1, ch)
    after()
    if sums is not None:
        sums[0]()
    table[pl.ds(0, own_count)] = own[...]
    land_y[0] = gsend[pl.ds(y * nz, nz)]
    land_c[0] = gsend[pl.ds(nrow + xc * nh, nh)]
    if lists is not None:
        lists()
    prepare(0)
    last = max(nz + 1, 9 if sums is None else 10)
    lax.fori_loop(1, last, step, 0)

    for way, copy, got, some in (
        (0, back_left, in_right, reach_right(z) > 0), (1, back_right, in_left, reach_left(z) > 0)
    ):
        @pl.when(some)
        def _():
            for ch in range(cut):
                copy(g, ch, got).wait_recv()
            for k in range(own_count):
                back[k] += got[g, k].astype(F32)

    lax.fori_loop(last - 3, nz + 1, lambda s, carry: (settle(s), carry)[1], 0)

    def sent(s, carry):
        for way, copy, buf in ((0, back_left, out_left), (1, back_right, out_right)):
            src, low, comes, goes_on, mine = coming(s, way)

            @pl.when(comes)
            def _():
                for ch in range(cut):
                    copy(src, ch, buf).wait_send()
        return carry

    lax.fori_loop(1, nz + 1, sent, 0)
    for d in range(1, nx):
        c_in(d, 1).wait_recv()
        c_out(d, 1).wait_send()


def list_exchange(place, idx, tiles, picks, i_s, i_r):
    ny, nz, nx, nrow = place.ny, place.nz, place.nx, place.nrow
    y, z, zh, r, c = place.y, place.z, place.zh, place.r, place.c
    pick_row, pick_col = picks

    def idx_copy(d):
        zz = lax.rem(z + d, nz)
        return remote(idx, tiles.at[z], i_s.at[d], i_r.at[z], y * nz + zz, c)

    def idx_wait(d):
        zz = lax.rem(z + d, nz)
        return remote(idx, tiles.at[zz], i_s.at[d], i_r.at[zz], y * nz + zz, c)

    idx_far = remote(idx, tiles.at[nz], i_s.at[0], i_r.at[nz], r, place.partner)

    def send():
        idx_far.start()
        for d in range(1, nz):
            idx_copy(d).start()
        tiles[z] = idx[...]

    def pick():
        for d in range(1, nz):
            idx_wait(d).wait_recv()
        idx_far.wait_recv()
        lists = tiles[...].astype(F32)
        along = lists[:nz].reshape(nz * 8, 128).astype(BF16)
        pair = jnp.concatenate([tiles[z].astype(F32), lists[nz]], axis=0).astype(BF16)
        lane = lax.broadcasted_iota(jnp.int32, (128, 128), 0)
        for d in range(ny):
            hot = jnp.where(lane == place.y_peer(d) * nz + z, 1.0, 0.0).astype(BF16)
            pick_row[d] = dot(along, hot).reshape(nz, 8, 128)
        for d in range(nx):
            hot = jnp.where(lane == nrow + zh * nx + place.x_peer(d), 1.0, 0.0).astype(BF16)
            pick_col[d] = dot(pair, hot).reshape(2, 8, 128)
        for d in range(1, nz):
            idx_copy(d).wait_send()
        idx_far.wait_send()

    return send, pick


def sum_stages(place, gr, gout, refs):
    ny, nz, sx = place.ny, place.nz, place.nx
    nx = sx // 2
    r, c, y, z, zh, xc = place.r, place.c, place.y, place.z, place.zh, place.xc
    core, x = lax.rem(xc, 2), lax.div(xc, 2)
    (a1, v1, a2, v2, a3, a4, a5, v5, w1, w2, s1, r1, s2, r2, s3, r3, s4, r4, s5, r5,
     s6, r6, s7, r7, s8, r8) = refs
    half = gr.shape[0] // 2
    part = half // nx
    piece = part // ny
    other = zh * sx + x * 2 + (1 - core)

    def xcol(d):
        xx = lax.rem(x + d, nx)
        return xx, zh * sx + xx * 2 + core

    def yrow(d):
        yy = lax.rem(y + d, ny)
        return yy, yy * nz + z

    def rows_of(i, n):
        return pl.ds(i * n, n)

    c1 = remote(gr.at[rows_of(1 - core, half)], a1, s1.at[0], r1.at[0], r, other)

    def c2(d):
        xx, col = xcol(d)
        return remote(v1.at[rows_of(xx, part)], a2.at[(nx - d) % nx], s2.at[d], r2.at[(nx - d) % nx], r, col)

    def c3(d):
        yy, row = yrow(d)
        return remote(v2.at[rows_of(yy, piece)], a3.at[(ny - d) % ny], s3.at[d], r3.at[(ny - d) % ny], row, c)

    def c4(d, slot):
        zz = lax.rem(z + d, nz)
        to = z if slot is None else zz
        return remote(a4.at[z], a4.at[to], s4.at[d], r4.at[to], y * nz + zz, c)

    c5 = remote(v5.at[0], a5, s5.at[0], r5.at[0], r, place.partner)

    def c6(d, slot):
        yy, row = yrow(d)
        to = y if slot is None else yy
        here = w1.at[rows_of(y, piece)]
        return remote(here, w1.at[rows_of(to, piece)], s6.at[d], r6.at[to], row, c)

    def c7(d, slot):
        xx, col = xcol(d)
        to = x if slot is None else xx
        here = w2.at[rows_of(x, part)]
        return remote(here, w2.at[rows_of(to, part)], s7.at[d], r7.at[to], r, col)

    c8 = remote(w2, gout.at[rows_of(core, half)], s8.at[0], r8.at[0], r, other)
    c8_in = remote(w2, gout.at[rows_of(1 - core, half)], s8.at[0], r8.at[0], r, other)

    def t0():
        c1.start()

    def t1():
        c1.wait_recv()
        v1[...] = gr[rows_of(core, half)] + a1[...]
        for d in range(1, nx):
            c2(d).start()

    def t2():
        total = v1[rows_of(x, part)]
        for d in range(1, nx):
            c2(d).wait_recv()
        for d in range(1, nx):
            total = total + a2[d]
        v2[...] = total
        for d in range(1, ny):
            c3(d).start()

    def t3():
        total = v2[rows_of(y, piece)]
        for d in range(1, ny):
            c3(d).wait_recv()
        for d in range(1, ny):
            total = total + a3[d]
        a4[z] = total
        for d in range(1, nz):
            c4(d, None).start()

    def t4():
        for d in range(1, nz):
            c4(d, 1).wait_recv()
        total = a4[0]
        for i in range(1, nz):
            total = total + a4[i]
        v5[0] = total
        c5.start()

    def t5():
        c5.wait_recv()
        w1[rows_of(y, piece)] = v5[0] + a5[...]
        for d in range(1, ny):
            c6(d, None).start()

    def t6():
        for d in range(1, ny):
            c6(d, 1).wait_recv()
        w2[rows_of(x, part)] = w1[...]
        for d in range(1, nx):
            c7(d, None).start()

    def t7():
        for d in range(1, nx):
            c7(d, 1).wait_recv()
        gout[rows_of(core, half)] = w2[...]
        c8.start()

    def t8():
        c8_in.wait_recv()
        c1.wait_send()
        for d in range(1, nx):
            c2(d).wait_send()
            c7(d, None).wait_send()
        for d in range(1, ny):
            c3(d).wait_send()
            c6(d, None).wait_send()
        for d in range(1, nz):
            c4(d, None).wait_send()
        c5.wait_send()
        c8.wait_send()

    return [t0, t1, t2, t3, t4, t5, t6, t7, t8]


class Links:
    def __init__(self, meta, edges, own_count):
        self.meta, self.edges, self.own_count = meta, edges, own_count

    def prev_dst(self, e):
        return self.meta[e]

    def prev_slot(self, e):
        return self.meta[self.edges + e]

    def last_dst(self, b):
        return self.meta[2 * self.edges + b]

    def last_slot(self, i):
        return self.meta[2 * self.edges + self.own_count + i]


def edge_links(split, own_count, size, dst, src):
    edges = dst.size
    slot = grad_slot(split, own_count, src)
    e = jnp.arange(edges, dtype=jnp.int32)
    early = e[None, :] < e[:, None]

    def latest(match):
        found = jnp.max(jnp.where(match, e[None, :], -1), axis=1)
        return jnp.where(found < 0, edges, found)

    return jnp.concatenate([
        latest((dst[None, :] == dst[:, None]) & early),
        latest((slot[None, :] == slot[:, None]) & early),
        latest(dst[None, :] == jnp.arange(own_count, dtype=jnp.int32)[:, None]),
        latest(slot[None, :] == jnp.arange(size, dtype=jnp.int32)[:, None]),
    ])


def grad_slot(split, own_count, t):
    nh, nx = split["zh"], split["xc"]
    first = own_count + split["y"] * split["z"]
    q = t - first
    return jnp.where(t < first, t, first + nh * lax.rem(q, nx) + lax.div(q, nx))


def running(edges, run, term, prev):
    def one(e, carry):
        run[e] = term(e) + run[prev(e)]
        return carry

    lax.fori_loop(0, edges, one, 0, unroll=4)


def spread(links, adj, dst, q, run):
    running(links.edges, run, lambda e: dot_at(adj[e], q[dst[e]]), links.prev_slot)


def gather(links, adj, src, table, run):
    running(links.edges, run, lambda e: dot(adj[e], table[src[e]]), links.prev_dst)


def send_out(links, own_count, run, gsend):
    @pl.loop(0, gsend.shape[0])
    def _(i):
        gsend[i] = run[links.last_slot(own_count + i)].astype(BF16)


def main_kernel(split, scale, n_phase, n_in, dst, src, meta, idx, *refs):
    place = Place(split)
    greet_all(place)
    far_in, refs = refs[:n_in], refs[n_in:]
    (hidden, table2, deg, base, back, gout), refs = refs[:6], refs[6:]
    near_in, refs = refs[:n_in], list(refs[n_in:])
    (in_s, table1, u_own, u_back, q, keep, grads, run_d, run_s, tiles, pick_row, pick_col,
     i_s, i_r) = refs[:14]
    del refs[:14]
    first, second, rest = refs[:n_phase], refs[n_phase:2 * n_phase], refs[2 * n_phase:]
    feat, adj, cot, ws1, wn1, ws2, wn2 = near_in
    loads = [pltpu.make_async_copy(a, b, in_s.at[i]) for i, (a, b) in enumerate(zip(far_in, near_in))]
    for load in loads:
        load.start()
    picks = (pick_row, pick_col)
    own_count, rows, width = feat.shape
    edges = adj.shape[0]
    links = Links(meta, edges, own_count)
    run_d[edges] = jnp.zeros((rows, width), F32)
    run_s[edges] = jnp.zeros((rows, width), F32)
    for load in loads:
        load.wait()

    ones = jnp.ones((rows, rows), BF16)
    running(edges, run_d, lambda e: dot(adj[e], ones), links.prev_dst)
    for b in range(own_count):
        deg[b] = 1.0 + run_d[links.last_dst(b)]
        q[b] = (cot[b].astype(F32) / deg[b]).astype(BF16)
    spread(links, adj, dst, q, run_s)
    send_out(links, own_count, run_s, first[0])
    await_all(place)
    send, pick = list_exchange(place, idx, tiles, picks, i_s, i_r)
    send()

    def after_two():
        for b in range(own_count):
            u_own[b] = run_s[links.last_slot(b)] + q[b].astype(F32)

    phase(place, CUT, feat, table1, u_back, picks, first, pick, lambda gsend: None, after_two, None)

    gather(links, adj, src, table1, run_d)
    for b in range(own_count):
        mean = ((feat[b].astype(F32) + run_d[links.last_dst(b)]) / deg[b]).astype(BF16)
        pre = dot(feat[b], ws1[...]) + dot(mean, wn1[...])
        s = 1.0 / (1.0 + jnp.exp(-pre))
        hidden[b] = (pre * s).astype(BF16)
        u = u_own[b] + u_back[b]
        hi = u.astype(BF16)
        lo = (u - hi.astype(F32)).astype(BF16)
        dh = dot_bt(cot[b], ws2[...]) + (dot_bt(hi, wn2[...]) + dot_bt(lo, wn2[...]))
        dpre = (dh * (s * (1.0 + pre * (1.0 - s)))).astype(BF16)
        q[b] = (dot_bt(dpre, wn1[...]) / deg[b]).astype(BF16)
        keep[0, b] = dpre
        keep[1, b] = mean
        keep[2, b] = hi
        keep[3, b] = lo

    def fill_one(gsend):
        spread(links, adj, dst, q, run_s)
        send_out(links, own_count, run_s, gsend)

    def weights(b, total):
        dpre = keep[0, b]
        return (
            total[0] + dot_at(feat[b], dpre),
            total[1] + dot_at(keep[1, b], dpre),
            total[2] + dot_at(hidden[b], cot[b]),
            total[3] + (dot_at(hidden[b], keep[2, b]) + dot_at(hidden[b], keep[3, b])),
        )

    def after_one():
        zero = jnp.zeros((width, width), F32)
        for i, part in enumerate(lax.fori_loop(0, own_count, weights, (zero,) * 4)):
            grads[pl.ds(i * width // UNIT, width // UNIT)] = (part * scale).reshape(width // UNIT, UNIT, width)
        for b in range(own_count):
            base[b] = dot_bt(keep[0, b], ws1[...]) + q[b].astype(F32) + run_s[links.last_slot(b)]

    phase(place, CUT, hidden, table2, back, picks, second, None, fill_one, after_one,
          sum_stages(place, grads, gout, rest))


def phase_scratch(split, own_count, rows, feat):
    ny, nz, nh, nx = split["y"], split["z"], split["zh"], split["xc"]
    ring = nh * nz
    blocks = (own_count, rows, feat)
    one = (rows, feat)
    dma = pltpu.SemaphoreType.DMA
    pieces = dma((ring, CUT))
    return [
        pltpu.VMEM((ny * nz + nh * nx,) + one, BF16),
        pltpu.VMEM((ring,) + blocks, BF16),
        pltpu.VMEM((ny, nz) + one, BF16),
        pltpu.VMEM((nx, 2) + one, BF16),
        pltpu.VMEM((ny, nz) + one, BF16),
        pltpu.VMEM((nx, nh) + one, BF16),
        pltpu.VMEM((ring,) + blocks, BF16),
        pltpu.VMEM((ring,) + blocks, BF16),
        pltpu.VMEM((ring,) + blocks, BF16),
        pltpu.VMEM((ring,) + blocks, BF16),
        pltpu.VMEM((2,) + blocks, F32),
        pltpu.VMEM((1,) + blocks, BF16),
        pieces, pieces, pieces,
        dma((ny, nz)), dma((ny, nz)), dma((nx, 2)), dma((nx, 2)),
        dma((ny, nz)), dma((ny, nz)), dma((nx,)), dma((nx,)),
        pieces, pieces, pieces, pieces,
    ]


def sum_scratch(split, units):
    ny, nz, cx = split["y"], split["z"], split["xc"] // 2
    half = units // 2
    part = half // cx
    piece = part // ny
    dma = pltpu.SemaphoreType.DMA
    return [
        pltpu.VMEM((half, UNIT, 128), F32),
        pltpu.VMEM((half, UNIT, 128), F32),
        pltpu.VMEM((cx, part, UNIT, 128), F32),
        pltpu.VMEM((part, UNIT, 128), F32),
        pltpu.VMEM((ny, piece, UNIT, 128), F32),
        pltpu.VMEM((nz, piece, UNIT, 128), F32),
        pltpu.VMEM((piece, UNIT, 128), F32),
        pltpu.VMEM((1, piece, UNIT, 128), F32),
        pltpu.VMEM((part, UNIT, 128), F32),
        pltpu.VMEM((half, UNIT, 128), F32),
        dma((1,)), dma((1,)), dma((cx,)), dma((cx,)), dma((ny,)), dma((ny,)),
        dma((nz,)), dma((nz,)), dma((1,)), dma((1,)), dma((ny,)), dma((ny,)),
        dma((cx,)), dma((cx,)), dma((1,)), dma((1,)),
    ]


def last_kernel(dst, src, meta, adj, hidden, table, deg, base, back, grads, ws2, wn2,
                out, grad_in, g1, g2, g3, g4, run):
    own_count, rows, width = hidden.shape
    edges = adj.shape[0]
    links = Links(meta, edges, own_count)
    run[edges] = jnp.zeros((rows, width), F32)
    gather(links, adj, src, table, run)
    for b in range(own_count):
        mean = ((hidden[b].astype(F32) + run[links.last_dst(b)]) / deg[b]).astype(BF16)
        out[b] = (dot(hidden[b], ws2[...]) + dot(mean, wn2[...])).astype(BF16)
        grad_in[b] = base[b] + back[b]
    for i, g in enumerate((g1, g2, g3, g4)):
        g[...] = grads[pl.ds(i * width // UNIT, width // UNIT)].reshape(width, width)


def call(body, edges, args, far, out_shape, scratch, params):
    smem = pl.BlockSpec(memory_space=pltpu.SMEM)
    vmem = pl.BlockSpec(memory_space=pltpu.VMEM)
    where = pl.BlockSpec(memory_space=pl.ANY)
    return pl.pallas_call(
        body,
        out_shape=out_shape,
        in_specs=[smem] * len(edges) + [vmem] * len(args) + [where] * len(far),
        out_specs=[vmem] * len(out_shape),
        scratch_shapes=scratch,
        compiler_params=pltpu.CompilerParams(vmem_limit_bytes=LIMIT, **params),
    )(*edges, *args, *far)


def local(
    split,
    nodes,
    features,
    adjacency,
    edge_dst,
    edge_src,
    send_row,
    send_col,
    w_self1,
    w_neigh1,
    w_self2,
    w_neigh2,
    cotangent,
):
    own = features[0, 0]
    adj = adjacency[0, 0]
    dst, src = edge_dst[0, 0], edge_src[0, 0]
    cot = cotangent[0, 0]
    own_count, rows, width = own.shape
    lists = jnp.concatenate([send_row.reshape(-1), send_col.reshape(-1)])
    remote_count = lists.size
    idx = jnp.broadcast_to(jnp.pad(lists, (0, 128 - remote_count))[None, :], (8, 128))
    size = own_count + remote_count
    edges = (dst, src, edge_links(split, own_count, size, dst, src))
    blocks = (own_count, rows, width)
    full = jax.ShapeDtypeStruct(blocks, F32)
    half = jax.ShapeDtypeStruct(blocks, BF16)
    weight = jax.ShapeDtypeStruct((width, width), F32)
    run = pltpu.VMEM((adj.shape[0] + 1, rows, width), F32)
    ny, nz, nx = split["y"], split["z"], split["xc"]
    dma = pltpu.SemaphoreType.DMA
    per_phase = phase_scratch(split, own_count, rows, width)
    far = (own, adj, cot, w_self1, w_neigh1, w_self2, w_neigh2)
    scratch = [pltpu.VMEM(a.shape, BF16) for a in far] + [
        dma((len(far),)),
        pltpu.VMEM((size, rows, width), BF16),
        pltpu.VMEM(blocks, F32),
        pltpu.VMEM(blocks, F32),
        pltpu.VMEM(blocks, BF16),
        pltpu.VMEM((4,) + blocks, BF16),
        pltpu.VMEM((4 * width // UNIT, UNIT, width), F32),
        run,
        run,
        pltpu.VMEM((nz + 1, 8, 128), jnp.int32),
        pltpu.VMEM((ny, nz, 8, 128), F32),
        pltpu.VMEM((nx, 2, 8, 128), F32),
        dma((nz,)),
        dma((nz + 1,)),
    ] + per_phase + per_phase + sum_scratch(split, 4 * width // UNIT)
    hidden, table, deg, base, back, grads = call(
        functools.partial(main_kernel, split, 1.0 / math.sqrt(nodes), len(per_phase), len(far)),
        edges,
        (idx,),
        far,
        [half, jax.ShapeDtypeStruct((size, rows, width), BF16), full, full, full,
         jax.ShapeDtypeStruct((4 * width // UNIT, UNIT, width), F32)],
        scratch,
        dict(collective_id=0, has_side_effects=True),
    )
    out, grad_in, g1, g2, g3, g4 = call(
        last_kernel,
        edges,
        (adj, hidden, table, deg, base, back, grads, w_self2, w_neigh2),
        (),
        [half, full, weight, weight, weight, weight],
        [run],
        {},
    )
    return out.reshape(features.shape), grad_in.reshape(features.shape), g1, g2, g3, g4


def solution(mesh):
    blocked = P("row", "col", None, None, None)
    placed = (
        blocked,
        blocked,
        P("row", "col", None),
        P("row", "col", None),
        P("row", "col", None, None),
        P("row", "col", None, None),
        P(),
        P(),
        P(),
        P(),
        blocked,
    )

    def whole(*args):
        shape = args[0].shape
        nodes = shape[0] * shape[1] * shape[2] * shape[3]
        return jax.shard_map(
            functools.partial(local, SPLIT, nodes),
            mesh=mesh,
            in_specs=placed,
            out_specs=(blocked, blocked, P(), P(), P(), P()),
            check_vma=False,
        )(*args)

    return whole
```

```python
import functools
import math

import jax
import jax.numpy as jnp
import numpy as np
from jax import lax
from jax.experimental import pallas as pl
from jax.experimental.pallas import tpu as pltpu
from jax.sharding import PartitionSpec as P

MESH = pl.DeviceIdType.MESH
BF16 = jnp.bfloat16
F32 = jnp.float32
LIMIT = 60 * 1024 * 1024
SPLIT = {"y": 4, "z": 8, "zh": 2, "xc": 8}
CUT = 2
UNIT = 16


def dot(a, b):
    return jnp.dot(a, b, preferred_element_type=F32)


def dot_bt(a, b):
    return lax.dot_general(a, b, (((1,), (1,)), ((), ())), preferred_element_type=F32)


def dot_at(a, b):
    return lax.dot_general(a, b, (((0,), (0,)), ((), ())), preferred_element_type=F32)


class Place:
    def __init__(self, split):
        self.split = split
        self.ny, self.nz, self.nh, self.nx = split["y"], split["z"], split["zh"], split["xc"]
        self.nrow, self.ring = self.ny * self.nz, self.nh * self.nz
        self.r = lax.axis_index("row")
        self.c = lax.axis_index("col")
        self.y, self.z = lax.div(self.r, self.nz), lax.rem(self.r, self.nz)
        self.zh, self.xc = lax.div(self.c, self.nx), lax.rem(self.c, self.nx)
        self.g = self.zh * self.nz + self.z
        self.partner = (1 - self.zh) * self.nx + self.xc

    def y_peer(self, d):
        return lax.rem(self.y + d, self.ny)

    def x_peer(self, d):
        return lax.rem(self.xc + d, self.nx)

    def at_ring(self, pos):
        pos = lax.rem(pos + self.ring, self.ring)
        return self.y * self.nz + lax.rem(pos, self.nz), lax.div(pos, self.nz) * self.nx + self.xc

    def reach_right(self, src):
        return jnp.where(src < self.nz // 2, self.nz, self.nz - 1 - src)

    def reach_left(self, src):
        return jnp.where(src < self.nz // 2, src, self.nz)


def remote(src, dst, ssem, rsem, row, col):
    return pltpu.make_async_remote_copy(
        src_ref=src, dst_ref=dst, send_sem=ssem, recv_sem=rsem,
        device_id=(row, col), device_id_type=MESH,
    )


def greet_all(place):
    barrier = pltpu.get_barrier_semaphore()
    y, z, zh, g, r, c = place.y, place.z, place.zh, place.g, place.r, place.c
    ny, nz, nx = place.ny, place.nz, place.nx

    def greet(row, col):
        pl.semaphore_signal(barrier, inc=1, device_id=(row, col), device_id_type=MESH)

    greet(r, place.partner)
    for d in range(1, nz):
        greet(y * nz + lax.rem(z + d, nz), c)
    for d in range(1, ny):
        greet(place.y_peer(d) * nz + z, c)
    for d in range(1, nx):
        greet(r, zh * nx + place.x_peer(d))

    @pl.when(z == 0)
    def _():
        greet(*place.at_ring(g - 1))

    @pl.when(z == nz - 1)
    def _():
        greet(*place.at_ring(g + 1))


def await_all(place):
    barrier = pltpu.get_barrier_semaphore()
    met = (place.ny - 1) + (place.nz - 1) + 1 + (place.nx - 1)
    at_end = (place.z == 0) | (place.z == place.nz - 1)

    @pl.when(at_end)
    def _():
        pl.semaphore_wait(barrier, met + 1)

    @pl.when(jnp.logical_not(at_end))
    def _():
        pl.semaphore_wait(barrier, met)


def phase(place, cut, own, table, back, picks, scratch, lists, fill, after, sums):
    ny, nz, nh, nx = place.ny, place.nz, place.nh, place.nx
    nrow, ring = place.nrow, place.ring
    r, c, y, z, zh, xc, g = place.r, place.c, place.y, place.z, place.zh, place.xc, place.g
    y_peer, x_peer, at_ring = place.y_peer, place.x_peer, place.at_ring
    reach_right, reach_left = place.reach_right, place.reach_left
    pick_row, pick_col = picks
    (gsend, chain, stage_y, stage_c, land_y, land_c, in_right, in_left,
     out_left, out_right, ready, far_out,
     f_r, f_sr, f_sl, yf_s, yf_r, cf_s, cf_r, yb_s, yb_r, cb_s, cb_r,
     br_r, bl_r, b_sl, b_sr) = scratch
    own_count, rows, feat = own.shape
    per = own_count // cut

    def part(ref, slot, ch):
        return ref.at[slot, pl.ds(ch * per, per)]

    def right(src, ch):
        ref = part(chain, src, ch)
        return remote(ref, ref, f_sr.at[src, ch], f_r.at[src, ch], *at_ring(g + 1))

    def left(src, ch):
        ref = part(chain, src, ch)
        return remote(ref, ref, f_sl.at[src, ch], f_r.at[src, ch], *at_ring(g - 1))

    def back_left(o, ch, buf):
        return remote(part(buf, o, ch), part(in_right, o, ch), b_sl.at[o, ch], br_r.at[o, ch],
                      *at_ring(g - 1))

    def back_right(o, ch, buf):
        return remote(part(buf, o, ch), part(in_left, o, ch), b_sr.at[o, ch], bl_r.at[o, ch],
                      *at_ring(g + 1))

    def y_back(d, o):
        yy = y_peer(d)
        return remote(gsend.at[yy * nz + o], land_y.at[(ny - d) % ny, o],
                      yb_s.at[d, o], yb_r.at[(ny - d) % ny, o], yy * nz + z, c)

    def x_back(d):
        xx = x_peer(d)
        return remote(gsend.at[pl.ds(nrow + xx * nh, nh)], land_c.at[(nx - d) % nx],
                      cb_s.at[d], cb_r.at[(nx - d) % nx], r, zh * nx + xx)

    def y_out(d, src):
        return remote(stage_y.at[d, src], table.at[own_count + y * nz + src],
                      yf_s.at[d, src], yf_r.at[d, src], y_peer(d) * nz + z, c)

    def y_in(d, src):
        yy = lax.rem(y + ny - d, ny)
        return remote(stage_y.at[d, src], table.at[own_count + yy * nz + src],
                      yf_s.at[d, src], yf_r.at[d, src], yy * nz + z, c)

    def col_slot(s, x_from):
        half = zh if s == 0 else 1 - zh
        return own_count + nrow + half * nx + x_from

    def c_out(d, s):
        return remote(stage_c.at[d, s], table.at[col_slot(s, xc)],
                      cf_s.at[d, s], cf_r.at[d, s], r, zh * nx + x_peer(d))

    def c_in(d, s):
        xx = lax.rem(xc + nx - d, nx)
        return remote(stage_c.at[d, s], table.at[col_slot(s, xx)],
                      cf_s.at[d, s], cf_r.at[d, s], r, zh * nx + xx)

    chain[g] = own[...]
    for ch in range(cut):
        @pl.when(reach_right(z) > 0)
        def _(ch=ch):
            right(g, ch).start()

        @pl.when(reach_left(z) > 0)
        def _(ch=ch):
            left(g, ch).start()

    if fill is not None:
        fill[0](gsend)
    for d in range(1, nx):
        x_back(d).start()
    if fill is not None:
        fill[1](gsend)

    def first_y(i, carry):
        away = nz - 1 - i
        for o, ok in ((z - away, away <= z), (z + away, (away > 0) & (z + away < nz))):
            @pl.when(ok)
            def _(o=o):
                for d in range(1, ny):
                    y_back(d, o).start()
        return carry

    lax.fori_loop(0, nz, first_y, 0)

    def hot_row(which, k):
        return jnp.where(which[0:1, :] == k, 1.0, 0.0)

    def choose(which, slot):
        total = None
        for k in range(own_count):
            term = chain[slot, k] * hot_row(which, k).astype(BF16)
            total = term if total is None else total + term
        return total

    def forward(src):
        slot = zh * nz + src
        for d in range(ny):
            chosen = choose(pick_row[d, src], slot)
            if d == 0:
                table[own_count + y * nz + src] = chosen
            else:
                stage_y[d, src] = chosen
                y_out(d, src).start()

    def forward_col(s, slot):
        for d in range(nx):
            chosen = choose(pick_col[d, s], slot)
            if d == 0:
                table[col_slot(s, xc)] = chosen
            else:
                stage_c[d, s] = chosen
                c_out(d, s).start()

    def placed(o, k):
        total = None
        for d in range(ny):
            term = land_y[d, o].astype(F32) * hot_row(pick_row[d, o], k)
            total = term if total is None else total + term
        return total

    def placed_col(half, s, k):
        total = None
        for d in range(nx):
            term = land_c[d, half].astype(F32) * hot_row(pick_col[d, s], k)
            total = term if total is None else total + term
        return total

    def y_arrived(o):
        for d in range(1, ny):
            y_back(d, o).wait_recv()

    def coming(s, way):
        src = lax.rem(g + ring - s if way == 0 else g + s, ring)
        low = lax.rem(src, nz)
        reach = reach_right(low) if way == 0 else reach_left(low)
        return src, low, (s >= 1) & (s <= nz) & (s <= reach), s < reach, lax.div(src, nz) == zh

    def fwd_step(s, ch):
        for way, copy in ((0, right), (1, left)):
            src, low, comes, goes_on, mine = coming(s, way)

            @pl.when(comes)
            def _():
                copy(src, ch).wait_recv()

            @pl.when(comes & goes_on)
            def _():
                copy(src, ch).start()

    def deliver(s):
        for way in range(2):
            src, low, comes, goes_on, mine = coming(s, way)

            @pl.when(comes & mine)
            def _():
                forward(low)

        @pl.when(s == nz)
        def _():
            forward_col(1, lax.rem(g + nz, ring))

    def prepare(t):
        for way in range(2):
            o, low, comes, has_in, mine = coming(nz - t, way)

            @pl.when(comes & mine & (t >= 0))
            def _():
                y_arrived(low)
                for k in range(own_count):
                    ready[way, k] = placed(low, k)

        @pl.when(t == 0)
        def _():
            for d in range(1, nx):
                x_back(d).wait_recv()
            for k in range(own_count):
                far_out[0, k] = placed_col(1 - zh, 1, k).astype(BF16)

    def far_copy(way, o, ch):
        if way == 0:
            return remote(part(far_out, 0, ch), part(in_right, o, ch), b_sl.at[o, ch], br_r.at[o, ch],
                          *at_ring(g - 1))
        return remote(part(far_out, 0, ch), part(in_left, o, ch), b_sr.at[o, ch], bl_r.at[o, ch],
                      *at_ring(g + 1))

    def bwd_step(t, ch):
        for way, copy, got, out in ((0, back_left, in_right, out_left), (1, back_right, in_left, out_right)):
            o, low, comes, has_in, mine = coming(nz - t, way)
            sends = comes & (t >= 0)

            @pl.when(sends & has_in)
            def _():
                copy(o, ch, out).wait_recv()

            @pl.when(sends & has_in & mine)
            def _():
                for k in range(ch * per, ch * per + per):
                    out[o, k] = (ready[way, k] + got[o, k].astype(F32)).astype(BF16)
                copy(o, ch, out).start()

            @pl.when(sends & has_in & jnp.logical_not(mine))
            def _():
                copy(o, ch, got).start()

            @pl.when(sends & jnp.logical_not(has_in) & mine)
            def _():
                for k in range(ch * per, ch * per + per):
                    out[o, k] = ready[way, k].astype(BF16)
                copy(o, ch, out).start()

            @pl.when(sends & jnp.logical_not(has_in) & jnp.logical_not(mine))
            def _():
                far_copy(way, o, ch).start()

    def settle(s):
        for way, copy in ((0, right), (1, left)):
            src, low, comes, goes_on, mine = coming(s, way)

            @pl.when((comes | (s == 0)) & goes_on)
            def _():
                for ch in range(cut):
                    copy(src, ch).wait_send()

            @pl.when((comes & mine) | ((s == 0) & (way == 0)))
            def _():
                for d in range(1, ny):
                    y_in(d, low).wait_recv()
                    y_out(d, low).wait_send()
                    y_back(d, low).wait_send()

    def step(s, carry):
        for ch in range(cut):
            @pl.when(s > 1)
            def _(ch=ch):
                fwd_step(s, ch)

            bwd_step(s - 1, ch)
        prepare(s)
        deliver(s)

        @pl.when(s == 1)
        def _():
            forward(z)

        @pl.when(s == 3)
        def _():
            forward_col(0, g)

        @pl.when(s == 5)
        def _():
            y_arrived(z)
            for k in range(own_count):
                back[k] = placed(z, k) + placed_col(zh, 0, k)

        @pl.when(s == 6)
        def _():
            for d in range(1, nx):
                x_back(d).wait_send()

        @pl.when(s == 7)
        def _():
            for d in range(1, nx):
                c_in(d, 0).wait_recv()
                c_out(d, 0).wait_send()

        @pl.when(s >= 3)
        def _():
            settle(s - 3)

        if sums is not None:
            for k in range(1, len(sums)):
                @pl.when(s == k)
                def _(k=k):
                    sums[k]()
        return carry

    for ch in range(cut):
        fwd_step(1, ch)
    after()
    if sums is not None:
        sums[0]()
    table[pl.ds(0, own_count)] = own[...]
    land_y[0] = gsend[pl.ds(y * nz, nz)]
    land_c[0] = gsend[pl.ds(nrow + xc * nh, nh)]
    if lists is not None:
        lists()
    prepare(0)
    last = max(nz + 1, 9 if sums is None else 10)
    lax.fori_loop(1, last, step, 0)

    for way, copy, got, some in (
        (0, back_left, in_right, reach_right(z) > 0), (1, back_right, in_left, reach_left(z) > 0)
    ):
        @pl.when(some)
        def _():
            for ch in range(cut):
                copy(g, ch, got).wait_recv()
            for k in range(own_count):
                back[k] += got[g, k].astype(F32)

    lax.fori_loop(last - 3, nz + 1, lambda s, carry: (settle(s), carry)[1], 0)

    def sent(s, carry):
        for way, copy, buf in ((0, back_left, out_left), (1, back_right, out_right)):
            src, low, comes, goes_on, mine = coming(s, way)

            @pl.when(comes)
            def _():
                for ch in range(cut):
                    copy(src, ch, buf).wait_send()
        return carry

    lax.fori_loop(1, nz + 1, sent, 0)
    for d in range(1, nx):
        c_in(d, 1).wait_recv()
        c_out(d, 1).wait_send()


def list_exchange(place, idx, tiles, picks, i_s, i_r):
    ny, nz, nx, nrow = place.ny, place.nz, place.nx, place.nrow
    y, z, zh, r, c = place.y, place.z, place.zh, place.r, place.c
    pick_row, pick_col = picks

    def idx_copy(d):
        zz = lax.rem(z + d, nz)
        return remote(idx, tiles.at[z], i_s.at[d], i_r.at[z], y * nz + zz, c)

    def idx_wait(d):
        zz = lax.rem(z + d, nz)
        return remote(idx, tiles.at[zz], i_s.at[d], i_r.at[zz], y * nz + zz, c)

    idx_far = remote(idx, tiles.at[nz], i_s.at[0], i_r.at[nz], r, place.partner)

    def send():
        idx_far.start()
        for d in range(1, nz):
            idx_copy(d).start()
        tiles[z] = idx[...]

    def pick():
        for d in range(1, nz):
            idx_wait(d).wait_recv()
        idx_far.wait_recv()
        lists = tiles[...].astype(F32)
        along = lists[:nz].reshape(nz * 8, 128).astype(BF16)
        pair = jnp.concatenate([tiles[z].astype(F32), lists[nz]], axis=0).astype(BF16)
        lane = lax.broadcasted_iota(jnp.int32, (128, 128), 0)
        for d in range(ny):
            hot = jnp.where(lane == place.y_peer(d) * nz + z, 1.0, 0.0).astype(BF16)
            pick_row[d] = dot(along, hot).reshape(nz, 8, 128)
        for d in range(nx):
            hot = jnp.where(lane == nrow + zh * nx + place.x_peer(d), 1.0, 0.0).astype(BF16)
            pick_col[d] = dot(pair, hot).reshape(2, 8, 128)
        for d in range(1, nz):
            idx_copy(d).wait_send()
        idx_far.wait_send()

    return send, pick


def sum_stages(place, gr, gout, refs):
    ny, nz, sx = place.ny, place.nz, place.nx
    nx = sx // 2
    r, c, y, z, zh, xc = place.r, place.c, place.y, place.z, place.zh, place.xc
    core, x = lax.rem(xc, 2), lax.div(xc, 2)
    (a1, v1, a2, v2, a3, a4, a5, v5, w1, w2, s1, r1, s2, r2, s3, r3, s4, r4, s5, r5,
     s6, r6, s7, r7, s8, r8) = refs
    half = gr.shape[0] // 2
    part = half // nx
    piece = part // ny
    other = zh * sx + x * 2 + (1 - core)

    def xcol(d):
        xx = lax.rem(x + d, nx)
        return xx, zh * sx + xx * 2 + core

    def yrow(d):
        yy = lax.rem(y + d, ny)
        return yy, yy * nz + z

    def rows_of(i, n):
        return pl.ds(i * n, n)

    c1 = remote(gr.at[rows_of(1 - core, half)], a1, s1.at[0], r1.at[0], r, other)

    def c2(d):
        xx, col = xcol(d)
        return remote(v1.at[rows_of(xx, part)], a2.at[(nx - d) % nx], s2.at[d], r2.at[(nx - d) % nx], r, col)

    def c3(d):
        yy, row = yrow(d)
        return remote(v2.at[rows_of(yy, piece)], a3.at[(ny - d) % ny], s3.at[d], r3.at[(ny - d) % ny], row, c)

    def c4(d, slot):
        zz = lax.rem(z + d, nz)
        to = z if slot is None else zz
        return remote(a4.at[z], a4.at[to], s4.at[d], r4.at[to], y * nz + zz, c)

    c5 = remote(v5.at[0], a5, s5.at[0], r5.at[0], r, place.partner)

    def c6(d, slot):
        yy, row = yrow(d)
        to = y if slot is None else yy
        here = w1.at[rows_of(y, piece)]
        return remote(here, w1.at[rows_of(to, piece)], s6.at[d], r6.at[to], row, c)

    def c7(d, slot):
        xx, col = xcol(d)
        to = x if slot is None else xx
        here = w2.at[rows_of(x, part)]
        return remote(here, w2.at[rows_of(to, part)], s7.at[d], r7.at[to], r, col)

    c8 = remote(w2, gout.at[rows_of(core, half)], s8.at[0], r8.at[0], r, other)
    c8_in = remote(w2, gout.at[rows_of(1 - core, half)], s8.at[0], r8.at[0], r, other)

    def t0():
        c1.start()

    def t1():
        c1.wait_recv()
        v1[...] = gr[rows_of(core, half)] + a1[...]
        for d in range(1, nx):
            c2(d).start()

    def t2():
        total = v1[rows_of(x, part)]
        for d in range(1, nx):
            c2(d).wait_recv()
        for d in range(1, nx):
            total = total + a2[d]
        v2[...] = total
        for d in range(1, ny):
            c3(d).start()

    def t3():
        total = v2[rows_of(y, piece)]
        for d in range(1, ny):
            c3(d).wait_recv()
        for d in range(1, ny):
            total = total + a3[d]
        a4[z] = total
        for d in range(1, nz):
            c4(d, None).start()

    def t4():
        for d in range(1, nz):
            c4(d, 1).wait_recv()
        total = a4[0]
        for i in range(1, nz):
            total = total + a4[i]
        v5[0] = total
        c5.start()

    def t5():
        c5.wait_recv()
        w1[rows_of(y, piece)] = v5[0] + a5[...]
        for d in range(1, ny):
            c6(d, None).start()

    def t6():
        for d in range(1, ny):
            c6(d, 1).wait_recv()
        w2[rows_of(x, part)] = w1[...]
        for d in range(1, nx):
            c7(d, None).start()

    def t7():
        for d in range(1, nx):
            c7(d, 1).wait_recv()
        gout[rows_of(core, half)] = w2[...]
        c8.start()

    def t8():
        c8_in.wait_recv()
        c1.wait_send()
        for d in range(1, nx):
            c2(d).wait_send()
            c7(d, None).wait_send()
        for d in range(1, ny):
            c3(d).wait_send()
            c6(d, None).wait_send()
        for d in range(1, nz):
            c4(d, None).wait_send()
        c5.wait_send()
        c8.wait_send()

    return [t0, t1, t2, t3, t4, t5, t6, t7, t8]


class Links:
    def __init__(self, meta, edges, own_count):
        self.meta, self.edges, self.own_count = meta, edges, own_count

    def prev_dst(self, e):
        return self.meta[e]

    def prev_slot(self, e):
        return self.meta[self.edges + e]

    def last_dst(self, b):
        return self.meta[2 * self.edges + b]

    def last_slot(self, i):
        return self.meta[2 * self.edges + self.own_count + i]


def edge_links(split, own_count, size, dst, src):
    edges = dst.size
    slot = grad_slot(split, own_count, src)
    wanted = jnp.concatenate([
        dst, slot, jnp.arange(own_count, dtype=jnp.int32), jnp.arange(size, dtype=jnp.int32)
    ])[:, None]
    by_dst = np.concatenate([np.ones(edges), np.zeros(edges), np.ones(own_count), np.zeros(size)]) > 0
    free = np.full(own_count + size, edges)
    before = np.concatenate([np.arange(edges), np.arange(edges), free])
    e = np.arange(edges, dtype=np.int32)[None, :]
    key = jnp.where(by_dst[:, None], dst[None, :], slot[None, :])
    early = e < before[:, None]
    found = jnp.max(jnp.where((key == wanted) & early, e, -1), axis=1)
    return jnp.where(found < 0, edges, found)


def grad_slot(split, own_count, t):
    nh, nx = split["zh"], split["xc"]
    first = own_count + split["y"] * split["z"]
    q = t - first
    return jnp.where(t < first, t, first + nh * lax.rem(q, nx) + lax.div(q, nx))


def running(edges, run, term, prev):
    def one(e, carry):
        run[e] = term(e) + run[prev(e)]
        return carry

    lax.fori_loop(0, edges, one, 0, unroll=7)


def spread(links, adj, dst, q, run):
    running(links.edges, run, lambda e: dot_at(adj[e], q[dst[e]]), links.prev_slot)


def gather(links, adj, src, table, run):
    running(links.edges, run, lambda e: dot(adj[e], table[src[e]]), links.prev_dst)


def send_out(links, own_count, run, gsend, first, last):
    @pl.loop(first, last)
    def _(i):
        gsend[i] = run[links.last_slot(own_count + i)].astype(BF16)


def main_kernel(split, scale, n_phase, n_in, dst, src, meta, idx, *refs):
    place = Place(split)
    greet_all(place)
    far_in, refs = refs[:n_in], refs[n_in:]
    (hidden, table2, deg, base, back, gout), refs = refs[:6], refs[6:]
    near_in, refs = refs[:n_in], list(refs[n_in:])
    (in_s, table1, u_own, u_back, q, keep, grads, run_d, run_s, tiles, pick_row, pick_col,
     i_s, i_r) = refs[:14]
    del refs[:14]
    first, second, rest = refs[:n_phase], refs[n_phase:2 * n_phase], refs[2 * n_phase:]
    feat, adj, cot, ws1, wn1, ws2, wn2 = near_in
    loads = [pltpu.make_async_copy(a, b, in_s.at[i]) for i, (a, b) in enumerate(zip(far_in, near_in))]
    for load in loads:
        load.start()
    picks = (pick_row, pick_col)
    own_count, rows, width = feat.shape
    edges = adj.shape[0]
    links = Links(meta, edges, own_count)
    run_d[edges] = jnp.zeros((rows, width), F32)
    run_s[edges] = jnp.zeros((rows, width), F32)
    for load in loads:
        load.wait()

    ones = jnp.ones((rows, rows), BF16)
    running(edges, run_d, lambda e: dot(adj[e], ones), links.prev_dst)
    for b in range(own_count):
        deg[b] = 1.0 + run_d[links.last_dst(b)]
        q[b] = (cot[b].astype(F32) / deg[b]).astype(BF16)
    spread(links, adj, dst, q, run_s)
    send_out(links, own_count, run_s, first[0], 0, place.nrow + place.nh * place.nx)
    await_all(place)
    send, pick = list_exchange(place, idx, tiles, picks, i_s, i_r)
    send()

    def after_two():
        for b in range(own_count):
            u_own[b] = run_s[links.last_slot(b)] + q[b].astype(F32)

    phase(place, CUT, feat, table1, u_back, picks, first, pick, None, after_two, None)

    gather(links, adj, src, table1, run_d)
    for b in range(own_count):
        mean = ((feat[b].astype(F32) + run_d[links.last_dst(b)]) / deg[b]).astype(BF16)
        pre = dot(feat[b], ws1[...]) + dot(mean, wn1[...])
        s = 1.0 / (1.0 + jnp.exp(-pre))
        hidden[b] = (pre * s).astype(BF16)
        u = u_own[b] + u_back[b]
        hi = u.astype(BF16)
        lo = (u - hi.astype(F32)).astype(BF16)
        dh = dot_bt(cot[b], ws2[...]) + (dot_bt(hi, wn2[...]) + dot_bt(lo, wn2[...]))
        dpre = (dh * (s * (1.0 + pre * (1.0 - s)))).astype(BF16)
        q[b] = (dot_bt(dpre, wn1[...]) / deg[b]).astype(BF16)
        keep[0, b] = dpre
        keep[1, b] = mean
        keep[2, b] = hi
        keep[3, b] = lo

    def fill_one(gsend):
        spread(links, adj, dst, q, run_s)
        send_out(links, own_count, run_s, gsend, place.nrow, place.nrow + place.nh * place.nx)

    def fill_rows(gsend):
        send_out(links, own_count, run_s, gsend, 0, place.nrow)

    def weights(b, total):
        dpre = keep[0, b]
        return (
            total[0] + dot_at(feat[b], dpre),
            total[1] + dot_at(keep[1, b], dpre),
            total[2] + dot_at(hidden[b], cot[b]),
            total[3] + (dot_at(hidden[b], keep[2, b]) + dot_at(hidden[b], keep[3, b])),
        )

    def after_one():
        zero = jnp.zeros((width, width), F32)
        for i, part in enumerate(lax.fori_loop(0, own_count, weights, (zero,) * 4)):
            grads[pl.ds(i * width // UNIT, width // UNIT)] = (part * scale).reshape(width // UNIT, UNIT, width)
        for b in range(own_count):
            base[b] = dot_bt(keep[0, b], ws1[...]) + q[b].astype(F32) + run_s[links.last_slot(b)]

    phase(place, CUT, hidden, table2, back, picks, second, None, (fill_one, fill_rows), after_one,
          sum_stages(place, grads, gout, rest))


def phase_scratch(split, own_count, rows, feat):
    ny, nz, nh, nx = split["y"], split["z"], split["zh"], split["xc"]
    ring = nh * nz
    blocks = (own_count, rows, feat)
    one = (rows, feat)
    dma = pltpu.SemaphoreType.DMA
    pieces = dma((ring, CUT))
    return [
        pltpu.VMEM((ny * nz + nh * nx,) + one, BF16),
        pltpu.VMEM((ring,) + blocks, BF16),
        pltpu.VMEM((ny, nz) + one, BF16),
        pltpu.VMEM((nx, 2) + one, BF16),
        pltpu.VMEM((ny, nz) + one, BF16),
        pltpu.VMEM((nx, nh) + one, BF16),
        pltpu.VMEM((ring,) + blocks, BF16),
        pltpu.VMEM((ring,) + blocks, BF16),
        pltpu.VMEM((ring,) + blocks, BF16),
        pltpu.VMEM((ring,) + blocks, BF16),
        pltpu.VMEM((2,) + blocks, F32),
        pltpu.VMEM((1,) + blocks, BF16),
        pieces, pieces, pieces,
        dma((ny, nz)), dma((ny, nz)), dma((nx, 2)), dma((nx, 2)),
        dma((ny, nz)), dma((ny, nz)), dma((nx,)), dma((nx,)),
        pieces, pieces, pieces, pieces,
    ]


def sum_scratch(split, units):
    ny, nz, cx = split["y"], split["z"], split["xc"] // 2
    half = units // 2
    part = half // cx
    piece = part // ny
    dma = pltpu.SemaphoreType.DMA
    return [
        pltpu.VMEM((half, UNIT, 128), F32),
        pltpu.VMEM((half, UNIT, 128), F32),
        pltpu.VMEM((cx, part, UNIT, 128), F32),
        pltpu.VMEM((part, UNIT, 128), F32),
        pltpu.VMEM((ny, piece, UNIT, 128), F32),
        pltpu.VMEM((nz, piece, UNIT, 128), F32),
        pltpu.VMEM((piece, UNIT, 128), F32),
        pltpu.VMEM((1, piece, UNIT, 128), F32),
        pltpu.VMEM((part, UNIT, 128), F32),
        pltpu.VMEM((half, UNIT, 128), F32),
        dma((1,)), dma((1,)), dma((cx,)), dma((cx,)), dma((ny,)), dma((ny,)),
        dma((nz,)), dma((nz,)), dma((1,)), dma((1,)), dma((ny,)), dma((ny,)),
        dma((cx,)), dma((cx,)), dma((1,)), dma((1,)),
    ]


def last_kernel(dst, src, meta, adj, hidden, table, deg, base, back, grads, ws2, wn2,
                out, grad_in, g1, g2, g3, g4, run):
    own_count, rows, width = hidden.shape
    edges = adj.shape[0]
    links = Links(meta, edges, own_count)
    run[edges] = jnp.zeros((rows, width), F32)
    gather(links, adj, src, table, run)
    for b in range(own_count):
        mean = ((hidden[b].astype(F32) + run[links.last_dst(b)]) / deg[b]).astype(BF16)
        out[b] = (dot(hidden[b], ws2[...]) + dot(mean, wn2[...])).astype(BF16)
        grad_in[b] = base[b] + back[b]
    for i, g in enumerate((g1, g2, g3, g4)):
        g[...] = grads[pl.ds(i * width // UNIT, width // UNIT)].reshape(width, width)


def call(body, edges, args, far, out_shape, scratch, params):
    smem = pl.BlockSpec(memory_space=pltpu.SMEM)
    vmem = pl.BlockSpec(memory_space=pltpu.VMEM)
    where = pl.BlockSpec(memory_space=pl.ANY)
    return pl.pallas_call(
        body,
        out_shape=out_shape,
        in_specs=[smem] * len(edges) + [vmem] * len(args) + [where] * len(far),
        out_specs=[vmem] * len(out_shape),
        scratch_shapes=scratch,
        compiler_params=pltpu.CompilerParams(vmem_limit_bytes=LIMIT, **params),
    )(*edges, *args, *far)


def local(
    split,
    nodes,
    features,
    adjacency,
    edge_dst,
    edge_src,
    send_row,
    send_col,
    w_self1,
    w_neigh1,
    w_self2,
    w_neigh2,
    cotangent,
):
    own = features[0, 0]
    adj = adjacency[0, 0]
    dst, src = edge_dst[0, 0], edge_src[0, 0]
    cot = cotangent[0, 0]
    own_count, rows, width = own.shape
    lists = jnp.concatenate([send_row.reshape(-1), send_col.reshape(-1)])
    remote_count = lists.size
    idx = jnp.broadcast_to(jnp.pad(lists, (0, 128 - remote_count))[None, :], (8, 128))
    size = own_count + remote_count
    edges = (dst, src, edge_links(split, own_count, size, dst, src))
    blocks = (own_count, rows, width)
    full = jax.ShapeDtypeStruct(blocks, F32)
    half = jax.ShapeDtypeStruct(blocks, BF16)
    weight = jax.ShapeDtypeStruct((width, width), F32)
    run = pltpu.VMEM((adj.shape[0] + 1, rows, width), F32)
    ny, nz, nx = split["y"], split["z"], split["xc"]
    dma = pltpu.SemaphoreType.DMA
    per_phase = phase_scratch(split, own_count, rows, width)
    far = (own, adj, cot, w_self1, w_neigh1, w_self2, w_neigh2)
    scratch = [pltpu.VMEM(a.shape, BF16) for a in far] + [
        dma((len(far),)),
        pltpu.VMEM((size, rows, width), BF16),
        pltpu.VMEM(blocks, F32),
        pltpu.VMEM(blocks, F32),
        pltpu.VMEM(blocks, BF16),
        pltpu.VMEM((4,) + blocks, BF16),
        pltpu.VMEM((4 * width // UNIT, UNIT, width), F32),
        run,
        run,
        pltpu.VMEM((nz + 1, 8, 128), jnp.int32),
        pltpu.VMEM((ny, nz, 8, 128), F32),
        pltpu.VMEM((nx, 2, 8, 128), F32),
        dma((nz,)),
        dma((nz + 1,)),
    ] + per_phase + per_phase + sum_scratch(split, 4 * width // UNIT)
    hidden, table, deg, base, back, grads = call(
        functools.partial(main_kernel, split, 1.0 / math.sqrt(nodes), len(per_phase), len(far)),
        edges,
        (idx,),
        far,
        [half, jax.ShapeDtypeStruct((size, rows, width), BF16), full, full, full,
         jax.ShapeDtypeStruct((4 * width // UNIT, UNIT, width), F32)],
        scratch,
        dict(collective_id=0, has_side_effects=True),
    )
    out, grad_in, g1, g2, g3, g4 = call(
        last_kernel,
        edges,
        (adj, hidden, table, deg, base, back, grads, w_self2, w_neigh2),
        (),
        [half, full, weight, weight, weight, weight],
        [run],
        {},
    )
    return out.reshape(features.shape), grad_in.reshape(features.shape), g1, g2, g3, g4


def solution(mesh):
    blocked = P("row", "col", None, None, None)
    placed = (
        blocked,
        blocked,
        P("row", "col", None),
        P("row", "col", None),
        P("row", "col", None, None),
        P("row", "col", None, None),
        P(),
        P(),
        P(),
        P(),
        blocked,
    )

    def whole(*args):
        shape = args[0].shape
        nodes = shape[0] * shape[1] * shape[2] * shape[3]
        return jax.shard_map(
            functools.partial(local, SPLIT, nodes),
            mesh=mesh,
            in_specs=placed,
            out_specs=(blocked, blocked, P(), P(), P(), P()),
            check_vma=False,
        )(*args)

    return whole
```
